128 devices in a mesh: ctx: 8 (over z, core), ep: 16 (over y, x).
Axes of the slice: x: 4, y: 4, z: 4, core: 2. Of those that a mesh axis runs over, the one named last changes fastest.
Arguments:
- query: bfloat16 [16, 1024, 4096], P('ep', 'ctx'), may hold values from -120 to 120
- keyval: bfloat16 [16, 1024, 512], P('ep', 'ctx'), may hold values from -4 to 4
- doc_lengths: int32 [16, 4], P('ep'), may hold values from 1 to 512, 1024 in all within a row
- norm_gain: float32 [4096], replicated, may hold values from 0.5 to 1.5
- router_logits: float32 [16, 1024, 3], P('ep', 'ctx'), may hold values from -10 to 310
- expert_ids: int32 [16, 1024, 3], P('ep', 'ctx'), may hold values from 0 to 127, all different within a row; in each aligned block of 128 rows (0 to 127, 128 to 255, ..., all dimensions but the last counted through in order) at most 4 rows name the same one
- grad_out: bfloat16 [16, 1024, 4096], P('ep', 'ctx'), may hold values from -6 to 6
- base_in: bfloat16 [128, 2, 4096, 768], P(('ctx', 'ep')), may hold values from -0.09375 to 0.09375
- low_in: bfloat16 [128, 2, 4096, 32], P(('ctx', 'ep')), may hold values from -0.09375 to 0.09375
- high_in: bfloat16 [128, 2, 32, 768], P(('ctx', 'ep')), may hold values from -1 to 1
- mag_in: float32 [128, 2, 768], P(('ctx', 'ep')), may hold values from 0.5 to 1.5
- base_out: bfloat16 [128, 768, 4096], P(('ctx', 'ep')), may hold values from -0.21875 to 0.21875
- low_out: bfloat16 [128, 768, 32], P(('ctx', 'ep')), may hold values from -0.21875 to 0.21875
- high_out: bfloat16 [128, 32, 4096], P(('ctx', 'ep')), may hold values from -1 to 1
- mag_out: float32 [128, 4096], P(('ctx', 'ep')), may hold values from 0.5 to 1.5
Outputs:
- grad_query: bfloat16 [16, 1024, 4096], P('ep', 'ctx')
- grad_keyval: bfloat16 [16, 1024, 512], P('ep', 'ctx')
- grad_logits: float32 [16, 1024, 3], P('ep', 'ctx')
- grad_low_in: float32 [128, 2, 4096, 32], P(('ctx', 'ep'))
- grad_high_in: float32 [128, 2, 32, 768], P(('ctx', 'ep'))
- grad_mag_in: float32 [128, 2, 768], P(('ctx', 'ep'))
- grad_low_out: float32 [128, 768, 32], P(('ctx', 'ep'))
- grad_high_out: float32 [128, 32, 4096], P(('ctx', 'ep'))
- grad_mag_out: float32 [128, 4096], P(('ctx', 'ep'))
The draws below stay inside these ranges and needn't reach their ends.
Inputs may be any that keep to these rules, and one draw needn't show every extreme that they name: `expert_ids`: each row names 3 different experts; within the rows of one device no expert is named more than 4 times, and in some device's rows one expert is named exactly 4 times. `doc_lengths`: each group's lengths sum to 1024; the longest is 512.
All inputs are finite; a program needn't handle non-finite values.
Results may differ from the reference program's by a relative error of at most 0.04.
Values may be sent and summed in bfloat16 or wider, within the bound.
A program may use at most 192 MiB of HBM per device.

```python
import math
import jax
import jax.numpy as jnp
import numpy as np
from jax import lax

D = 4096
HEAD_SIZE = 128
QUERY_HEADS = 32
KEYVAL_HEADS = 2
FFW = 768
RK = 32
TOP = 3
DOCS = 4
TOK = 128
CONTEXT_GROUPS = 16
PACKED_TOKENS = 1024
MOST_DOC = 512
EXPERTS = 128
CAP = 4
N_CTX = 8
N_EP = 16


def key_base(key):
    return jax.random.truncated_normal(key, -4.0, 4.0, (CONTEXT_GROUPS, PACKED_TOKENS, KEYVAL_HEADS * HEAD_SIZE), jnp.float32)


def draw_keyval(key, part):
    offset_start = key_base(key)
    key = jax.random.fold_in(key, 11)
    value_rows = jax.random.truncated_normal(key, -4.0, 4.0, (CONTEXT_GROUPS, PACKED_TOKENS, KEYVAL_HEADS * HEAD_SIZE), jnp.float32)
    key_rows = offset_start
    return jnp.concatenate([key_rows, value_rows], axis=2).astype(jnp.bfloat16)


def draw_query(key, part):
    key = jax.random.fold_in(key, 12)
    value_rows = jax.random.truncated_normal(key, -4.0, 4.0, (CONTEXT_GROUPS, PACKED_TOKENS, QUERY_HEADS * HEAD_SIZE), jnp.float32)
    return value_rows.astype(jnp.bfloat16)


def draw_router_logits(key, part):
    key = jax.random.fold_in(key, 13)
    value_rows = 2.0 * jax.random.truncated_normal(key, -4.0, 4.0, (CONTEXT_GROUPS, PACKED_TOKENS, TOP), jnp.float32)
    return value_rows


def block_scale(rng, dims, split, low, top_value):
    gain, own = 1.0, jax.random.fold_in(rng, 6)
    for dim, blocks in split:
        heights = jnp.exp(jax.random.uniform(jax.random.fold_in(own, dim), (blocks,), jnp.float32, low / len(split), top_value / len(split)))
        gain = gain * jnp.repeat(heights, dims[dim] // blocks).reshape([-1 if axis == dim else 1 for axis in range(len(dims))])
    return gain


def length_profile(amount, total, limit, slope):
    weights = [(1 << 20) // math.isqrt(rank ** slope) + 1 for rank in range(2, amount + 1)]
    spare, holding = total - limit - (amount - 1), [1] * (amount - 1)
    while spare > 0:
        candidates = [i for i in range(amount - 1) if holding[i] < limit]
        mass, budget = sum([weights[i] for i in candidates]), spare
        for i in candidates:
            extra = min(limit - holding[i], max(1, budget * weights[i] // mass), spare)
            holding[i] = holding[i] + extra
            spare = spare - extra
    return np.array([limit] + holding)


def uneven(key, amount, total, most, lean):
    if amount == 2:
        one = jax.random.randint(key, (), max(1, total - most), min(most, total - 1) + 1)
        return jnp.stack([one, total - one])
    sizes = jnp.asarray(length_profile(amount, total, most, lean), jnp.int32)
    couples = (amount - 1) // 2
    source_of, sink = sizes[1:1 + 2 * couples:2], sizes[2:2 + 2 * couples:2]
    slack = jnp.minimum(source_of - 1, most - sink)
    shifted = jax.random.randint(jax.random.fold_in(key, 1), (couples,), 0, 1 << 20) % (slack + 1)
    sizes = sizes.at[1:1 + 2 * couples:2].set(source_of - shifted).at[2:2 + 2 * couples:2].set(sink + shifted)
    return sizes[jax.random.permutation(jax.random.fold_in(key, 2), amount)]


def routed_block(own_key, own, number, rows, count, top, most, lean):
    sequence = jax.random.permutation(own_key, count)
    heavy_load, usual = portions_of(count, rows * top, most, lean, True), portions_of(count, rows * top, most, lean, False)
    places = jnp.arange(count)

    def named(sizes, offset_by):
        used = int((sizes > 0).sum())
        fixed = max(1, used // 4)
        moved = fixed + (places - fixed + offset_by * (used - fixed)) % max(1, count - fixed)
        return jnp.zeros((count,), jnp.int32).at[sequence[jnp.where(places < fixed, places, moved)]].set(jnp.asarray(sizes, jnp.int32))

    sizes = jnp.where(number % 4 == 0, named(heavy_load, number // 4), named(usual, number - number // 4 - 1))
    mixed = jax.random.permutation(jax.random.fold_in(own, 3), count)
    donor, sink = mixed[0:count // 2 * 2:2], mixed[1:count // 2 * 2:2]
    room = jnp.minimum(sizes[donor] - 1, most - sizes[sink]) // 2
    room = jnp.where((donor == sequence[0]) | (sink == sequence[0]) | (sizes[sink] == 0), 0, jnp.maximum(room, 0))
    moved = jax.random.randint(jax.random.fold_in(own, 4), (count // 2,), 0, 1 << 20) % (room + 1)
    sizes = sizes.at[donor].add(-moved).at[sink].add(moved)
    members = jnp.searchsorted(jnp.cumsum(sizes), jnp.arange(rows * top), side="right").astype(jnp.int32)
    listing = members.reshape(top, rows).T
    listing = listing[jax.random.permutation(jax.random.fold_in(own, 1), rows)]
    offset_by = jax.random.randint(jax.random.fold_in(own, 2), (rows, 1), 0, top)
    return jnp.take_along_axis(listing, (jnp.arange(top)[None, :] + offset_by) % top, axis=1)


def portions_of(count, total, reach, lean, full):
    portions = [(1 << 20) // math.isqrt(grade ** lean) + 1 for grade in range(1, count + 1)]
    largest = reach if full else min(reach, max(-(-total // count), total * portions[0] // sum(portions)))
    least = 1 if total - largest >= count - 1 else 0
    given, spare = [largest] + [least] * (count - 1), total - largest - least * (count - 1)
    while spare > 0:
        free = [i for i in range(1, count) if given[i] < largest] or [i for i in range(1, count) if given[i] < reach]
        mass, left = sum([portions[i] for i in free]), spare
        for i in free:
            extra = min(reach - given[i], max(1, left * portions[i] // mass), spare)
            given[i] = given[i] + extra
            spare = spare - extra
    return np.array(given)


def scatter_about(stream_key, shape, width, reach, shards=(), kind=jnp.bfloat16):
    entries = width * jax.random.normal(stream_key, shape, jnp.float32)
    if shards:
        entries = entries * block_scale(stream_key, shape, shards, -0.22, 0.18)
    return jnp.clip(entries, -reach, reach).astype(kind)


def setup_inputs(seed: int = 0) -> dict:
    splits = jax.random.split(jax.random.key(seed), 16)
    query = draw_query(jax.random.fold_in(splits[15], 71), 0)
    keyval = draw_keyval(jax.random.fold_in(splits[15], 71), 0)
    doc_lengths = jax.vmap(lambda own: uneven(own, DOCS, PACKED_TOKENS, MOST_DOC, 2))(jax.random.split(splits[2], CONTEXT_GROUPS)).reshape((CONTEXT_GROUPS, DOCS)).astype(jnp.int32)
    norm_gain = jnp.clip(1.0 + 0.1 * jax.random.normal(splits[3], (D,), jnp.float32), 0.5, 1.5)
    router_logits = draw_router_logits(jax.random.fold_in(splits[15], 71), 0)
    expert_ids_keys = jax.random.split(jax.random.fold_in(splits[5], 1), CONTEXT_GROUPS * PACKED_TOKENS // TOK)
    expert_ids_turns = jax.random.permutation(jax.random.fold_in(splits[5], 3), CONTEXT_GROUPS * PACKED_TOKENS // TOK)
    expert_ids = jax.vmap(lambda own, number: routed_block(jax.random.fold_in(splits[5], 2), own, number, TOK, EXPERTS, TOP, CAP, 2))(expert_ids_keys, expert_ids_turns).reshape((CONTEXT_GROUPS, PACKED_TOKENS, TOP))
    grad_out = scatter_about(splits[6], (CONTEXT_GROUPS, PACKED_TOKENS, D), 1.0, 6.0, ((0, 16), (1, 8)))
    base_in = scatter_about(splits[7], (EXPERTS, 2, D, FFW), D ** -0.5, 0.09375, ((0, 128),))
    low_in = scatter_about(splits[8], (EXPERTS, 2, D, RK), D ** -0.5, 0.09375, ((0, 128),))
    high_in = scatter_about(splits[9], (EXPERTS, 2, RK, FFW), RK ** -0.5, 1.0, ((0, 128),))
    mag_in = jnp.clip(1.0 + 0.1 * jax.random.normal(splits[10], (EXPERTS, 2, FFW), jnp.float32), 0.5, 1.5)
    base_out = scatter_about(splits[11], (EXPERTS, FFW, D), FFW ** -0.5, 0.21875, ((0, 128),))
    low_out = scatter_about(splits[12], (EXPERTS, FFW, RK), FFW ** -0.5, 0.21875, ((0, 128),))
    high_out = scatter_about(splits[13], (EXPERTS, RK, D), RK ** -0.5, 1.0, ((0, 128),))
    mag_out = jnp.clip(1.0 + 0.1 * jax.random.normal(splits[14], (EXPERTS, D), jnp.float32), 0.5, 1.5)
    return dict(query=query, keyval=keyval, doc_lengths=doc_lengths, norm_gain=norm_gain, router_logits=router_logits, expert_ids=expert_ids, grad_out=grad_out, base_in=base_in, low_in=low_in, high_in=high_in, mag_in=mag_in, base_out=base_out, low_out=low_out, high_out=high_out, mag_out=mag_out)


NEGATIVE = -1e+30
EPSILON = 1e-06

def document_index(positions, doc_ends):
    return lax.optimization_barrier(jnp.sum((positions[:, None] >= doc_ends[None, :]).astype(jnp.int32), axis=1))

def contract(left, right, left_dim, right_dim):
    return lax.dot_general(left, right, (((left_dim,), (right_dim,)), ((), ())), preferred_element_type=jnp.float32)

def column_norm(offset_start, low_rank, high_rank):
    merged = offset_start.astype(jnp.float32) + jnp.dot(low_rank, high_rank, preferred_element_type=jnp.float32)
    return jnp.sqrt(lax.optimization_barrier(jnp.sum(merged * merged, axis=0)))

def dora_expert(inputs, cotangent, base_in, low_in, high_in, mag_in, base_out, low_out, high_out, mag_out):
    linear = []
    low_acts = []
    norms_in = []
    for branch in range(2):
        norms_in.append(column_norm(base_in[branch], low_in[branch], high_in[branch]))
        low_act = jnp.dot(inputs, low_in[branch], preferred_element_type=jnp.float32).astype(jnp.bfloat16)
        low_acts.append(low_act)
        linear.append(jnp.dot(inputs, base_in[branch], preferred_element_type=jnp.float32) + jnp.dot(low_act, high_in[branch], preferred_element_type=jnp.float32))
    scales_in = [mag_in[branch] / norms_in[branch] for branch in range(2)]
    gate_value = linear[0] * scales_in[0]
    up_value = linear[1] * scales_in[1]
    sigmoid = jax.nn.sigmoid(gate_value)
    activated = gate_value * sigmoid
    hidden_units = (activated * up_value).astype(jnp.bfloat16)
    norm_out = column_norm(base_out, low_out, high_out)
    scale_out = mag_out / norm_out
    low_down = jnp.dot(hidden_units, low_out, preferred_element_type=jnp.float32).astype(jnp.bfloat16)
    linear_out = jnp.dot(hidden_units, base_out, preferred_element_type=jnp.float32) + jnp.dot(low_down, high_out, preferred_element_type=jnp.float32)
    incoming = cotangent.astype(jnp.float32)
    products = lax.optimization_barrier(jnp.sum(incoming * linear_out * scale_out, axis=1))
    grad_mag_out = lax.optimization_barrier(jnp.sum(incoming * linear_out, axis=0)) / norm_out
    grad_linear_out = (incoming * scale_out).astype(jnp.bfloat16)
    back_low = contract(grad_linear_out, high_out, 1, 1).astype(jnp.bfloat16)
    grad_high_out = contract(low_down, grad_linear_out, 0, 0)
    grad_low_out = contract(hidden_units, back_low, 0, 0)
    grad_hidden = contract(grad_linear_out, base_out, 1, 1) + contract(back_low, low_out, 1, 1)
    grad_values = [grad_hidden * up_value * sigmoid * (1.0 + gate_value * (1.0 - sigmoid)), grad_hidden * activated]
    grad_inputs = jnp.zeros(inputs.shape, jnp.float32)
    grad_low_in = []
    grad_high_in = []
    grad_mag_in = []
    for branch in range(2):
        grad_mag_in.append(lax.optimization_barrier(jnp.sum(grad_values[branch] * linear[branch], axis=0)) / norms_in[branch])
        grad_linear = (grad_values[branch] * scales_in[branch]).astype(jnp.bfloat16)
        back_branch = contract(grad_linear, high_in[branch], 1, 1).astype(jnp.bfloat16)
        grad_high_in.append(contract(low_acts[branch], grad_linear, 0, 0))
        grad_low_in.append(contract(inputs, back_branch, 0, 0))
        grad_inputs = grad_inputs + contract(grad_linear, base_in[branch], 1, 1) + contract(back_branch, low_in[branch], 1, 1)
    grads = (jnp.stack(grad_low_in), jnp.stack(grad_high_in), jnp.stack(grad_mag_in), grad_low_out, grad_high_out, grad_mag_out)
    return (grad_inputs.astype(jnp.bfloat16), products, grads)

def slot_numbers(flat_ids, expert_count):
    onehot = (flat_ids[:, None] == jnp.arange(expert_count, dtype=jnp.int32)[None, :]).astype(jnp.int32)
    before = jnp.cumsum(onehot, axis=0) - onehot
    return lax.optimization_barrier(jnp.sum(before * onehot, axis=1))

def group_scores(query_per_group, keyval_per_group, lengths):
    heads_per_group = QUERY_HEADS // KEYVAL_HEADS
    doc_ends = jnp.cumsum(lengths)
    positions = jnp.arange(PACKED_TOKENS, dtype=jnp.int32)
    documents = document_index(positions, doc_ends)
    allowed = (positions[None, :] <= positions[:, None]) & (documents[None, :] == documents[:, None])
    query_rows = query_per_group.reshape(PACKED_TOKENS, KEYVAL_HEADS, heads_per_group, HEAD_SIZE).astype(jnp.float32)
    key_rows = keyval_per_group[:, :KEYVAL_HEADS * HEAD_SIZE].reshape(PACKED_TOKENS, KEYVAL_HEADS, HEAD_SIZE).astype(jnp.float32)
    value_rows = keyval_per_group[:, KEYVAL_HEADS * HEAD_SIZE:].reshape(PACKED_TOKENS, KEYVAL_HEADS, HEAD_SIZE).astype(jnp.float32)
    raw = jnp.einsum('tkgd,nkd->kgtn', query_rows, key_rows) * HEAD_SIZE ** (-0.5)
    raw = jnp.where(allowed, raw, NEGATIVE)
    peak = lax.optimization_barrier(jnp.max(raw, axis=-1, keepdims=True))
    expo = jnp.where(allowed, jnp.exp(raw - peak), 0.0)
    total = lax.optimization_barrier(jnp.sum(expo, axis=-1, keepdims=True))
    return (expo, total, query_rows, key_rows, value_rows)

def group_forward(query_per_group, keyval_per_group, lengths):
    expo, total, query_rows, key_rows, value_rows = group_scores(query_per_group, keyval_per_group, lengths)
    weights = lax.optimization_barrier(expo.astype(jnp.bfloat16)).astype(jnp.float32)
    heads_out = jnp.einsum('kgtn,nkd->kgtd', weights, value_rows) / total
    return heads_out.transpose(2, 0, 1, 3).reshape(PACKED_TOKENS, QUERY_HEADS * HEAD_SIZE)

def group_backward(query_per_group, keyval_per_group, lengths, gradient_per_group, attention_per_group):
    heads_per_group = QUERY_HEADS // KEYVAL_HEADS
    expo, total, query_rows, key_rows, value_rows = group_scores(query_per_group, keyval_per_group, lengths)
    prob = expo / total
    gradient_pieces = gradient_per_group.reshape(PACKED_TOKENS, KEYVAL_HEADS, heads_per_group, HEAD_SIZE)
    attention_pieces = attention_per_group.reshape(PACKED_TOKENS, KEYVAL_HEADS, heads_per_group, HEAD_SIZE)
    delta = lax.optimization_barrier(jnp.sum(gradient_pieces * attention_pieces, axis=-1)).transpose(1, 2, 0)[..., None]
    grad_heads = lax.optimization_barrier(gradient_pieces.astype(jnp.bfloat16)).astype(jnp.float32)
    dprob = jnp.einsum('tkgd,nkd->kgtn', grad_heads, value_rows)
    dscore = lax.optimization_barrier((prob * (dprob - delta)).astype(jnp.bfloat16)).astype(jnp.float32)
    grad_q = jnp.einsum('kgtn,nkd->tkgd', dscore, key_rows) * HEAD_SIZE ** (-0.5)
    key_gradient = jnp.einsum('kgtn,tkgd->nkd', dscore, query_rows) * HEAD_SIZE ** (-0.5)
    prob_rounded = lax.optimization_barrier(prob.astype(jnp.bfloat16)).astype(jnp.float32)
    value_gradient = jnp.einsum('kgtn,tkgd->nkd', prob_rounded, grad_heads)
    keyval_gradient = jnp.concatenate([key_gradient.reshape(PACKED_TOKENS, KEYVAL_HEADS * HEAD_SIZE), value_gradient.reshape(PACKED_TOKENS, KEYVAL_HEADS * HEAD_SIZE)], axis=1)
    return (grad_q.reshape(PACKED_TOKENS, QUERY_HEADS * HEAD_SIZE).astype(jnp.bfloat16), keyval_gradient.astype(jnp.bfloat16))

def reference(query, keyval, doc_lengths, norm_gain, router_logits, expert_ids, grad_out, base_in, low_in, high_in, mag_in, base_out, low_out, high_out, mag_out):
    rows_all = CONTEXT_GROUPS * PACKED_TOKENS
    attn = lax.map(lambda item: group_forward(item[0], item[1], item[2]), (query, keyval, doc_lengths))
    attn = attn.reshape(rows_all, D)
    hidden = lax.optimization_barrier(attn.astype(jnp.bfloat16)).astype(jnp.float32)
    rinv = lax.rsqrt(lax.optimization_barrier(jnp.mean(hidden * hidden, axis=-1, keepdims=True)) + EPSILON)
    normed = (hidden * rinv * norm_gain).astype(jnp.bfloat16)
    logits = router_logits.reshape(rows_all, TOP)
    gate_peak = lax.optimization_barrier(jnp.max(logits, axis=-1, keepdims=True))
    gate_expo = jnp.exp(logits - gate_peak)
    gates = gate_expo / lax.optimization_barrier(jnp.sum(gate_expo, axis=-1, keepdims=True))
    gates_flat = gates.reshape(rows_all * TOP)
    blocks = expert_ids.reshape(CONTEXT_GROUPS, N_CTX, TOK * TOP)
    slots = jax.vmap(jax.vmap(lambda flat: slot_numbers(flat, EXPERTS)))(blocks)
    source = jnp.arange(N_CTX, dtype=jnp.int32)[None, :, None] * N_EP + jnp.arange(CONTEXT_GROUPS, dtype=jnp.int32)[:, None, None]
    source = jnp.broadcast_to(source, blocks.shape)
    assign = jnp.arange(rows_all * TOP, dtype=jnp.int32).reshape(CONTEXT_GROUPS, N_CTX, TOK * TOP)
    table = jnp.full((EXPERTS, EXPERTS, CAP), -1, jnp.int32).at[blocks, source, slots].set(assign)
    grad_flat = grad_out.reshape(rows_all, D)

    def expert_step(carry, items):
        grad_normed, grad_gate = carry
        table_e, bin_e, lin_e, hin_e, min_e, bout_e, lout_e, hout_e, mout_e = items
        flat = table_e.reshape(EXPERTS * CAP)
        valid = flat >= 0
        safe = jnp.where(valid, flat, 0)
        token = safe // TOP
        inputs = jnp.where(valid[:, None], normed[token], jnp.zeros((), jnp.bfloat16))
        cotangent = jnp.where(valid[:, None], grad_flat[token], jnp.zeros((), jnp.bfloat16))
        grad_rows, products, grads = dora_expert(inputs, cotangent, bin_e, lin_e, hin_e, min_e, bout_e, lout_e, hout_e, mout_e)
        weight = jnp.where(valid, gates_flat[safe], 0.0)
        grad_normed = grad_normed.at[token].add(weight[:, None] * grad_rows.astype(jnp.float32))
        rounded = lax.optimization_barrier(products.astype(jnp.bfloat16)).astype(jnp.float32)
        grad_gate = grad_gate.at[safe].add(jnp.where(valid, rounded, 0.0))
        return ((grad_normed, grad_gate), grads)
    init = (jnp.zeros((rows_all, D), jnp.float32), jnp.zeros((rows_all * TOP,), jnp.float32))
    (grad_normed, grad_gate), expert_grads = lax.scan(expert_step, init, (table, base_in, low_in, high_in, mag_in, base_out, low_out, high_out, mag_out))
    grad_gate = grad_gate.reshape(rows_all, TOP)
    grad_logits = gates * (grad_gate - lax.optimization_barrier(jnp.sum(gates * grad_gate, axis=-1, keepdims=True)))
    scaled = grad_normed * norm_gain
    grad_attn = grad_flat.astype(jnp.float32) + rinv * scaled - hidden * (rinv * rinv * rinv) * lax.optimization_barrier(jnp.mean(hidden * scaled, axis=-1, keepdims=True))
    grad_query, grad_keyval = lax.map(lambda item: group_backward(item[0], item[1], item[2], item[3], item[4]), (query, keyval, doc_lengths, grad_attn.reshape(CONTEXT_GROUPS, PACKED_TOKENS, D), attn.reshape(CONTEXT_GROUPS, PACKED_TOKENS, D)))
    return (grad_query, grad_keyval, grad_logits.reshape(CONTEXT_GROUPS, PACKED_TOKENS, TOP), expert_grads[0], expert_grads[1], expert_grads[2], expert_grads[3], expert_grads[4], expert_grads[5])
```

```python
import functools

import jax
import jax.numpy as jnp
from jax import lax
from jax.experimental import pallas as pl
from jax.experimental.pallas import tpu as pltpu
from jax.sharding import PartitionSpec as P

F32 = jnp.float32
BF16 = jnp.bfloat16
MESH = pl.DeviceIdType.MESH
HEAD = 128
NEGATIVE = -1e30
EPSILON = 1e-06
CAP = 4
BLOCK = 16
GROUP = 256
PER_GROUP = GROUP // BLOCK
REACH = 4
MB = 1 << 20


def params(megabytes):
    return pltpu.CompilerParams(vmem_limit_bytes=megabytes * MB)


def cost(flops, size, transcendentals=0):
    return pl.CostEstimate(flops=flops, bytes_accessed=size, transcendentals=transcendentals)


def iota(shape, dim):
    return lax.broadcasted_iota(jnp.int32, shape, dim)


def dot(left, right):
    return jnp.dot(left, right, preferred_element_type=F32)


def contract(left, right, left_dim, right_dim):
    return lax.dot_general(
        left, right, (((left_dim,), (right_dim,)), ((), ())), preferred_element_type=F32
    )


def is_row(row, col, slots, halves):
    pieces = BLOCK // (slots * halves)
    span = PER_GROUP * slots * halves
    return (
        (row // span == (col // (slots * halves)) % pieces)
        & ((row // (PER_GROUP * slots)) % halves == (col // slots) % halves)
        & ((row // slots) % PER_GROUP == col // BLOCK)
        & (row % slots == col % slots)
    )


def to_rows(slots, halves):
    same = is_row(iota((GROUP, GROUP), 0), iota((GROUP, GROUP), 1), slots, halves)
    return same.astype(F32).astype(BF16)


def to_blocks(slots, halves):
    same = is_row(iota((GROUP, GROUP), 1), iota((GROUP, GROUP), 0), slots, halves)
    return same.astype(F32).astype(BF16)


def dispatch_kernel(with_norm, slots_ref, rows_ref, gain_ref, *rest):
    outs, rinv_ref, stack = rest[:-2], rest[-2], rest[-1]
    tokens, width = rows_ref.shape
    slots = CAP // len(outs)
    pieces = BLOCK // slots
    piece = width // pieces

    @pl.when(pl.program_id(0) == 0)
    def _():
        if with_norm:
            square = jnp.zeros((tokens, 1), F32)
            for p in range(pieces):
                part = rows_ref[:, p * piece : (p + 1) * piece].astype(F32)
                square = square + jnp.sum(part * part, axis=1, keepdims=True)
            rinv = lax.rsqrt(square / width + EPSILON)
        else:
            rinv = jnp.ones((tokens, 1), F32)
        rinv_ref[...] = rinv
        for p in range(pieces):
            cols = slice(p * piece, (p + 1) * piece)
            part = rows_ref[:, cols]
            if with_norm:
                part = (part.astype(F32) * rinv * gain_ref[:, cols]).astype(BF16)
            stack[p * tokens : (p + 1) * tokens, :] = part

    spread = (iota((GROUP, PER_GROUP), 0) // BLOCK == iota((GROUP, PER_GROUP), 1)).astype(F32)
    slot = dot(spread.astype(BF16), slots_ref[...].astype(BF16))
    row = iota((GROUP, tokens), 0)
    for half, out_ref in enumerate(outs):
        hit = slot == (half * slots + row % slots).astype(F32)
        parts = []
        for p in range(pieces):
            own = hit & ((row // slots) % pieces == p)
            parts.append(jnp.where(own, 1.0, 0.0).astype(BF16))
        out_ref[...] = dot(jnp.concatenate(parts, axis=1), stack[...]).astype(BF16)


def dispatch(slots, rows, gain, with_norm, halves):
    experts, tokens = slots.shape
    width = rows.shape[1]
    total = experts * BLOCK
    pieces = BLOCK * halves // CAP
    piece = width // pieces
    whole = lambda shape: pl.BlockSpec(shape, lambda i: (0, 0))
    return pl.pallas_call(
        functools.partial(dispatch_kernel, with_norm),
        grid=(total // GROUP,),
        in_specs=[
            pl.BlockSpec((PER_GROUP, tokens), lambda i: (i, 0)),
            whole((tokens, width)),
            whole((1, width)),
        ],
        out_specs=[pl.BlockSpec((GROUP, piece), lambda i: (i, 0))] * halves + [whole((tokens, 1))],
        out_shape=[jax.ShapeDtypeStruct((total, piece), BF16)] * halves
        + [jax.ShapeDtypeStruct((tokens, 1), F32)],
        scratch_shapes=[pltpu.VMEM((pieces * tokens, piece), BF16)],
        compiler_params=params(60),
        cost_estimate=cost(2 * total * tokens * width * halves, 10 * MB),
        name="dispatch",
    )(slots, rows, gain)


def unpack_kernel(halves, blocks_ref, out_ref):
    piece = blocks_ref.shape[1]
    slots = CAP // halves
    pieces = BLOCK // CAP
    rows = dot(to_rows(slots, halves), blocks_ref[...]).astype(BF16)
    count = PER_GROUP * slots
    for p in range(pieces):
        for half in range(halves):
            first = (p * halves + half) * count
            out_ref[half, :, p * piece : (p + 1) * piece] = rows[first : first + count, :]


def unpack(blocks, halves):
    total, piece = blocks.shape
    pieces = BLOCK // CAP
    count = total // pieces // halves
    return pl.pallas_call(
        functools.partial(unpack_kernel, halves),
        grid=(total // GROUP,),
        in_specs=[pl.BlockSpec((GROUP, piece), lambda i: (i, 0))],
        out_specs=pl.BlockSpec(
            (halves, GROUP // pieces // halves, pieces * piece), lambda i: (0, i, 0)
        ),
        out_shape=jax.ShapeDtypeStruct((halves, count, pieces * piece), BF16),
        compiler_params=params(60),
        cost_estimate=cost(2 * total * GROUP * piece, 8 * MB),
        name="unpack",
    )(blocks)


def neighbours(position, count):
    near = []
    for j in range(1, REACH + 1):
        near.append((position + j < count, j))
        near.append((position >= j, -j))
    return near


def greet(position, count):
    barrier = pltpu.get_barrier_semaphore()
    for present, j in neighbours(position, count):

        @pl.when(present)
        def _():
            pl.semaphore_signal(
                barrier, inc=1, device_id={"ctx": position + j}, device_id_type=MESH
            )

    peers = jnp.minimum(position, REACH) + jnp.minimum(count - 1 - position, REACH)
    pl.semaphore_wait(barrier, peers)


def gather_kernel(count, own_ref, seen_ref, send_sem, recv_sem, own_sem):
    tokens = own_ref.shape[0]
    me = lax.axis_index("ctx")

    def copy(j):
        return pltpu.make_async_remote_copy(
            src_ref=own_ref,
            dst_ref=seen_ref.at[pl.ds((REACH - j) * tokens, tokens)],
            send_sem=send_sem.at[j - 1],
            recv_sem=recv_sem.at[j - 1],
            device_id={"ctx": me + j},
            device_id_type=MESH,
        )

    keep = pltpu.make_async_copy(own_ref, seen_ref.at[pl.ds(REACH * tokens, tokens)], own_sem)
    keep.start()
    greet(me, count)
    for j in range(REACH, 0, -1):

        @pl.when(me + j < count)
        def _():
            copy(j).start()

    for j in range(1, REACH + 1):

        @pl.when(me < j)
        def _():
            seen_ref[(REACH - j) * tokens : (REACH - j + 1) * tokens, :] = jnp.zeros(
                own_ref.shape, own_ref.dtype
            )

    keep.wait()
    for j in range(1, REACH + 1):

        @pl.when(me >= j)
        def _():
            copy(j).wait_recv()

        @pl.when(me + j < count)
        def _():
            copy(j).wait_send()


def gather(own, count):
    tokens, width = own.shape
    vmem = pl.BlockSpec(memory_space=pltpu.VMEM)
    return pl.pallas_call(
        functools.partial(gather_kernel, count),
        in_specs=[vmem],
        out_specs=vmem,
        out_shape=jax.ShapeDtypeStruct(((REACH + 1) * tokens, width), own.dtype),
        scratch_shapes=[
            pltpu.SemaphoreType.DMA((REACH,)),
            pltpu.SemaphoreType.DMA((REACH,)),
            pltpu.SemaphoreType.DMA,
        ],
        compiler_params=pltpu.CompilerParams(
            collective_id=0, has_side_effects=True, vmem_limit_bytes=60 * MB
        ),
        name="gather",
    )(own)


def scatter_kernel(count, kv_heads, *rest):
    terms, (out_ref, landed, send_sem, recv_sem) = rest[:kv_heads], rest[kv_heads:]
    tokens = out_ref.shape[0]
    half = out_ref.shape[1] // 2
    me = lax.axis_index("ctx")

    def copy(j, m):
        return pltpu.make_async_remote_copy(
            src_ref=terms[m].at[pl.ds((REACH - j) * tokens, tokens)],
            dst_ref=landed.at[j - 1, m],
            send_sem=send_sem.at[j - 1, m],
            recv_sem=recv_sem.at[j - 1, m],
            device_id={"ctx": me - j},
            device_id_type=MESH,
        )

    greet(me, count)
    for j in range(REACH, 0, -1):

        @pl.when(me >= j)
        def _():
            for m in range(kv_heads):
                copy(j, m).start()

    for j in range(1, REACH + 1):

        @pl.when(me + j < count)
        def _():
            for m in range(kv_heads):
                copy(j, m).wait_recv()

        @pl.when(me + j >= count)
        def _():
            landed[j - 1] = jnp.zeros(landed.shape[1:], landed.dtype)

        @pl.when(me >= j)
        def _():
            for m in range(kv_heads):
                copy(j, m).wait_send()

    for m in range(kv_heads):
        total = terms[m][REACH * tokens :, :].astype(F32)
        for j in range(REACH):
            total = total + landed[j, m].astype(F32)
        out_ref[:, m * HEAD : (m + 1) * HEAD] = total[:, :HEAD].astype(BF16)
        out_ref[:, half + m * HEAD : half + (m + 1) * HEAD] = total[:, HEAD:].astype(BF16)


def scatter(terms, tokens, count):
    kv_heads = len(terms)
    width = terms[0].shape[1]
    vmem = pl.BlockSpec(memory_space=pltpu.VMEM)
    return pl.pallas_call(
        functools.partial(scatter_kernel, count, kv_heads),
        in_specs=[vmem] * kv_heads,
        out_specs=vmem,
        out_shape=jax.ShapeDtypeStruct((tokens, kv_heads * width), BF16),
        scratch_shapes=[
            pltpu.VMEM((REACH, kv_heads, tokens, width), BF16),
            pltpu.SemaphoreType.DMA((REACH, kv_heads)),
            pltpu.SemaphoreType.DMA((REACH, kv_heads)),
        ],
        compiler_params=pltpu.CompilerParams(
            collective_id=1, has_side_effects=True, vmem_limit_bytes=60 * MB
        ),
        name="scatter",
    )(*terms)


def visible(place_ref, window, tokens):
    kpos = place_ref[0] + iota((window, tokens), 0)
    qpos = place_ref[1] + iota((window, tokens), 1)
    kdoc = jnp.zeros((window, tokens), jnp.int32)
    qdoc = jnp.zeros((window, tokens), jnp.int32)
    for d in range(4):
        end = place_ref[2 + d]
        kdoc = kdoc + (kpos >= end).astype(jnp.int32)
        qdoc = qdoc + (qpos >= end).astype(jnp.int32)
    return (kpos >= 0) & (kpos <= qpos) & (kdoc == qdoc)


def head_pair(ref, h):
    return jnp.concatenate(
        [ref[:, h * HEAD : (h + 1) * HEAD], ref[:, (h + 1) * HEAD : (h + 2) * HEAD]], axis=0
    )


def attend_kernel(heads, per_kv, place_ref, query_ref, keyval_ref, prob_ref, out_ref, bias):
    tokens = query_ref.shape[0]
    window = keyval_ref.shape[0]
    step = pl.program_id(0)
    half = keyval_ref.shape[1] // 2
    scale = HEAD ** (-0.5)

    @pl.when(step == 0)
    def _():
        hidden = jnp.where(visible(place_ref, window, tokens), 0.0, NEGATIVE)
        bias[:, :tokens] = hidden
        bias[:, tokens:] = hidden

    for m in range(half // HEAD):

        @pl.when(step // (per_kv // heads) == m)
        def _():
            keys = keyval_ref[:, m * HEAD : (m + 1) * HEAD]
            values_t = keyval_ref[:, half + m * HEAD : half + (m + 1) * HEAD].T
            for h in range(0, heads, 2):
                raw = contract(keys, head_pair(query_ref, h), 1, 1) * scale + bias[...]
                peak = jnp.max(raw, axis=0, keepdims=True)
                expo = jnp.exp(raw - peak)
                total = jnp.sum(expo, axis=0, keepdims=True)
                prob = (expo * (1.0 / total)).astype(BF16)
                prob_ref[0, :, h * tokens : (h + 2) * tokens] = prob
                mixed = dot(values_t, prob).T.astype(BF16)
                out_ref[:, h * HEAD : (h + 1) * HEAD] = mixed[:tokens]
                out_ref[:, (h + 1) * HEAD : (h + 2) * HEAD] = mixed[tokens:]


def attend(place, query, keyval):
    tokens, width = query.shape
    window = keyval.shape[0]
    kv_heads = keyval.shape[1] // 2 // HEAD
    per_kv = width // HEAD // kv_heads
    heads = 4
    steps = width // HEAD // heads
    return pl.pallas_call(
        functools.partial(attend_kernel, heads, per_kv),
        grid=(steps,),
        in_specs=[
            pl.BlockSpec(memory_space=pltpu.SMEM),
            pl.BlockSpec((tokens, heads * HEAD), lambda i: (0, i)),
            pl.BlockSpec(keyval.shape, lambda i: (0, 0)),
        ],
        out_specs=[
            pl.BlockSpec((1, window, heads * tokens), lambda i: (i, 0, 0)),
            pl.BlockSpec((tokens, heads * HEAD), lambda i: (0, i)),
        ],
        out_shape=[
            jax.ShapeDtypeStruct((steps, window, heads * tokens), BF16),
            jax.ShapeDtypeStruct((tokens, width), BF16),
        ],
        scratch_shapes=[pltpu.VMEM((window, 2 * tokens), F32)],
        compiler_params=params(60),
        cost_estimate=cost(4 * tokens * width * window, 9 * MB, tokens * width * window // HEAD),
        name="attend",
    )(place, query, keyval)


def attend_back_kernel(
    heads, query_ref, grad_ref, prob_ref, keys_ref, values_ref,
    grad_query_ref, grad_keyval_ref, key_sum, value_sum,
):
    step = pl.program_id(0)
    tokens = query_ref.shape[0]
    scale = HEAD ** (-0.5)

    @pl.when(step == 0)
    def _():
        key_sum[...] = jnp.zeros_like(key_sum)
        value_sum[...] = jnp.zeros_like(value_sum)

    keys_t = keys_ref[...].T
    values = values_ref[...]
    for h in range(0, heads, 2):
        grad = head_pair(grad_ref, h)
        prob = prob_ref[0, :, h * tokens : (h + 2) * tokens]
        wide = prob.astype(F32)
        moved = wide * contract(values, grad, 1, 1)
        delta = jnp.sum(moved, axis=0, keepdims=True)
        dscore = (moved - wide * delta).astype(BF16)
        grad_query = (dot(keys_t, dscore) * scale).T.astype(BF16)
        grad_query_ref[:, h * HEAD : (h + 1) * HEAD] = grad_query[:tokens]
        grad_query_ref[:, (h + 1) * HEAD : (h + 2) * HEAD] = grad_query[tokens:]
        key_sum[...] += dot(dscore, head_pair(query_ref, h))
        value_sum[...] += dot(prob, grad)

    @pl.when(step == pl.num_programs(0) - 1)
    def _():
        grad_keyval_ref[:, :HEAD] = (key_sum[...] * scale).astype(BF16)
        grad_keyval_ref[:, HEAD:] = value_sum[...].astype(BF16)


def attend_back(m, query, grad, prob, keyval):
    tokens, width = query.shape
    window = keyval.shape[0]
    kv_heads = keyval.shape[1] // 2 // HEAD
    heads = prob.shape[2] // tokens
    steps = prob.shape[0] // kv_heads
    rows = pl.BlockSpec((tokens, heads * HEAD), lambda i: (0, m * steps + i))
    return pl.pallas_call(
        functools.partial(attend_back_kernel, heads),
        grid=(steps,),
        in_specs=[
            rows,
            rows,
            pl.BlockSpec((1,) + prob.shape[1:], lambda i: (m * steps + i, 0, 0)),
            pl.BlockSpec((window, HEAD), lambda i: (0, m)),
            pl.BlockSpec((window, HEAD), lambda i: (0, kv_heads + m)),
        ],
        out_specs=[
            pl.BlockSpec((tokens, heads * HEAD), lambda i: (0, i)),
            pl.BlockSpec((window, 2 * HEAD), lambda i: (0, 0)),
        ],
        out_shape=[
            jax.ShapeDtypeStruct((tokens, width // kv_heads), BF16),
            jax.ShapeDtypeStruct((window, 2 * HEAD), BF16),
        ],
        scratch_shapes=[pltpu.VMEM((window, HEAD), F32), pltpu.VMEM((window, HEAD), F32)],
        compiler_params=params(60),
        cost_estimate=cost(4 * tokens * width * window, 5 * MB),
        name="attend_back",
    )(query, grad, prob, keyval, keyval)


def combine_terms(half, halves, tokens, slots_ref, gates_ref, blocks_ref):
    step = pl.program_id(0)
    count = blocks_ref.shape[0]
    experts = slots_ref.shape[1]
    slots = CAP // halves
    pieces = BLOCK // slots
    spread = (
        iota((experts, count), 0) == step * (count // BLOCK) + iota((experts, count), 1) // BLOCK
    ).astype(F32).astype(BF16)
    slot = dot(slots_ref[...].astype(BF16), spread)
    gate = dot(gates_ref[...].astype(BF16), spread)
    col = iota((tokens, count), 1)
    gate = jnp.where(slot == (half * slots + col % slots).astype(F32), gate, 0.0)
    parts = []
    for p in range(pieces):
        parts.append(jnp.where((col // slots) % pieces == p, gate, 0.0).astype(BF16))
    return dot(jnp.concatenate(parts, axis=0), blocks_ref[...])


def combine_first_kernel(halves, tokens, slots_ref, gates_ref, blocks_ref, acc_ref):
    part = combine_terms(0, halves, tokens, slots_ref, gates_ref, blocks_ref)

    @pl.when(pl.program_id(0) == 0)
    def _():
        acc_ref[...] = part

    @pl.when(pl.program_id(0) != 0)
    def _():
        acc_ref[...] += part


def combine_last_kernel(
    halves, slots_ref, gates_ref, blocks_ref, first_ref, gain_ref, grad_out_ref, hidden_ref,
    rinv_ref, grad_ref, acc,
):
    step = pl.program_id(0)
    tokens, width = hidden_ref.shape
    pieces = acc.shape[0] // tokens
    piece = width // pieces
    part = combine_terms(halves - 1, halves, tokens, slots_ref, gates_ref, blocks_ref)

    @pl.when(step == 0)
    def _():
        acc[...] = first_ref[...] + part

    @pl.when(step != 0)
    def _():
        acc[...] += part

    @pl.when(step == pl.num_programs(0) - 1)
    def _():
        rinv = rinv_ref[...]
        mean = jnp.zeros((tokens, 1), F32)
        for p in range(pieces):
            cols = slice(p * piece, (p + 1) * piece)
            rows = slice(p * tokens, (p + 1) * tokens)
            scaled = acc[rows, :] * gain_ref[:, cols]
            acc[rows, :] = scaled
            mean = mean + jnp.sum(hidden_ref[:, cols].astype(F32) * scaled, axis=1, keepdims=True)
        mean = mean / width * (rinv * rinv * rinv)
        for p in range(pieces):
            cols = slice(p * piece, (p + 1) * piece)
            rows = slice(p * tokens, (p + 1) * tokens)
            grad = (
                grad_out_ref[:, cols].astype(F32)
                + rinv * acc[rows, :]
                - hidden_ref[:, cols].astype(F32) * mean
            )
            grad_ref[:, cols] = grad.astype(BF16)


def combine_first(slots, gates, blocks, halves):
    tokens = slots.shape[0]
    total, piece = blocks.shape
    pieces = BLOCK * halves // CAP
    rows = 2 * GROUP
    whole = lambda shape: pl.BlockSpec(shape, lambda i: (0, 0))
    return pl.pallas_call(
        functools.partial(combine_first_kernel, halves, tokens),
        grid=(total // rows,),
        in_specs=[
            whole(slots.shape),
            whole(gates.shape),
            pl.BlockSpec((rows, piece), lambda i: (i, 0)),
        ],
        out_specs=whole((pieces * tokens, piece)),
        out_shape=jax.ShapeDtypeStruct((pieces * tokens, piece), F32),
        compiler_params=params(60),
        cost_estimate=cost(1, 1),
        name="combine_first",
    )(slots, gates, blocks)


def combine_last(slots, gates, blocks, first, gain, grad_out, hidden, rinv, halves):
    tokens, width = hidden.shape
    total, piece = blocks.shape
    rows = 2 * GROUP
    whole = lambda shape: pl.BlockSpec(shape, lambda i: (0, 0))
    return pl.pallas_call(
        functools.partial(combine_last_kernel, halves),
        grid=(total // rows,),
        in_specs=[
            whole(slots.shape),
            whole(gates.shape),
            pl.BlockSpec((rows, piece), lambda i: (i, 0)),
            whole(first.shape),
            whole(gain.shape),
            whole(grad_out.shape),
            whole(hidden.shape),
            whole(rinv.shape),
        ],
        out_specs=whole((tokens, width)),
        out_shape=jax.ShapeDtypeStruct((tokens, width), BF16),
        scratch_shapes=[pltpu.VMEM(first.shape, F32)],
        compiler_params=params(60),
        cost_estimate=cost(2 * total * tokens * width, 8 * MB),
        name="combine_last",
    )(slots, gates, blocks, first, gain, grad_out, hidden, rinv)


def expert_kernel(
    slots, blocks_hbm, base_hbm, low_ref, high_ref, scale_ref, grad_hidden_ref,
    out_hbm, inputs_hbm, units_ref, low_act_ref, grad_linear_ref, back_ref, products_ref, mag_ref,
    blocks, base, inputs, linear, out_rows, in_sem, base_sem, row_sem, out_sem,
):
    groups = blocks.shape[0] // GROUP
    piece = blocks.shape[1]
    pieces = BLOCK // slots
    span = PER_GROUP * slots
    ffw = base.shape[2]
    depth = base.shape[1]
    tile = 256
    tiles = ffw // tile
    rank = high_ref.shape[1]

    def load_blocks(g):
        rows = pl.ds(pl.multiple_of(g * GROUP, GROUP), GROUP)
        return pltpu.make_async_copy(blocks_hbm.at[rows], blocks.at[rows], in_sem.at[g])

    def load_base(n):
        cols = pl.ds(pl.multiple_of((n % tiles) * tile, tile), tile)
        j = n // tiles
        return pltpu.make_async_copy(
            base_hbm.at[j, :, cols], base.at[j, :, cols], base_sem.at[n]
        )

    def store_rows(g):
        rows = pl.ds(pl.multiple_of(g * GROUP, GROUP), GROUP)
        return pltpu.make_async_copy(out_rows.at[rows], out_hbm.at[rows], out_sem.at[g])

    for g in range(groups):
        load_blocks(g).start()
    for n in range(2 * tiles):
        load_base(n).start()

    permute = to_rows(slots, 1)

    def unpack_group(g, _):
        load_blocks(g).wait()
        rows = dot(permute, blocks[pl.ds(pl.multiple_of(g * GROUP, GROUP), GROUP), :]).astype(BF16)
        place = pl.ds(pl.multiple_of(g * span, span), span)
        for p in range(pieces):
            inputs[place, p * piece : (p + 1) * piece] = rows[p * span : (p + 1) * span, :]
        return 0

    lax.fori_loop(0, groups, unpack_group, 0)
    keep = pltpu.make_async_copy(inputs, inputs_hbm, row_sem)
    keep.start()

    low_act_ref[...] = dot(inputs[...], low_ref[...]).astype(BF16)

    def forward(n, _):
        load_base(n).wait()
        j = n // tiles
        cols = pl.ds(pl.multiple_of((n % tiles) * tile, tile), tile)
        linear[j, :, cols] = dot(inputs[...], base[j, :, cols])
        return 0

    lax.fori_loop(0, 2 * tiles, forward, 0)

    for n in range(tiles):
        cols = slice(n * tile, (n + 1) * tile)
        gate_linear = linear[0, :, cols] + dot(low_act_ref[:, :rank], high_ref[0, :, cols])
        up_linear = linear[1, :, cols] + dot(low_act_ref[:, rank:], high_ref[1, :, cols])
        gate_scale = scale_ref[0:1, cols]
        up_scale = scale_ref[1:2, cols]
        gate = gate_linear * gate_scale
        up = up_linear * up_scale
        sigmoid = 1.0 / (1.0 + jnp.exp(-gate))
        active = gate * sigmoid
        units = (active * up).astype(BF16)
        units_ref[:, cols] = units
        grad_hidden = grad_hidden_ref[:, cols]
        part = jnp.sum(units.astype(F32) * grad_hidden, axis=1, keepdims=True)
        if n == 0:
            products_ref[...] = part
        else:
            products_ref[...] += part
        grad_gate = grad_hidden * up * sigmoid * (1.0 + gate * (1.0 - sigmoid))
        grad_up = grad_hidden * active
        mag_ref[0:1, cols] = jnp.sum(grad_gate * gate_linear, axis=0, keepdims=True)
        mag_ref[1:2, cols] = jnp.sum(grad_up * up_linear, axis=0, keepdims=True)
        grad_linear_ref[0, :, cols] = (grad_gate * gate_scale).astype(BF16)
        grad_linear_ref[1, :, cols] = (grad_up * up_scale).astype(BF16)

    for j in range(2):
        back_ref[:, j * rank : (j + 1) * rank] = contract(
            grad_linear_ref[j], high_ref[j], 1, 1
        ).astype(BF16)

    keep.wait()

    def backward(n, _):
        rows = pl.ds(pl.multiple_of(n * tile, tile), tile)
        grad = contract(grad_linear_ref[0], base[0, rows, :], 1, 1)
        grad = grad + contract(grad_linear_ref[1], base[1, rows, :], 1, 1)
        grad = grad + contract(back_ref[...], low_ref[rows, :], 1, 1)
        inputs[:, rows] = grad.astype(BF16)
        return 0

    lax.fori_loop(0, depth // tile, backward, 0)

    arrange = to_blocks(slots, 1)

    def pack_group(g, _):
        place = pl.ds(pl.multiple_of(g * span, span), span)
        stack = jnp.concatenate(
            [inputs[place, p * piece : (p + 1) * piece] for p in range(pieces)], axis=0
        )
        rows = pl.ds(pl.multiple_of(g * GROUP, GROUP), GROUP)
        out_rows[rows, :] = dot(arrange, stack).astype(BF16)
        store_rows(g).start()
        return 0

    lax.fori_loop(0, groups, pack_group, 0)
    for g in range(groups):
        store_rows(g).wait()


def expert(slots, blocks, base, low, high, scale, grad_hidden):
    total, piece = blocks.shape
    branches, depth, ffw = base.shape
    count = total * slots // BLOCK
    rank2 = low.shape[1]
    groups = total // GROUP
    vmem = pl.BlockSpec(memory_space=pltpu.VMEM)
    hbm = pl.BlockSpec(memory_space=pl.ANY)
    return pl.pallas_call(
        functools.partial(expert_kernel, slots),
        in_specs=[hbm, hbm, vmem, vmem, vmem, vmem],
        out_specs=[hbm, hbm, vmem, vmem, vmem, vmem, vmem, vmem],
        out_shape=[
            jax.ShapeDtypeStruct((total, piece), BF16),
            jax.ShapeDtypeStruct((count, depth), BF16),
            jax.ShapeDtypeStruct((count, ffw), BF16),
            jax.ShapeDtypeStruct((count, rank2), BF16),
            jax.ShapeDtypeStruct((branches, count, ffw), BF16),
            jax.ShapeDtypeStruct((count, rank2), BF16),
            jax.ShapeDtypeStruct((count, 1), F32),
            jax.ShapeDtypeStruct((branches, ffw), F32),
        ],
        scratch_shapes=[
            pltpu.VMEM((total, piece), BF16),
            pltpu.VMEM(base.shape, BF16),
            pltpu.VMEM((count, depth), BF16),
            pltpu.VMEM((branches, count, ffw), F32),
            pltpu.VMEM((total, piece), BF16),
            pltpu.SemaphoreType.DMA((groups,)),
            pltpu.SemaphoreType.DMA((2 * ffw // 256,)),
            pltpu.SemaphoreType.DMA,
            pltpu.SemaphoreType.DMA((groups,)),
        ],
        compiler_params=params(56),
        cost_estimate=cost(4 * count * depth * ffw * branches, 30 * MB),
        name="expert",
    )(blocks, base, low, high, scale, grad_hidden)


def expert_grads_kernel(
    halves, cotangent_ref, grad_ref, base_ref, high_ref, units_ref, low_out_ref, back_low_ref,
    *rest
):
    inputs = rest[:halves]
    low_acts, grad_linears, backs = (
        rest[halves : 2 * halves], rest[2 * halves : 3 * halves], rest[3 * halves : 4 * halves]
    )
    mag_ref, high_grad_ref, low_in_ref, low_grad_ref, high_in_ref, low_down, low_down_t, back_t = (
        rest[4 * halves :]
    )
    count = units_ref.shape[0] // halves
    rank = low_out_ref.shape[1]

    @pl.when(pl.program_id(0) == 0)
    def _():
        low = dot(units_ref[...], low_out_ref[...])
        low_down[...] = low.astype(BF16)
        low_down_t[...] = low.T.astype(BF16)
        low_grad_ref[...] = dot(back_low_ref[...].astype(F32).T.astype(BF16), units_ref[...])
        high_in_ref[...] = jnp.zeros_like(high_in_ref)
        for h in range(halves):
            back_t[h] = backs[h][...].astype(F32).T.astype(BF16)
            low_act_t = low_acts[h][...].astype(F32).T.astype(BF16)
            for j in range(2):
                high_in_ref[j] += dot(low_act_t[j * rank : (j + 1) * rank], grad_linears[h][j])

    mag = jnp.zeros((1, base_ref.shape[1]), F32)
    low_in = jnp.zeros(low_in_ref.shape, F32)
    for h in range(halves):
        rows = slice(h * count, (h + 1) * count)
        linear = dot(units_ref[rows, :], base_ref[...]) + dot(low_down[rows, :], high_ref[...])
        mag = mag + jnp.sum(linear * cotangent_ref[rows, :].astype(F32), axis=0, keepdims=True)
        low_in = low_in + dot(back_t[h], inputs[h][...])
    mag_ref[...] = mag
    low_in_ref[...] = low_in
    high_grad_ref[...] = dot(low_down_t[...], grad_ref[...])


def expert_grads(
    cotangent, grad_linear, base, high, units, low_out, back_low, inputs, low_acts, grad_linears,
    backs,
):
    halves = len(inputs)
    ffw, width = base.shape
    count, rank = back_low.shape
    tile = 512
    whole = lambda array: pl.BlockSpec(array.shape, lambda i: (0,) * array.ndim)
    part = lambda rows: pl.BlockSpec((rows, tile), lambda i: (0, i))
    fixed = [units, low_out, back_low]
    return pl.pallas_call(
        functools.partial(expert_grads_kernel, halves),
        grid=(width // tile,),
        in_specs=[part(count), part(count), part(ffw), part(rank)]
        + [whole(array) for array in fixed]
        + [part(count // halves)] * halves
        + [whole(array) for array in low_acts + grad_linears + backs],
        out_specs=[
            part(1),
            part(rank),
            part(2 * rank),
            pl.BlockSpec((rank, ffw), lambda i: (0, 0)),
            pl.BlockSpec((2, rank, ffw), lambda i: (0, 0, 0)),
        ],
        out_shape=[
            jax.ShapeDtypeStruct((1, width), F32),
            jax.ShapeDtypeStruct((rank, width), F32),
            jax.ShapeDtypeStruct((2 * rank, width), F32),
            jax.ShapeDtypeStruct((rank, ffw), F32),
            jax.ShapeDtypeStruct((2, rank, ffw), F32),
        ],
        scratch_shapes=[
            pltpu.VMEM((count, rank), BF16),
            pltpu.VMEM((rank, count), BF16),
            pltpu.VMEM((halves, 2 * rank, count // halves), BF16),
        ],
        compiler_params=params(60),
        cost_estimate=cost(1, 1),
        name="expert_grads",
    )(cotangent, grad_linear, base, high, *fixed, *inputs, *low_acts, *grad_linears, *backs)


def square_norm(base, low, high):
    merged = base.astype(F32) + dot(low, high)
    return jnp.sqrt(jnp.sum(merged * merged, axis=0))


def shards(
    query, keyval, doc_lengths, norm_gain, router_logits, expert_ids, grad_out,
    base_in, low_in, high_in, mag_in, base_out, low_out, high_out, mag_out,
):
    query, local_kv, grad_out = query[0], keyval[0], grad_out[0]
    base_in, low_in, high_in, mag_in = base_in[0], low_in[0], high_in[0], mag_in[0]
    base_out, low_out, high_out, mag_out = base_out[0], low_out[0], high_out[0], mag_out[0]
    ids = expert_ids[0]
    tokens, width = query.shape
    top = ids.shape[1]
    experts = lax.axis_size("ctx") * lax.axis_size("ep")
    axes = ("ctx", "ep")
    gain = norm_gain[None, :]
    halves = 2
    slots_each = CAP // halves
    ctx_count = lax.axis_size("ctx")

    def exchange(blocks):
        split = blocks.reshape(experts, BLOCK, blocks.shape[1])
        moved = lax.all_to_all(split, axes, split_axis=0, concat_axis=0, tiled=True)
        return moved.reshape(blocks.shape)

    named = jnp.zeros((experts, tokens), jnp.bool_)
    each = jnp.arange(experts, dtype=jnp.int32)[:, None]
    for k in range(top):
        named = named | (ids[:, k][None, :] == each)
    earlier = jnp.arange(tokens)[:, None] < jnp.arange(tokens)[None, :]
    before = dot(named.astype(BF16), earlier.astype(BF16))
    slots = jnp.where(named, before, -1.0)

    seen = gather(local_kv, ctx_count)
    first = lax.axis_index("ctx") * tokens
    place = jnp.concatenate(
        [
            jnp.stack([first - REACH * tokens, first]).astype(jnp.int32),
            jnp.cumsum(doc_lengths[0]).astype(jnp.int32),
        ]
    )

    outgoing_grad, _ = dispatch(slots, grad_out, gain, False, 1)
    outgoing_grad, seen = lax.optimization_barrier((outgoing_grad, seen))
    arrived_grad = exchange(outgoing_grad)

    prob, hidden = attend(place, query, seen)
    *outgoing, rinv = dispatch(slots, hidden, gain, True, halves)

    norm_in = jnp.stack([square_norm(base_in[j], low_in[j], high_in[j]) for j in range(2)])
    scale_in = mag_in / norm_in
    norm_out = square_norm(base_out, low_out, high_out)
    scale_out = mag_out / norm_out
    cotangent = unpack(arrived_grad, halves).reshape(experts * CAP, width)
    grad_linear_out = (cotangent.astype(F32) * scale_out).astype(BF16)
    back_low = contract(grad_linear_out, high_out, 1, 1).astype(BF16)
    grad_hidden = contract(grad_linear_out, base_out, 1, 1) + contract(back_low, low_out, 1, 1)
    low_pair = jnp.concatenate([low_in[0], low_in[1]], axis=1)
    arrived = [exchange(outgoing[0])]
    second, grad_hidden, scale_in, low_pair, _ = lax.optimization_barrier(
        (outgoing[1], grad_hidden, scale_in, low_pair, arrived[0])
    )
    arrived.append(exchange(second))

    rows_each = experts * slots_each
    returned, results = [], []
    for h in range(halves):
        outgoing_rows, *result = expert(
            slots_each, arrived[h], base_in, low_pair, high_in, scale_in,
            grad_hidden[h * rows_each : (h + 1) * rows_each],
        )
        returned.append(exchange(outgoing_rows))
        results.append(result)
    results, first_returned = lax.optimization_barrier((results, returned[0]))
    returned[0] = first_returned
    inputs, units, low_acts, grad_linears, backs, products, mag_sums = zip(*results)

    mag_sum, grad_high_out, low_in_t, low_out_t, grad_high_in = expert_grads(
        cotangent, grad_linear_out, base_out, high_out, jnp.concatenate(units, axis=0), low_out,
        back_low, inputs, low_acts, grad_linears, backs,
    )
    grad_mag_out = mag_sum[0] / norm_out
    grad_low_out = low_out_t.T
    grad_low_in = low_in_t.reshape(2, -1, width).transpose(0, 2, 1)
    grad_mag_in = sum(mag_sums) / norm_in
    products = jnp.concatenate(
        [part.astype(BF16).reshape(experts, slots_each) for part in products], axis=1
    )

    logits = router_logits[0]
    gate_expo = jnp.exp(logits - jnp.max(logits, axis=-1, keepdims=True))
    gates = gate_expo / jnp.sum(gate_expo, axis=-1, keepdims=True)
    dense_gates = jnp.zeros((tokens, experts), F32)
    chosen = [ids[:, k : k + 1] == each.reshape(1, experts) for k in range(top)]
    for k in range(top):
        dense_gates = dense_gates + jnp.where(chosen[k], gates[:, k : k + 1], 0.0)
    token_slots = slots.T
    partial = combine_first(token_slots, dense_gates, returned[0], halves)
    grad_heads = combine_last(
        token_slots, dense_gates, returned[1], partial, gain, grad_out, hidden, rinv, halves
    )
    products, grad_heads = lax.optimization_barrier((products, grad_heads))
    returned_products = lax.all_to_all(products, axes, split_axis=0, concat_axis=0, tiled=True)
    dense_products = jnp.zeros((tokens, experts), F32)
    for r in range(CAP):
        dense_products = dense_products + jnp.where(
            token_slots == r, returned_products[:, r].astype(F32)[None, :], 0.0
        )
    grad_gate = jnp.stack(
        [jnp.sum(jnp.where(chosen[k], dense_products, 0.0), axis=1) for k in range(top)], axis=1
    )
    grad_logits = gates * (grad_gate - jnp.sum(gates * grad_gate, axis=-1, keepdims=True))

    queries, terms = [], []
    for m in range(local_kv.shape[1] // 2 // HEAD):
        query_part, term = attend_back(m, query, grad_heads, prob, seen)
        queries.append(query_part)
        terms.append(term)
    grad_keyval = scatter(terms, tokens, ctx_count)
    grad_query = jnp.concatenate(queries, axis=1)
    return (
        grad_query[None],
        grad_keyval[None],
        grad_logits[None],
        grad_low_in[None],
        grad_high_in[None],
        grad_mag_in[None],
        grad_low_out[None],
        grad_high_out[None],
        grad_mag_out[None],
    )


def solution(mesh):
    rows = P("ep", "ctx", None)
    own = lambda extra: P(("ctx", "ep"), *([None] * extra))
    in_specs = (
        rows, rows, P("ep", None), P(), rows, rows, rows,
        own(3), own(3), own(3), own(2), own(2), own(2), own(2), own(1),
    )
    out_specs = (rows, rows, rows, own(3), own(3), own(2), own(2), own(2), own(1))
    return jax.shard_map(shards, mesh=mesh, in_specs=in_specs, out_specs=out_specs, check_vma=False)
```

```python
import functools

import jax
import jax.numpy as jnp
from jax import lax
from jax.experimental import pallas as pl
from jax.experimental.pallas import tpu as pltpu
from jax.sharding import PartitionSpec as P

F32 = jnp.float32
BF16 = jnp.bfloat16
MESH = pl.DeviceIdType.MESH
HEAD = 128
NEGATIVE = -1e30
EPSILON = 1e-06
CAP = 4
BLOCK = 16
GROUP = 256
PER_GROUP = GROUP // BLOCK
REACH = 4
MB = 1 << 20


def params(megabytes):
    return pltpu.CompilerParams(vmem_limit_bytes=megabytes * MB)


def cost(flops, size, transcendentals=0):
    return pl.CostEstimate(flops=flops, bytes_accessed=size, transcendentals=transcendentals)


def iota(shape, dim):
    return lax.broadcasted_iota(jnp.int32, shape, dim)


def dot(left, right):
    return jnp.dot(left, right, preferred_element_type=F32)


def contract(left, right, left_dim, right_dim):
    return lax.dot_general(
        left, right, (((left_dim,), (right_dim,)), ((), ())), preferred_element_type=F32
    )


def is_row(row, col, slots, halves):
    pieces = BLOCK // (slots * halves)
    span = PER_GROUP * slots * halves
    return (
        (row // span == (col // (slots * halves)) % pieces)
        & ((row // (PER_GROUP * slots)) % halves == (col // slots) % halves)
        & ((row // slots) % PER_GROUP == col // BLOCK)
        & (row % slots == col % slots)
    )


def to_rows(slots, halves):
    same = is_row(iota((GROUP, GROUP), 0), iota((GROUP, GROUP), 1), slots, halves)
    return same.astype(F32).astype(BF16)


def to_blocks(slots, halves):
    same = is_row(iota((GROUP, GROUP), 1), iota((GROUP, GROUP), 0), slots, halves)
    return same.astype(F32).astype(BF16)


def dispatch_kernel(with_norm, slots_ref, rows_ref, gain_ref, *rest):
    outs, rinv_ref, stack = rest[:-2], rest[-2], rest[-1]
    tokens, width = rows_ref.shape
    slots = CAP // len(outs)
    pieces = BLOCK // slots
    piece = width // pieces

    @pl.when(pl.program_id(0) == 0)
    def _():
        if with_norm:
            square = jnp.zeros((tokens, 1), F32)
            for p in range(pieces):
                part = rows_ref[:, p * piece : (p + 1) * piece].astype(F32)
                square = square + jnp.sum(part * part, axis=1, keepdims=True)
            rinv = lax.rsqrt(square / width + EPSILON)
        else:
            rinv = jnp.ones((tokens, 1), F32)
        rinv_ref[...] = rinv
        for p in range(pieces):
            cols = slice(p * piece, (p + 1) * piece)
            part = rows_ref[:, cols]
            if with_norm:
                part = (part.astype(F32) * rinv * gain_ref[:, cols]).astype(BF16)
            stack[p * tokens : (p + 1) * tokens, :] = part

    spread = (iota((GROUP, PER_GROUP), 0) // BLOCK == iota((GROUP, PER_GROUP), 1)).astype(F32)
    slot = dot(spread.astype(BF16), slots_ref[...].astype(BF16))
    row = iota((GROUP, tokens), 0)
    for half, out_ref in enumerate(outs):
        hit = slot == (half * slots + row % slots).astype(F32)
        parts = []
        for p in range(pieces):
            own = hit & ((row // slots) % pieces == p)
            parts.append(jnp.where(own, 1.0, 0.0).astype(BF16))
        out_ref[...] = dot(jnp.concatenate(parts, axis=1), stack[...]).astype(BF16)


def dispatch(slots, rows, gain, with_norm, halves):
    experts, tokens = slots.shape
    width = rows.shape[1]
    total = experts * BLOCK
    pieces = BLOCK * halves // CAP
    piece = width // pieces
    whole = lambda shape: pl.BlockSpec(shape, lambda i: (0, 0))
    return pl.pallas_call(
        functools.partial(dispatch_kernel, with_norm),
        grid=(total // GROUP,),
        in_specs=[
            pl.BlockSpec((PER_GROUP, tokens), lambda i: (i, 0)),
            whole((tokens, width)),
            whole((1, width)),
        ],
        out_specs=[pl.BlockSpec((GROUP, piece), lambda i: (i, 0))] * halves + [whole((tokens, 1))],
        out_shape=[jax.ShapeDtypeStruct((total, piece), BF16)] * halves
        + [jax.ShapeDtypeStruct((tokens, 1), F32)],
        scratch_shapes=[pltpu.VMEM((pieces * tokens, piece), BF16)],
        compiler_params=params(60),
        cost_estimate=cost(2 * total * tokens * width * halves, 10 * MB),
        name="dispatch",
    )(slots, rows, gain)


def unpack_kernel(halves, blocks_ref, out_ref):
    piece = blocks_ref.shape[1]
    slots = CAP // halves
    pieces = BLOCK // CAP
    rows = dot(to_rows(slots, halves), blocks_ref[...]).astype(BF16)
    count = PER_GROUP * slots
    for p in range(pieces):
        for half in range(halves):
            first = (p * halves + half) * count
            out_ref[half, :, p * piece : (p + 1) * piece] = rows[first : first + count, :]


def unpack(blocks, halves):
    total, piece = blocks.shape
    pieces = BLOCK // CAP
    count = total // pieces // halves
    return pl.pallas_call(
        functools.partial(unpack_kernel, halves),
        grid=(total // GROUP,),
        in_specs=[pl.BlockSpec((GROUP, piece), lambda i: (i, 0))],
        out_specs=pl.BlockSpec(
            (halves, GROUP // pieces // halves, pieces * piece), lambda i: (0, i, 0)
        ),
        out_shape=jax.ShapeDtypeStruct((halves, count, pieces * piece), BF16),
        compiler_params=params(60),
        cost_estimate=cost(2 * total * GROUP * piece, 8 * MB),
        name="unpack",
    )(blocks)


def open_kernel(
    count, own_ref, slots_ref, rows_ref, seen_ref, out_hbm, stack, blocks, send_sem, recv_sem,
    own_sem, out_sem,
):
    tokens, width = rows_ref.shape
    pieces = BLOCK // CAP
    piece = width // pieces
    groups = blocks.shape[0] // GROUP
    me = lax.axis_index("ctx")
    core = me % 2
    other = me + 1 - 2 * core

    def slot(j):
        return seen_ref.at[pl.ds((REACH - j) * tokens, tokens)]

    def copy(source, j, target, index):
        return pltpu.make_async_remote_copy(
            src_ref=source,
            dst_ref=slot(j),
            send_sem=send_sem.at[index],
            recv_sem=recv_sem.at[index],
            device_id={"ctx": target},
            device_id_type=MESH,
        )

    near = copy(own_ref, 2, me + 2, 0)
    far = copy(own_ref, 4, me + 4, 1)
    beside = copy(own_ref, 1, other, 2)
    near_even = copy(slot(2), 3, other, 3)
    near_odd = copy(slot(2), 1, other, 3)
    far_odd = copy(slot(4), 3, other, 4)

    keep = pltpu.make_async_copy(own_ref, slot(0), own_sem)
    keep.start()
    barrier = pltpu.get_barrier_semaphore()
    peers = 1
    for offset in (2, 4, -2, -4):
        present = (me + offset >= 0) & (me + offset < count)
        peers = peers + present.astype(jnp.int32)

        @pl.when(present)
        def _():
            pl.semaphore_signal(
                barrier, inc=1, device_id={"ctx": me + offset}, device_id_type=MESH
            )

    pl.semaphore_signal(barrier, inc=1, device_id={"ctx": other}, device_id_type=MESH)
    pl.semaphore_wait(barrier, peers)

    @pl.when(me + 4 < count)
    def _():
        far.start()

    @pl.when(me + 2 < count)
    def _():
        near.start()

    @pl.when(core == 0)
    def _():
        beside.start()

    for j in range(1, REACH + 1):

        @pl.when(me < j)
        def _():
            seen_ref[(REACH - j) * tokens : (REACH - j + 1) * tokens, :] = jnp.zeros(
                own_ref.shape, own_ref.dtype
            )

    for p in range(pieces):
        stack[p * tokens : (p + 1) * tokens, :] = rows_ref[:, p * piece : (p + 1) * piece]
    spread = (iota((GROUP, PER_GROUP), 0) // BLOCK == iota((GROUP, PER_GROUP), 1)).astype(F32)
    spread = spread.astype(BF16)
    row = iota((GROUP, tokens), 0)

    def store(g):
        rows = pl.ds(pl.multiple_of(g * GROUP, GROUP), GROUP)
        return pltpu.make_async_copy(blocks.at[rows], out_hbm.at[rows], out_sem.at[g])

    def pick(g, _):
        named = slots_ref[pl.ds(pl.multiple_of(g * PER_GROUP, PER_GROUP), PER_GROUP), :]
        hit = dot(spread, named.astype(BF16)) == (row % CAP).astype(F32)
        parts = []
        for p in range(pieces):
            own = hit & ((row // CAP) % pieces == p)
            parts.append(jnp.where(own, 1.0, 0.0).astype(BF16))
        rows = pl.ds(pl.multiple_of(g * GROUP, GROUP), GROUP)
        blocks[rows, :] = dot(jnp.concatenate(parts, axis=1), stack[...]).astype(BF16)
        store(g).start()
        return 0

    lax.fori_loop(0, groups, pick, 0)

    @pl.when(me >= 2)
    def _():
        near.wait_recv()

        @pl.when(core == 0)
        def _():
            near_even.start()

        @pl.when(core == 1)
        def _():
            near_odd.start()

    @pl.when(me >= 4)
    def _():
        far.wait_recv()

        @pl.when(core == 1)
        def _():
            far_odd.start()

    @pl.when(core == 1)
    def _():
        beside.wait_recv()

    @pl.when(core == 0)
    def _():
        beside.wait_send()

    @pl.when(me >= 2)
    def _():
        near_even.wait_send()
        near_even.wait_recv()

    @pl.when((me >= 4) & (core == 1))
    def _():
        far_odd.wait_send()

    @pl.when((me >= 4) & (core == 0))
    def _():
        far_odd.wait_recv()

    @pl.when(me + 4 < count)
    def _():
        far.wait_send()

    @pl.when(me + 2 < count)
    def _():
        near.wait_send()

    keep.wait()
    for g in range(groups):
        store(g).wait()


def open_exchange(own, slots, rows, count):
    experts, tokens = slots.shape
    total = experts * BLOCK
    piece = rows.shape[1] * CAP // BLOCK
    vmem = pl.BlockSpec(memory_space=pltpu.VMEM)
    return pl.pallas_call(
        functools.partial(open_kernel, count),
        in_specs=[vmem] * 3,
        out_specs=[vmem, pl.BlockSpec(memory_space=pl.ANY)],
        out_shape=[
            jax.ShapeDtypeStruct(((REACH + 1) * tokens, own.shape[1]), own.dtype),
            jax.ShapeDtypeStruct((total, piece), BF16),
        ],
        scratch_shapes=[
            pltpu.VMEM((BLOCK // CAP * tokens, piece), BF16),
            pltpu.VMEM((total, piece), BF16),
            pltpu.SemaphoreType.DMA((5,)),
            pltpu.SemaphoreType.DMA((5,)),
            pltpu.SemaphoreType.DMA,
            pltpu.SemaphoreType.DMA((total // GROUP,)),
        ],
        compiler_params=pltpu.CompilerParams(
            collective_id=0, has_side_effects=True, vmem_limit_bytes=60 * MB
        ),
        name="open_exchange",
    )(own, slots, rows)


def visible(place_ref, window, tokens):
    kpos = place_ref[0] + iota((window, tokens), 0)
    qpos = place_ref[1] + iota((window, tokens), 1)
    kdoc = jnp.zeros((window, tokens), jnp.int32)
    qdoc = jnp.zeros((window, tokens), jnp.int32)
    for d in range(4):
        end = place_ref[2 + d]
        kdoc = kdoc + (kpos >= end).astype(jnp.int32)
        qdoc = qdoc + (qpos >= end).astype(jnp.int32)
    return (kpos >= 0) & (kpos <= qpos) & (kdoc == qdoc)


def head_pair(ref, h):
    return jnp.concatenate(
        [ref[:, h * HEAD : (h + 1) * HEAD], ref[:, (h + 1) * HEAD : (h + 2) * HEAD]], axis=0
    )


def attend_kernel(heads, per_kv, place_ref, query_ref, keyval_ref, prob_ref, out_ref, bias):
    tokens = query_ref.shape[0]
    window = keyval_ref.shape[0]
    step = pl.program_id(0)
    half = keyval_ref.shape[1] // 2
    scale = HEAD ** (-0.5)

    @pl.when(step == 0)
    def _():
        hidden = jnp.where(visible(place_ref, window, tokens), 0.0, NEGATIVE)
        bias[:, :tokens] = hidden
        bias[:, tokens:] = hidden

    for m in range(half // HEAD):

        @pl.when(step // (per_kv // heads) == m)
        def _():
            keys = keyval_ref[:, m * HEAD : (m + 1) * HEAD]
            values_t = keyval_ref[:, half + m * HEAD : half + (m + 1) * HEAD].T
            for h in range(0, heads, 2):
                raw = contract(keys, head_pair(query_ref, h), 1, 1) * scale + bias[...]
                peak = jnp.max(raw, axis=0, keepdims=True)
                expo = jnp.exp(raw - peak)
                total = jnp.sum(expo, axis=0, keepdims=True)
                prob = (expo * (1.0 / total)).astype(BF16)
                prob_ref[0, :, h * tokens : (h + 2) * tokens] = prob
                mixed = dot(values_t, prob).T.astype(BF16)
                out_ref[:, h * HEAD : (h + 1) * HEAD] = mixed[:tokens]
                out_ref[:, (h + 1) * HEAD : (h + 2) * HEAD] = mixed[tokens:]


def attend(place, query, keyval):
    tokens, width = query.shape
    window = keyval.shape[0]
    kv_heads = keyval.shape[1] // 2 // HEAD
    per_kv = width // HEAD // kv_heads
    heads = 4
    steps = width // HEAD // heads
    return pl.pallas_call(
        functools.partial(attend_kernel, heads, per_kv),
        grid=(steps,),
        in_specs=[
            pl.BlockSpec(memory_space=pltpu.SMEM),
            pl.BlockSpec((tokens, heads * HEAD), lambda i: (0, i)),
            pl.BlockSpec(keyval.shape, lambda i: (0, 0)),
        ],
        out_specs=[
            pl.BlockSpec((1, window, heads * tokens), lambda i: (i, 0, 0)),
            pl.BlockSpec((tokens, heads * HEAD), lambda i: (0, i)),
        ],
        out_shape=[
            jax.ShapeDtypeStruct((steps, window, heads * tokens), BF16),
            jax.ShapeDtypeStruct((tokens, width), BF16),
        ],
        scratch_shapes=[pltpu.VMEM((window, 2 * tokens), F32)],
        compiler_params=params(60),
        cost_estimate=cost(4 * tokens * width * window, 9 * MB, tokens * width * window // HEAD),
        name="attend",
    )(place, query, keyval)


def finish_kernel(
    heads, steps_per_kv, count, ep_count, query_ref, grad_ref, prob_ref, keys_ref, values_ref,
    products_ref, grad_query_ref, grad_keyval_ref, returned_ref,
    key_sum, value_sum, terms, landed, gathered, turned, arrived,
    send_sem, recv_sem, ctx_send, ctx_recv, ep_send, ep_recv,
):
    step = pl.program_id(0)
    last = pl.num_programs(0) - 1
    tokens = query_ref.shape[0]
    half = grad_keyval_ref.shape[1] // 2
    scale = HEAD ** (-0.5)
    me = lax.axis_index("ctx")
    place = lax.axis_index("ep")
    barrier = pltpu.get_barrier_semaphore()

    def send_terms(j, m):
        return pltpu.make_async_remote_copy(
            src_ref=terms.at[m, pl.ds((REACH - j) * tokens, tokens)],
            dst_ref=landed.at[j - 1, m],
            send_sem=send_sem.at[j - 1, m],
            recv_sem=recv_sem.at[j - 1, m],
            device_id={"ctx": me - j},
            device_id_type=MESH,
        )

    def along_ctx(d):
        target = (me + d) % count
        return pltpu.make_async_remote_copy(
            src_ref=products_ref.at[target],
            dst_ref=gathered.at[me],
            send_sem=ctx_send.at[d - 1],
            recv_sem=ctx_recv.at[d - 1],
            device_id={"ctx": target},
            device_id_type=MESH,
        )

    def along_ep(d):
        target = (place + d) % ep_count
        return pltpu.make_async_remote_copy(
            src_ref=turned.at[target],
            dst_ref=arrived.at[place],
            send_sem=ep_send.at[d - 1],
            recv_sem=ep_recv.at[d - 1],
            device_id={"ep": target},
            device_id_type=MESH,
        )

    @pl.when(step == 0)
    def _():
        for d in range(1, count):
            pl.semaphore_signal(
                barrier, inc=1, device_id={"ctx": (me + d) % count}, device_id_type=MESH
            )
        for d in range(1, ep_count):
            pl.semaphore_signal(
                barrier, inc=1, device_id={"ep": (place + d) % ep_count}, device_id_type=MESH
            )
        gathered[me] = products_ref[me]

    @pl.when(step == 1)
    def _():
        pl.semaphore_wait(barrier, count + ep_count - 2)
        for d in range(1, count):
            along_ctx(d).start()

    @pl.when(step == steps_per_kv - 1)
    def _():
        for d in range(1, count):
            along_ctx(d).wait_recv()
        for c in range(count):
            turned[:, c, :] = gathered[c]
        arrived[place] = turned[place]
        for d in range(1, ep_count):
            along_ep(d).start()

    @pl.when(step % steps_per_kv == 0)
    def _():
        key_sum[...] = jnp.zeros_like(key_sum)
        value_sum[...] = jnp.zeros_like(value_sum)

    keys_t = keys_ref[...].T
    values = values_ref[...]
    for h in range(0, heads, 2):
        grad = head_pair(grad_ref, h)
        prob = prob_ref[0, :, h * tokens : (h + 2) * tokens]
        wide = prob.astype(F32)
        moved = wide * contract(values, grad, 1, 1)
        delta = jnp.sum(moved, axis=0, keepdims=True)
        dscore = (moved - wide * delta).astype(BF16)
        grad_query = (dot(keys_t, dscore) * scale).T.astype(BF16)
        grad_query_ref[:, h * HEAD : (h + 1) * HEAD] = grad_query[:tokens]
        grad_query_ref[:, (h + 1) * HEAD : (h + 2) * HEAD] = grad_query[tokens:]
        key_sum[...] += dot(dscore, head_pair(query_ref, h))
        value_sum[...] += dot(prob, grad)

    for m in range(landed.shape[1]):

        @pl.when(step == (m + 1) * steps_per_kv - 1)
        def _():
            terms[m, :, :HEAD] = (key_sum[...] * scale).astype(BF16)
            terms[m, :, HEAD:] = value_sum[...].astype(BF16)
            for j in range(REACH, 0, -1):

                @pl.when(me >= j)
                def _():
                    send_terms(j, m).start()

    @pl.when(step == last)
    def _():
        for d in range(1, count):
            along_ctx(d).wait_send()
        for d in range(1, ep_count):
            along_ep(d).wait_send()
            along_ep(d).wait_recv()
        returned_ref[...] = arrived[...]
        for m in range(landed.shape[1]):
            for j in range(1, REACH + 1):

                @pl.when(me + j < count)
                def _():
                    send_terms(j, m).wait_recv()

                @pl.when(me + j >= count)
                def _():
                    landed[j - 1, m] = jnp.zeros(landed.shape[2:], landed.dtype)

            total = terms[m, REACH * tokens :, :].astype(F32)
            for j in range(REACH):
                total = total + landed[j, m].astype(F32)
            grad_keyval_ref[:, m * HEAD : (m + 1) * HEAD] = total[:, :HEAD].astype(BF16)
            grad_keyval_ref[:, half + m * HEAD : half + (m + 1) * HEAD] = total[:, HEAD:].astype(
                BF16
            )
            for j in range(1, REACH + 1):

                @pl.when(me >= j)
                def _():
                    send_terms(j, m).wait_send()


def finish(query, grad, prob, keyval, products):
    tokens, width = query.shape
    window = keyval.shape[0]
    count, ep_count, lanes = products.shape
    kv_heads = keyval.shape[1] // 2 // HEAD
    heads = prob.shape[2] // tokens
    steps = prob.shape[0]
    steps_per_kv = steps // kv_heads
    rows = pl.BlockSpec((tokens, heads * HEAD), lambda i: (0, i))
    return pl.pallas_call(
        functools.partial(finish_kernel, heads, steps_per_kv, count, ep_count),
        grid=(steps,),
        in_specs=[
            rows,
            rows,
            pl.BlockSpec((1,) + prob.shape[1:], lambda i: (i, 0, 0)),
            pl.BlockSpec((window, HEAD), lambda i: (0, i // steps_per_kv)),
            pl.BlockSpec((window, HEAD), lambda i: (0, kv_heads + i // steps_per_kv)),
            pl.BlockSpec(products.shape, lambda i: (0, 0, 0)),
        ],
        out_specs=[
            rows,
            pl.BlockSpec((tokens, keyval.shape[1]), lambda i: (0, 0)),
            pl.BlockSpec((ep_count, count, lanes), lambda i: (0, 0, 0)),
        ],
        out_shape=[
            jax.ShapeDtypeStruct((tokens, width), BF16),
            jax.ShapeDtypeStruct((tokens, keyval.shape[1]), BF16),
            jax.ShapeDtypeStruct((ep_count, count, lanes), F32),
        ],
        scratch_shapes=[
            pltpu.VMEM((window, HEAD), F32),
            pltpu.VMEM((window, HEAD), F32),
            pltpu.VMEM((kv_heads, window, 2 * HEAD), BF16),
            pltpu.VMEM((REACH, kv_heads, tokens, 2 * HEAD), BF16),
            pltpu.VMEM((count, ep_count, lanes), F32),
            pltpu.VMEM((ep_count, count, lanes), F32),
            pltpu.VMEM((ep_count, count, lanes), F32),
            pltpu.SemaphoreType.DMA((REACH, kv_heads)),
            pltpu.SemaphoreType.DMA((REACH, kv_heads)),
            pltpu.SemaphoreType.DMA((count - 1,)),
            pltpu.SemaphoreType.DMA((count - 1,)),
            pltpu.SemaphoreType.DMA((ep_count - 1,)),
            pltpu.SemaphoreType.DMA((ep_count - 1,)),
        ],
        compiler_params=pltpu.CompilerParams(
            collective_id=1, has_side_effects=True, vmem_limit_bytes=60 * MB
        ),
        cost_estimate=cost(8 * tokens * width * window, 10 * MB),
        name="finish",
    )(query, grad, prob, keyval, keyval, products)


def combine_terms(half, halves, tokens, slots_ref, gates_ref, blocks_ref):
    step = pl.program_id(0)
    count = blocks_ref.shape[0]
    experts = slots_ref.shape[1]
    slots = CAP // halves
    pieces = BLOCK // slots
    spread = (
        iota((experts, count), 0) == step * (count // BLOCK) + iota((experts, count), 1) // BLOCK
    ).astype(F32).astype(BF16)
    slot = dot(slots_ref[...].astype(BF16), spread)
    gate = dot(gates_ref[...].astype(BF16), spread)
    col = iota((tokens, count), 1)
    gate = jnp.where(slot == (half * slots + col % slots).astype(F32), gate, 0.0)
    parts = []
    for p in range(pieces):
        parts.append(jnp.where((col // slots) % pieces == p, gate, 0.0).astype(BF16))
    return dot(jnp.concatenate(parts, axis=0), blocks_ref[...])


def combine_first_kernel(halves, tokens, slots_ref, gates_ref, blocks_ref, acc_ref):
    part = combine_terms(0, halves, tokens, slots_ref, gates_ref, blocks_ref)

    @pl.when(pl.program_id(0) == 0)
    def _():
        acc_ref[...] = part

    @pl.when(pl.program_id(0) != 0)
    def _():
        acc_ref[...] += part


def combine_last_kernel(
    halves, slots_ref, gates_ref, blocks_ref, gain_ref, rinv_ref, first_hbm, grad_out_hbm,
    hidden_hbm, grad_ref, acc, first_ref, grad_out_ref, hidden_ref, sem,
):
    step = pl.program_id(0)
    tokens, width = hidden_ref.shape
    loads = [
        pltpu.make_async_copy(source, target, sem.at[i])
        for i, (source, target) in enumerate(
            [(first_hbm, first_ref), (grad_out_hbm, grad_out_ref), (hidden_hbm, hidden_ref)]
        )
    ]

    @pl.when(step == 0)
    def _():
        for load in loads:
            load.start()

    pieces = acc.shape[0] // tokens
    piece = width // pieces
    part = combine_terms(halves - 1, halves, tokens, slots_ref, gates_ref, blocks_ref)

    @pl.when(step == 0)
    def _():
        acc[...] = part

    @pl.when(step != 0)
    def _():
        acc[...] += part

    @pl.when(step == pl.num_programs(0) - 1)
    def _():
        for load in loads:
            load.wait()
        rinv = rinv_ref[...]
        mean = jnp.zeros((tokens, 1), F32)
        for p in range(pieces):
            cols = slice(p * piece, (p + 1) * piece)
            rows = slice(p * tokens, (p + 1) * tokens)
            scaled = (acc[rows, :] + first_ref[rows, :]) * gain_ref[:, cols]
            acc[rows, :] = scaled
            mean = mean + jnp.sum(hidden_ref[:, cols].astype(F32) * scaled, axis=1, keepdims=True)
        mean = mean / width * (rinv * rinv * rinv)
        for p in range(pieces):
            cols = slice(p * piece, (p + 1) * piece)
            rows = slice(p * tokens, (p + 1) * tokens)
            grad = (
                grad_out_ref[:, cols].astype(F32)
                + rinv * acc[rows, :]
                - hidden_ref[:, cols].astype(F32) * mean
            )
            grad_ref[:, cols] = grad.astype(BF16)


def combine_first(slots, gates, blocks, halves):
    tokens = slots.shape[0]
    total, piece = blocks.shape
    pieces = BLOCK * halves // CAP
    rows = 2 * GROUP
    whole = lambda shape: pl.BlockSpec(shape, lambda i: (0, 0))
    return pl.pallas_call(
        functools.partial(combine_first_kernel, halves, tokens),
        grid=(total // rows,),
        in_specs=[
            whole(slots.shape),
            whole(gates.shape),
            pl.BlockSpec((rows, piece), lambda i: (i, 0)),
        ],
        out_specs=whole((pieces * tokens, piece)),
        out_shape=jax.ShapeDtypeStruct((pieces * tokens, piece), F32),
        compiler_params=params(60),
        cost_estimate=cost(1, 1),
        name="combine_first",
    )(slots, gates, blocks)


def combine_last(slots, gates, blocks, first, gain, grad_out, hidden, rinv, halves):
    tokens, width = hidden.shape
    total, piece = blocks.shape
    rows = 2 * GROUP
    whole = lambda shape: pl.BlockSpec(shape, lambda i: (0, 0))
    return pl.pallas_call(
        functools.partial(combine_last_kernel, halves),
        grid=(total // rows,),
        in_specs=[
            whole(slots.shape),
            whole(gates.shape),
            pl.BlockSpec((rows, piece), lambda i: (i, 0)),
            whole(gain.shape),
            whole(rinv.shape),
        ]
        + [pl.BlockSpec(memory_space=pl.ANY)] * 3,
        out_specs=whole((tokens, width)),
        out_shape=jax.ShapeDtypeStruct((tokens, width), BF16),
        scratch_shapes=[
            pltpu.VMEM(first.shape, F32),
            pltpu.VMEM(first.shape, F32),
            pltpu.VMEM(grad_out.shape, BF16),
            pltpu.VMEM(hidden.shape, BF16),
            pltpu.SemaphoreType.DMA((3,)),
        ],
        compiler_params=params(60),
        cost_estimate=cost(2 * total * tokens * width, 8 * MB),
        name="combine_last",
    )(slots, gates, blocks, gain, rinv, first, grad_out, hidden)


def expert_kernel(
    slots, blocks_hbm, base_hbm, low_ref, high_ref, scale_ref, grad_hidden_ref,
    out_hbm, inputs_hbm, units_ref, low_act_ref, grad_linear_ref, back_ref, products_ref, mag_ref,
    blocks, base, inputs, linear, out_rows, in_sem, base_sem, row_sem, out_sem,
):
    groups = blocks.shape[0] // GROUP
    piece = blocks.shape[1]
    pieces = BLOCK // slots
    span = PER_GROUP * slots
    ffw = base.shape[2]
    depth = base.shape[1]
    tile = 256
    tiles = ffw // tile
    rank = high_ref.shape[1]

    def load_blocks(g):
        rows = pl.ds(pl.multiple_of(g * GROUP, GROUP), GROUP)
        return pltpu.make_async_copy(blocks_hbm.at[rows], blocks.at[rows], in_sem.at[g])

    def load_base(n):
        cols = pl.ds(pl.multiple_of((n % tiles) * tile, tile), tile)
        j = n // tiles
        return pltpu.make_async_copy(
            base_hbm.at[j, :, cols], base.at[j, :, cols], base_sem.at[n]
        )

    def store_rows(g):
        rows = pl.ds(pl.multiple_of(g * GROUP, GROUP), GROUP)
        return pltpu.make_async_copy(out_rows.at[rows], out_hbm.at[rows], out_sem.at[g])

    for g in range(groups):
        load_blocks(g).start()
    for n in range(2 * tiles):
        load_base(n).start()

    permute = to_rows(slots, 1)

    def unpack_group(g, _):
        load_blocks(g).wait()
        rows = dot(permute, blocks[pl.ds(pl.multiple_of(g * GROUP, GROUP), GROUP), :]).astype(BF16)
        place = pl.ds(pl.multiple_of(g * span, span), span)
        for p in range(pieces):
            inputs[place, p * piece : (p + 1) * piece] = rows[p * span : (p + 1) * span, :]
        return 0

    lax.fori_loop(0, groups, unpack_group, 0)
    keep = pltpu.make_async_copy(inputs, inputs_hbm, row_sem)
    keep.start()

    low_act_ref[...] = dot(inputs[...], low_ref[...]).astype(BF16)

    def forward(n, _):
        load_base(n).wait()
        j = n // tiles
        cols = pl.ds(pl.multiple_of((n % tiles) * tile, tile), tile)
        linear[j, :, cols] = dot(inputs[...], base[j, :, cols])
        return 0

    lax.fori_loop(0, 2 * tiles, forward, 0)

    for n in range(tiles):
        cols = slice(n * tile, (n + 1) * tile)
        gate_linear = linear[0, :, cols] + dot(low_act_ref[:, :rank], high_ref[0, :, cols])
        up_linear = linear[1, :, cols] + dot(low_act_ref[:, rank:], high_ref[1, :, cols])
        gate_scale = scale_ref[0:1, cols]
        up_scale = scale_ref[1:2, cols]
        gate = gate_linear * gate_scale
        up = up_linear * up_scale
        sigmoid = 1.0 / (1.0 + jnp.exp(-gate))
        active = gate * sigmoid
        units = (active * up).astype(BF16)
        units_ref[:, cols] = units
        grad_hidden = grad_hidden_ref[:, cols]
        part = jnp.sum(units.astype(F32) * grad_hidden, axis=1, keepdims=True)
        if n == 0:
            products_ref[...] = part
        else:
            products_ref[...] += part
        grad_gate = grad_hidden * up * sigmoid * (1.0 + gate * (1.0 - sigmoid))
        grad_up = grad_hidden * active
        mag_ref[0:1, cols] = jnp.sum(grad_gate * gate_linear, axis=0, keepdims=True)
        mag_ref[1:2, cols] = jnp.sum(grad_up * up_linear, axis=0, keepdims=True)
        grad_linear_ref[0, :, cols] = (grad_gate * gate_scale).astype(BF16)
        grad_linear_ref[1, :, cols] = (grad_up * up_scale).astype(BF16)

    for j in range(2):
        back_ref[:, j * rank : (j + 1) * rank] = contract(
            grad_linear_ref[j], high_ref[j], 1, 1
        ).astype(BF16)

    keep.wait()

    def backward(n, _):
        rows = pl.ds(pl.multiple_of(n * tile, tile), tile)
        grad = contract(grad_linear_ref[0], base[0, rows, :], 1, 1)
        grad = grad + contract(grad_linear_ref[1], base[1, rows, :], 1, 1)
        grad = grad + contract(back_ref[...], low_ref[rows, :], 1, 1)
        inputs[:, rows] = grad.astype(BF16)
        return 0

    lax.fori_loop(0, depth // tile, backward, 0)

    arrange = to_blocks(slots, 1)

    def pack_group(g, _):
        place = pl.ds(pl.multiple_of(g * span, span), span)
        stack = jnp.concatenate(
            [inputs[place, p * piece : (p + 1) * piece] for p in range(pieces)], axis=0
        )
        rows = pl.ds(pl.multiple_of(g * GROUP, GROUP), GROUP)
        out_rows[rows, :] = dot(arrange, stack).astype(BF16)
        store_rows(g).start()
        return 0

    lax.fori_loop(0, groups, pack_group, 0)
    for g in range(groups):
        store_rows(g).wait()


def expert(slots, blocks, base, low, high, scale, grad_hidden):
    total, piece = blocks.shape
    branches, depth, ffw = base.shape
    count = total * slots // BLOCK
    rank2 = low.shape[1]
    groups = total // GROUP
    vmem = pl.BlockSpec(memory_space=pltpu.VMEM)
    hbm = pl.BlockSpec(memory_space=pl.ANY)
    return pl.pallas_call(
        functools.partial(expert_kernel, slots),
        in_specs=[hbm, hbm, vmem, vmem, vmem, vmem],
        out_specs=[hbm, hbm, vmem, vmem, vmem, vmem, vmem, vmem],
        out_shape=[
            jax.ShapeDtypeStruct((total, piece), BF16),
            jax.ShapeDtypeStruct((count, depth), BF16),
            jax.ShapeDtypeStruct((count, ffw), BF16),
            jax.ShapeDtypeStruct((count, rank2), BF16),
            jax.ShapeDtypeStruct((branches, count, ffw), BF16),
            jax.ShapeDtypeStruct((count, rank2), BF16),
            jax.ShapeDtypeStruct((count, 1), F32),
            jax.ShapeDtypeStruct((branches, ffw), F32),
        ],
        scratch_shapes=[
            pltpu.VMEM((total, piece), BF16),
            pltpu.VMEM(base.shape, BF16),
            pltpu.VMEM((count, depth), BF16),
            pltpu.VMEM((branches, count, ffw), F32),
            pltpu.VMEM((total, piece), BF16),
            pltpu.SemaphoreType.DMA((groups,)),
            pltpu.SemaphoreType.DMA((2 * ffw // 256,)),
            pltpu.SemaphoreType.DMA,
            pltpu.SemaphoreType.DMA((groups,)),
        ],
        compiler_params=params(56),
        cost_estimate=cost(4 * count * depth * ffw * branches, 30 * MB),
        name="expert",
    )(blocks, base, low, high, scale, grad_hidden)


def expert_grads_kernel(
    halves, cotangent_ref, scale_ref, base_ref, high_ref, units_ref, low_out_ref, back_low_ref,
    *rest
):
    inputs = rest[:halves]
    low_acts, grad_linears, backs = (
        rest[halves : 2 * halves], rest[2 * halves : 3 * halves], rest[3 * halves : 4 * halves]
    )
    mag_ref, high_grad_ref, low_in_ref, low_grad_ref, high_in_ref, low_down, low_down_t, back_t = (
        rest[4 * halves :]
    )
    count = units_ref.shape[0] // halves
    rank = low_out_ref.shape[1]

    @pl.when(pl.program_id(0) == 0)
    def _():
        low = dot(units_ref[...], low_out_ref[...])
        low_down[...] = low.astype(BF16)
        low_down_t[...] = low.T.astype(BF16)
        low_grad_ref[...] = dot(back_low_ref[...].astype(F32).T.astype(BF16), units_ref[...])
        high_in_ref[...] = jnp.zeros_like(high_in_ref)
        for h in range(halves):
            back_t[h] = backs[h][...].astype(F32).T.astype(BF16)
            low_act_t = low_acts[h][...].astype(F32).T.astype(BF16)
            for j in range(2):
                high_in_ref[j] += dot(low_act_t[j * rank : (j + 1) * rank], grad_linears[h][j])

    mag = jnp.zeros((1, base_ref.shape[1]), F32)
    low_in = jnp.zeros(low_in_ref.shape, F32)
    for h in range(halves):
        rows = slice(h * count, (h + 1) * count)
        linear = dot(units_ref[rows, :], base_ref[...]) + dot(low_down[rows, :], high_ref[...])
        mag = mag + jnp.sum(linear * cotangent_ref[rows, :].astype(F32), axis=0, keepdims=True)
        low_in = low_in + dot(back_t[h], inputs[h][...])
    mag_ref[...] = mag
    low_in_ref[...] = low_in
    grad = (cotangent_ref[...].astype(F32) * scale_ref[...]).astype(BF16)
    high_grad_ref[...] = dot(low_down_t[...], grad)


def expert_grads(
    cotangent, scale, base, high, units, low_out, back_low, inputs, low_acts, grad_linears,
    backs,
):
    halves = len(inputs)
    ffw, width = base.shape
    count, rank = back_low.shape
    tile = 512
    whole = lambda array: pl.BlockSpec(array.shape, lambda i: (0,) * array.ndim)
    part = lambda rows: pl.BlockSpec((rows, tile), lambda i: (0, i))
    fixed = [units, low_out, back_low]
    return pl.pallas_call(
        functools.partial(expert_grads_kernel, halves),
        grid=(width // tile,),
        in_specs=[part(count), part(1), part(ffw), part(rank)]
        + [whole(array) for array in fixed]
        + [part(count // halves)] * halves
        + [whole(array) for array in low_acts + grad_linears + backs],
        out_specs=[
            part(1),
            part(rank),
            part(2 * rank),
            pl.BlockSpec((rank, ffw), lambda i: (0, 0)),
            pl.BlockSpec((2, rank, ffw), lambda i: (0, 0, 0)),
        ],
        out_shape=[
            jax.ShapeDtypeStruct((1, width), F32),
            jax.ShapeDtypeStruct((rank, width), F32),
            jax.ShapeDtypeStruct((2 * rank, width), F32),
            jax.ShapeDtypeStruct((rank, ffw), F32),
            jax.ShapeDtypeStruct((2, rank, ffw), F32),
        ],
        scratch_shapes=[
            pltpu.VMEM((count, rank), BF16),
            pltpu.VMEM((rank, count), BF16),
            pltpu.VMEM((halves, 2 * rank, count // halves), BF16),
        ],
        compiler_params=params(60),
        cost_estimate=cost(1, 1),
        name="expert_grads",
    )(cotangent, scale, base, high, *fixed, *inputs, *low_acts, *grad_linears, *backs)


def square_norm(base, low, high):
    merged = base.astype(F32) + dot(low, high)
    return jnp.sqrt(jnp.sum(merged * merged, axis=0))


def shards(
    query, keyval, doc_lengths, norm_gain, router_logits, expert_ids, grad_out,
    base_in, low_in, high_in, mag_in, base_out, low_out, high_out, mag_out,
):
    query, local_kv, grad_out = query[0], keyval[0], grad_out[0]
    base_in, low_in, high_in, mag_in = base_in[0], low_in[0], high_in[0], mag_in[0]
    base_out, low_out, high_out, mag_out = base_out[0], low_out[0], high_out[0], mag_out[0]
    ids = expert_ids[0]
    tokens, width = query.shape
    top = ids.shape[1]
    experts = lax.axis_size("ctx") * lax.axis_size("ep")
    axes = ("ctx", "ep")
    gain = norm_gain[None, :]
    halves = 2
    slots_each = CAP // halves
    ctx_count = lax.axis_size("ctx")

    def exchange(blocks):
        split = blocks.reshape(experts, BLOCK, blocks.shape[1])
        moved = lax.all_to_all(split, axes, split_axis=0, concat_axis=0, tiled=True)
        return moved.reshape(blocks.shape)

    named = jnp.zeros((experts, tokens), jnp.bool_)
    each = jnp.arange(experts, dtype=jnp.int32)[:, None]
    for k in range(top):
        named = named | (ids[:, k][None, :] == each)
    earlier = jnp.arange(tokens)[:, None] < jnp.arange(tokens)[None, :]
    before = dot(named.astype(BF16), earlier.astype(BF16))
    slots = jnp.where(named, before, -1.0)

    seen, outgoing_grad = open_exchange(local_kv, slots, grad_out, ctx_count)
    first = lax.axis_index("ctx") * tokens
    place = jnp.concatenate(
        [
            jnp.stack([first - REACH * tokens, first]).astype(jnp.int32),
            jnp.cumsum(doc_lengths[0]).astype(jnp.int32),
        ]
    )

    arrived_grad = exchange(outgoing_grad)

    prob, hidden = attend(place, query, seen)
    *outgoing, rinv = dispatch(slots, hidden, gain, True, halves)

    norm_in = jnp.stack([square_norm(base_in[j], low_in[j], high_in[j]) for j in range(2)])
    scale_in = mag_in / norm_in
    norm_out = square_norm(base_out, low_out, high_out)
    scale_out = mag_out / norm_out
    cotangent = unpack(arrived_grad, halves).reshape(experts * CAP, width)
    grad_linear_out = (cotangent.astype(F32) * scale_out).astype(BF16)
    back_low = contract(grad_linear_out, high_out, 1, 1).astype(BF16)
    grad_hidden = contract(grad_linear_out, base_out, 1, 1) + contract(back_low, low_out, 1, 1)
    low_pair = jnp.concatenate([low_in[0], low_in[1]], axis=1)
    arrived = [exchange(outgoing[0])]
    second, grad_hidden, scale_in, low_pair, _ = lax.optimization_barrier(
        (outgoing[1], grad_hidden, scale_in, low_pair, arrived[0])
    )
    arrived.append(exchange(second))

    rows_each = experts * slots_each
    returned, results = [], []
    for h in range(halves):
        outgoing_rows, *result = expert(
            slots_each, arrived[h], base_in, low_pair, high_in, scale_in,
            grad_hidden[h * rows_each : (h + 1) * rows_each],
        )
        returned.append(exchange(outgoing_rows))
        results.append(result)
    results, first_returned = lax.optimization_barrier((results, returned[0]))
    returned[0] = first_returned
    inputs, units, low_acts, grad_linears, backs, products, mag_sums = zip(*results)

    mag_sum, grad_high_out, low_in_t, low_out_t, grad_high_in = expert_grads(
        cotangent, scale_out[None, :], base_out, high_out, jnp.concatenate(units, axis=0), low_out,
        back_low, inputs, low_acts, grad_linears, backs,
    )
    grad_mag_out = mag_sum[0] / norm_out
    grad_low_out = low_out_t.T
    grad_low_in = low_in_t.reshape(2, -1, width).transpose(0, 2, 1)
    grad_mag_in = sum(mag_sums) / norm_in
    products = jnp.concatenate(
        [part.astype(BF16).astype(F32).reshape(experts, slots_each) for part in products], axis=1
    )
    products = jnp.pad(products, ((0, 0), (0, HEAD - CAP))).reshape(ctx_count, -1, HEAD)

    logits = router_logits[0]
    gate_expo = jnp.exp(logits - jnp.max(logits, axis=-1, keepdims=True))
    gates = gate_expo / jnp.sum(gate_expo, axis=-1, keepdims=True)
    dense_gates = jnp.zeros((tokens, experts), F32)
    chosen = [ids[:, k : k + 1] == each.reshape(1, experts) for k in range(top)]
    for k in range(top):
        dense_gates = dense_gates + jnp.where(chosen[k], gates[:, k : k + 1], 0.0)
    token_slots = slots.T
    partial = combine_first(token_slots, dense_gates, returned[0], halves)
    grad_heads = combine_last(
        token_slots, dense_gates, returned[1], partial, gain, grad_out, hidden, rinv, halves
    )
    grad_query, grad_keyval, arrived_products = finish(query, grad_heads, prob, seen, products)
    returned_products = arrived_products.transpose(1, 0, 2).reshape(experts, HEAD)
    dense_products = jnp.zeros((tokens, experts), F32)
    for r in range(CAP):
        dense_products = dense_products + jnp.where(
            token_slots == r, returned_products[:, r][None, :], 0.0
        )
    grad_gate = jnp.stack(
        [jnp.sum(jnp.where(chosen[k], dense_products, 0.0), axis=1) for k in range(top)], axis=1
    )
    grad_logits = gates * (grad_gate - jnp.sum(gates * grad_gate, axis=-1, keepdims=True))

    return (
        grad_query[None],
        grad_keyval[None],
        grad_logits[None],
        grad_low_in[None],
        grad_high_in[None],
        grad_mag_in[None],
        grad_low_out[None],
        grad_high_out[None],
        grad_mag_out[None],
    )


def solution(mesh):
    rows = P("ep", "ctx", None)
    own = lambda extra: P(("ctx", "ep"), *([None] * extra))
    in_specs = (
        rows, rows, P("ep", None), P(), rows, rows, rows,
        own(3), own(3), own(3), own(2), own(2), own(2), own(2), own(1),
    )
    out_specs = (rows, rows, rows, own(3), own(3), own(2), own(2), own(2), own(1))
    return jax.shard_map(shards, mesh=mesh, in_specs=in_specs, out_specs=out_specs, check_vma=False)
```

```python
import functools

import jax
import jax.numpy as jnp
from jax import lax
from jax.experimental import pallas as pl
from jax.experimental.pallas import tpu as pltpu
from jax.sharding import PartitionSpec as P

F32 = jnp.float32
BF16 = jnp.bfloat16
MESH = pl.DeviceIdType.MESH
HEAD = 128
NEGATIVE = -1e30
EPSILON = 1e-06
CAP = 4
BLOCK = 16
GROUP = 256
PER_GROUP = GROUP // BLOCK
REACH = 4
MB = 1 << 20


def params(megabytes):
    return pltpu.CompilerParams(vmem_limit_bytes=megabytes * MB)


def cost(flops, size, transcendentals=0):
    return pl.CostEstimate(flops=flops, bytes_accessed=size, transcendentals=transcendentals)


def iota(shape, dim):
    return lax.broadcasted_iota(jnp.int32, shape, dim)


def dot(left, right):
    return jnp.dot(left, right, preferred_element_type=F32)


def contract(left, right, left_dim, right_dim):
    return lax.dot_general(
        left, right, (((left_dim,), (right_dim,)), ((), ())), preferred_element_type=F32
    )


def is_row(row, col, slots, halves):
    pieces = BLOCK // (slots * halves)
    span = PER_GROUP * slots * halves
    return (
        (row // span == (col // (slots * halves)) % pieces)
        & ((row // (PER_GROUP * slots)) % halves == (col // slots) % halves)
        & ((row // slots) % PER_GROUP == col // BLOCK)
        & (row % slots == col % slots)
    )


def to_rows(slots, halves):
    same = is_row(iota((GROUP, GROUP), 0), iota((GROUP, GROUP), 1), slots, halves)
    return same.astype(F32).astype(BF16)


def to_blocks(slots, halves):
    same = is_row(iota((GROUP, GROUP), 1), iota((GROUP, GROUP), 0), slots, halves)
    return same.astype(F32).astype(BF16)


def dispatch_kernel(with_norm, slots_ref, rows_ref, gain_ref, *rest):
    outs, rinv_ref, stack = rest[:-2], rest[-2], rest[-1]
    tokens, width = rows_ref.shape
    slots = CAP // len(outs)
    pieces = BLOCK // slots
    piece = width // pieces

    @pl.when(pl.program_id(0) == 0)
    def _():
        if with_norm:
            square = jnp.zeros((tokens, 1), F32)
            for p in range(pieces):
                part = rows_ref[:, p * piece : (p + 1) * piece].astype(F32)
                square = square + jnp.sum(part * part, axis=1, keepdims=True)
            rinv = lax.rsqrt(square / width + EPSILON)
        else:
            rinv = jnp.ones((tokens, 1), F32)
        rinv_ref[...] = rinv
        for p in range(pieces):
            cols = slice(p * piece, (p + 1) * piece)
            part = rows_ref[:, cols]
            if with_norm:
                part = (part.astype(F32) * rinv * gain_ref[:, cols]).astype(BF16)
            stack[p * tokens : (p + 1) * tokens, :] = part

    spread = (iota((GROUP, PER_GROUP), 0) // BLOCK == iota((GROUP, PER_GROUP), 1)).astype(F32)
    slot = dot(spread.astype(BF16), slots_ref[...].astype(BF16))
    row = iota((GROUP, tokens), 0)
    for half, out_ref in enumerate(outs):
        hit = slot == (half * slots + row % slots).astype(F32)
        parts = []
        for p in range(pieces):
            own = hit & ((row // slots) % pieces == p)
            parts.append(jnp.where(own, 1.0, 0.0).astype(BF16))
        out_ref[...] = dot(jnp.concatenate(parts, axis=1), stack[...]).astype(BF16)


def dispatch(slots, rows, gain, with_norm, halves):
    experts, tokens = slots.shape
    width = rows.shape[1]
    total = experts * BLOCK
    pieces = BLOCK * halves // CAP
    piece = width // pieces
    whole = lambda shape: pl.BlockSpec(shape, lambda i: (0, 0))
    return pl.pallas_call(
        functools.partial(dispatch_kernel, with_norm),
        grid=(total // GROUP,),
        in_specs=[
            pl.BlockSpec((PER_GROUP, tokens), lambda i: (i, 0)),
            whole((tokens, width)),
            whole((1, width)),
        ],
        out_specs=[pl.BlockSpec((GROUP, piece), lambda i: (i, 0))] * halves + [whole((tokens, 1))],
        out_shape=[jax.ShapeDtypeStruct((total, piece), BF16)] * halves
        + [jax.ShapeDtypeStruct((tokens, 1), F32)],
        scratch_shapes=[pltpu.VMEM((pieces * tokens, piece), BF16)],
        compiler_params=params(60),
        cost_estimate=cost(2 * total * tokens * width * halves, 10 * MB),
        name="dispatch",
    )(slots, rows, gain)


def unpack_kernel(halves, blocks_ref, out_ref):
    piece = blocks_ref.shape[1]
    slots = CAP // halves
    pieces = BLOCK // CAP
    rows = dot(to_rows(slots, halves), blocks_ref[...]).astype(BF16)
    count = PER_GROUP * slots
    for p in range(pieces):
        for half in range(halves):
            first = (p * halves + half) * count
            out_ref[half, :, p * piece : (p + 1) * piece] = rows[first : first + count, :]


def unpack(blocks, halves):
    total, piece = blocks.shape
    pieces = BLOCK // CAP
    count = total // pieces // halves
    return pl.pallas_call(
        functools.partial(unpack_kernel, halves),
        grid=(total // GROUP,),
        in_specs=[pl.BlockSpec((GROUP, piece), lambda i: (i, 0))],
        out_specs=pl.BlockSpec(
            (halves, GROUP // pieces // halves, pieces * piece), lambda i: (0, i, 0)
        ),
        out_shape=jax.ShapeDtypeStruct((halves, count, pieces * piece), BF16),
        compiler_params=params(60),
        cost_estimate=cost(2 * total * GROUP * piece, 8 * MB),
        name="unpack",
    )(blocks)


def open_kernel(
    count, own_ref, slots_ref, rows_ref, seen_ref, out_hbm, stack, blocks, send_sem, recv_sem,
    own_sem, out_sem,
):
    tokens, width = rows_ref.shape
    pieces = BLOCK // CAP
    piece = width // pieces
    groups = blocks.shape[0] // GROUP
    me = lax.axis_index("ctx")
    core = me % 2
    other = me + 1 - 2 * core

    def slot(j):
        return seen_ref.at[pl.ds((REACH - j) * tokens, tokens)]

    def copy(source, j, target, index):
        return pltpu.make_async_remote_copy(
            src_ref=source,
            dst_ref=slot(j),
            send_sem=send_sem.at[index],
            recv_sem=recv_sem.at[index],
            device_id={"ctx": target},
            device_id_type=MESH,
        )

    near = copy(own_ref, 2, me + 2, 0)
    far = copy(own_ref, 4, me + 4, 1)
    beside = copy(own_ref, 1, other, 2)
    near_even = copy(slot(2), 3, other, 3)
    near_odd = copy(slot(2), 1, other, 3)
    far_odd = copy(slot(4), 3, other, 4)

    keep = pltpu.make_async_copy(own_ref, slot(0), own_sem)
    keep.start()
    barrier = pltpu.get_barrier_semaphore()
    peers = 1
    for offset in (2, 4, -2, -4):
        present = (me + offset >= 0) & (me + offset < count)
        peers = peers + present.astype(jnp.int32)

        @pl.when(present)
        def _():
            pl.semaphore_signal(
                barrier, inc=1, device_id={"ctx": me + offset}, device_id_type=MESH
            )

    pl.semaphore_signal(barrier, inc=1, device_id={"ctx": other}, device_id_type=MESH)
    pl.semaphore_wait(barrier, peers)

    @pl.when(me + 4 < count)
    def _():
        far.start()

    @pl.when(me + 2 < count)
    def _():
        near.start()

    @pl.when(core == 0)
    def _():
        beside.start()

    for j in range(1, REACH + 1):

        @pl.when(me < j)
        def _():
            seen_ref[(REACH - j) * tokens : (REACH - j + 1) * tokens, :] = jnp.zeros(
                own_ref.shape, own_ref.dtype
            )

    for p in range(pieces):
        stack[p * tokens : (p + 1) * tokens, :] = rows_ref[:, p * piece : (p + 1) * piece]
    spread = (iota((GROUP, PER_GROUP), 0) // BLOCK == iota((GROUP, PER_GROUP), 1)).astype(F32)
    spread = spread.astype(BF16)
    row = iota((GROUP, tokens), 0)

    def store(g):
        rows = pl.ds(pl.multiple_of(g * GROUP, GROUP), GROUP)
        return pltpu.make_async_copy(blocks.at[rows], out_hbm.at[rows], out_sem.at[g])

    def pick(g, _):
        named = slots_ref[pl.ds(pl.multiple_of(g * PER_GROUP, PER_GROUP), PER_GROUP), :]
        hit = dot(spread, named.astype(BF16)) == (row % CAP).astype(F32)
        parts = []
        for p in range(pieces):
            own = hit & ((row // CAP) % pieces == p)
            parts.append(jnp.where(own, 1.0, 0.0).astype(BF16))
        rows = pl.ds(pl.multiple_of(g * GROUP, GROUP), GROUP)
        blocks[rows, :] = dot(jnp.concatenate(parts, axis=1), stack[...]).astype(BF16)
        store(g).start()
        return 0

    lax.fori_loop(0, groups, pick, 0)

    @pl.when(me >= 2)
    def _():
        near.wait_recv()

        @pl.when(core == 0)
        def _():
            near_even.start()

        @pl.when(core == 1)
        def _():
            near_odd.start()

    @pl.when(me >= 4)
    def _():
        far.wait_recv()

        @pl.when(core == 1)
        def _():
            far_odd.start()

    @pl.when(core == 1)
    def _():
        beside.wait_recv()

    @pl.when(core == 0)
    def _():
        beside.wait_send()

    @pl.when(me >= 2)
    def _():
        near_even.wait_send()
        near_even.wait_recv()

    @pl.when((me >= 4) & (core == 1))
    def _():
        far_odd.wait_send()

    @pl.when((me >= 4) & (core == 0))
    def _():
        far_odd.wait_recv()

    @pl.when(me + 4 < count)
    def _():
        far.wait_send()

    @pl.when(me + 2 < count)
    def _():
        near.wait_send()

    keep.wait()
    for g in range(groups):
        store(g).wait()


def open_exchange(own, slots, rows, count):
    experts, tokens = slots.shape
    total = experts * BLOCK
    piece = rows.shape[1] * CAP // BLOCK
    vmem = pl.BlockSpec(memory_space=pltpu.VMEM)
    return pl.pallas_call(
        functools.partial(open_kernel, count),
        in_specs=[vmem] * 3,
        out_specs=[vmem, pl.BlockSpec(memory_space=pl.ANY)],
        out_shape=[
            jax.ShapeDtypeStruct(((REACH + 1) * tokens, own.shape[1]), own.dtype),
            jax.ShapeDtypeStruct((total, piece), BF16),
        ],
        scratch_shapes=[
            pltpu.VMEM((BLOCK // CAP * tokens, piece), BF16),
            pltpu.VMEM((total, piece), BF16),
            pltpu.SemaphoreType.DMA((5,)),
            pltpu.SemaphoreType.DMA((5,)),
            pltpu.SemaphoreType.DMA,
            pltpu.SemaphoreType.DMA((total // GROUP,)),
        ],
        compiler_params=pltpu.CompilerParams(
            collective_id=0, has_side_effects=True, vmem_limit_bytes=60 * MB
        ),
        name="open_exchange",
    )(own, slots, rows)


def visible(place_ref, window, tokens):
    kpos = place_ref[0] + iota((window, tokens), 0)
    qpos = place_ref[1] + iota((window, tokens), 1)
    kdoc = jnp.zeros((window, tokens), jnp.int32)
    qdoc = jnp.zeros((window, tokens), jnp.int32)
    for d in range(4):
        end = place_ref[2 + d]
        kdoc = kdoc + (kpos >= end).astype(jnp.int32)
        qdoc = qdoc + (qpos >= end).astype(jnp.int32)
    return (kpos >= 0) & (kpos <= qpos) & (kdoc == qdoc)


def stack_heads(ref, heads):
    return jnp.concatenate([ref[:, h * HEAD : (h + 1) * HEAD] for h in range(heads)], axis=0)


def head_pair(ref, h):
    return jnp.concatenate(
        [ref[:, h * HEAD : (h + 1) * HEAD], ref[:, (h + 1) * HEAD : (h + 2) * HEAD]], axis=0
    )


def attend_kernel(heads, per_kv, place_ref, query_ref, keyval_ref, prob_ref, out_ref, bias):
    tokens = query_ref.shape[0]
    window = keyval_ref.shape[0]
    step = pl.program_id(0)
    half = keyval_ref.shape[1] // 2
    scale = HEAD ** (-0.5)

    @pl.when(step == 0)
    def _():
        hidden = jnp.where(visible(place_ref, window, tokens), 0.0, NEGATIVE)
        bias[:, :tokens] = hidden
        bias[:, tokens:] = hidden

    for m in range(half // HEAD):

        @pl.when(step // (per_kv // heads) == m)
        def _():
            keys = keyval_ref[:, m * HEAD : (m + 1) * HEAD]
            values_t = keyval_ref[:, half + m * HEAD : half + (m + 1) * HEAD].T
            for h in range(0, heads, 2):
                raw = contract(keys, head_pair(query_ref, h), 1, 1) * scale + bias[...]
                peak = jnp.max(raw, axis=0, keepdims=True)
                expo = jnp.exp(raw - peak)
                total = jnp.sum(expo, axis=0, keepdims=True)
                prob = (expo * (1.0 / total)).astype(BF16)
                prob_ref[0, :, h * tokens : (h + 2) * tokens] = prob
                mixed = dot(values_t, prob).T.astype(BF16)
                out_ref[:, h * HEAD : (h + 1) * HEAD] = mixed[:tokens]
                out_ref[:, (h + 1) * HEAD : (h + 2) * HEAD] = mixed[tokens:]


def attend(place, query, keyval):
    tokens, width = query.shape
    window = keyval.shape[0]
    kv_heads = keyval.shape[1] // 2 // HEAD
    per_kv = width // HEAD // kv_heads
    heads = 8
    steps = width // HEAD // heads
    return pl.pallas_call(
        functools.partial(attend_kernel, heads, per_kv),
        grid=(steps,),
        in_specs=[
            pl.BlockSpec(memory_space=pltpu.SMEM),
            pl.BlockSpec((tokens, heads * HEAD), lambda i: (0, i)),
            pl.BlockSpec(keyval.shape, lambda i: (0, 0)),
        ],
        out_specs=[
            pl.BlockSpec((1, window, heads * tokens), lambda i: (i, 0, 0)),
            pl.BlockSpec((tokens, heads * HEAD), lambda i: (0, i)),
        ],
        out_shape=[
            jax.ShapeDtypeStruct((steps, window, heads * tokens), BF16),
            jax.ShapeDtypeStruct((tokens, width), BF16),
        ],
        scratch_shapes=[pltpu.VMEM((window, 2 * tokens), F32)],
        compiler_params=params(60),
        cost_estimate=cost(4 * tokens * width * window, 9 * MB, tokens * width * window // HEAD),
        name="attend",
    )(place, query, keyval)


def finish_kernel(
    heads, steps_per_kv, count, ep_count, query_ref, grad_ref, prob_ref, keys_ref, values_ref,
    products_ref, grad_query_ref, grad_keyval_ref, returned_ref,
    key_sum, value_sum, terms, landed, gathered, turned, arrived,
    send_sem, recv_sem, ctx_send, ctx_recv, ep_send, ep_recv,
):
    step = pl.program_id(0)
    last = pl.num_programs(0) - 1
    tokens = query_ref.shape[0]
    half = grad_keyval_ref.shape[1] // 2
    scale = HEAD ** (-0.5)
    me = lax.axis_index("ctx")
    place = lax.axis_index("ep")
    barrier = pltpu.get_barrier_semaphore()

    def send_terms(j, m):
        return pltpu.make_async_remote_copy(
            src_ref=terms.at[m, pl.ds((REACH - j) * tokens, tokens)],
            dst_ref=landed.at[j - 1, m],
            send_sem=send_sem.at[j - 1, m],
            recv_sem=recv_sem.at[j - 1, m],
            device_id={"ctx": me - j},
            device_id_type=MESH,
        )

    def along_ctx(d):
        target = (me + d) % count
        return pltpu.make_async_remote_copy(
            src_ref=products_ref.at[target],
            dst_ref=gathered.at[me],
            send_sem=ctx_send.at[d - 1],
            recv_sem=ctx_recv.at[d - 1],
            device_id={"ctx": target},
            device_id_type=MESH,
        )

    def along_ep(d):
        target = (place + d) % ep_count
        return pltpu.make_async_remote_copy(
            src_ref=turned.at[target],
            dst_ref=arrived.at[place],
            send_sem=ep_send.at[d - 1],
            recv_sem=ep_recv.at[d - 1],
            device_id={"ep": target},
            device_id_type=MESH,
        )

    @pl.when(step == 0)
    def _():
        for d in range(1, count):
            pl.semaphore_signal(
                barrier, inc=1, device_id={"ctx": (me + d) % count}, device_id_type=MESH
            )
        for d in range(1, ep_count):
            pl.semaphore_signal(
                barrier, inc=1, device_id={"ep": (place + d) % ep_count}, device_id_type=MESH
            )
        gathered[me] = products_ref[me]

    @pl.when(step == 1)
    def _():
        pl.semaphore_wait(barrier, count + ep_count - 2)
        for d in range(1, count):
            along_ctx(d).start()

    @pl.when(step == last - 1)
    def _():
        for d in range(1, count):
            along_ctx(d).wait_recv()
        for c in range(count):
            turned[:, c, :] = gathered[c]
        arrived[place] = turned[place]
        for d in range(1, ep_count):
            along_ep(d).start()

    @pl.when(step % steps_per_kv == 0)
    def _():
        key_sum[...] = jnp.zeros_like(key_sum)
        value_sum[...] = jnp.zeros_like(value_sum)

    grad = stack_heads(grad_ref, heads)
    prob = prob_ref[0]
    wide = prob.astype(F32)
    moved = wide * contract(values_ref[...], grad, 1, 1)
    delta = jnp.sum(moved, axis=0, keepdims=True)
    dscore = (moved - wide * delta).astype(BF16)
    grad_query = (dot(keys_ref[...].T, dscore) * scale).T.astype(BF16)
    for h in range(heads):
        grad_query_ref[:, h * HEAD : (h + 1) * HEAD] = grad_query[h * tokens : (h + 1) * tokens]
    key_sum[...] += dot(dscore, stack_heads(query_ref, heads))
    value_sum[...] += dot(prob, grad)

    for m in range(landed.shape[1]):

        @pl.when(step == (m + 1) * steps_per_kv - 1)
        def _():
            terms[m, :, :HEAD] = (key_sum[...] * scale).astype(BF16)
            terms[m, :, HEAD:] = value_sum[...].astype(BF16)
            for j in range(REACH, 0, -1):

                @pl.when(me >= j)
                def _():
                    send_terms(j, m).start()

    @pl.when(step == last)
    def _():
        for d in range(1, count):
            along_ctx(d).wait_send()
        for d in range(1, ep_count):
            along_ep(d).wait_send()
            along_ep(d).wait_recv()
        returned_ref[...] = arrived[...]
        for m in range(landed.shape[1]):
            for j in range(1, REACH + 1):

                @pl.when(me + j < count)
                def _():
                    send_terms(j, m).wait_recv()

                @pl.when(me + j >= count)
                def _():
                    landed[j - 1, m] = jnp.zeros(landed.shape[2:], landed.dtype)

            total = terms[m, REACH * tokens :, :].astype(F32)
            for j in range(REACH):
                total = total + landed[j, m].astype(F32)
            grad_keyval_ref[:, m * HEAD : (m + 1) * HEAD] = total[:, :HEAD].astype(BF16)
            grad_keyval_ref[:, half + m * HEAD : half + (m + 1) * HEAD] = total[:, HEAD:].astype(
                BF16
            )
            for j in range(1, REACH + 1):

                @pl.when(me >= j)
                def _():
                    send_terms(j, m).wait_send()


def finish(query, grad, prob, keyval, products):
    tokens, width = query.shape
    window = keyval.shape[0]
    count, ep_count, lanes = products.shape
    kv_heads = keyval.shape[1] // 2 // HEAD
    heads = prob.shape[2] // tokens
    steps = prob.shape[0]
    steps_per_kv = steps // kv_heads
    rows = pl.BlockSpec((tokens, heads * HEAD), lambda i: (0, i))
    return pl.pallas_call(
        functools.partial(finish_kernel, heads, steps_per_kv, count, ep_count),
        grid=(steps,),
        in_specs=[
            rows,
            rows,
            pl.BlockSpec((1,) + prob.shape[1:], lambda i: (i, 0, 0)),
            pl.BlockSpec((window, HEAD), lambda i: (0, i // steps_per_kv)),
            pl.BlockSpec((window, HEAD), lambda i: (0, kv_heads + i // steps_per_kv)),
            pl.BlockSpec(products.shape, lambda i: (0, 0, 0)),
        ],
        out_specs=[
            rows,
            pl.BlockSpec((tokens, keyval.shape[1]), lambda i: (0, 0)),
            pl.BlockSpec((ep_count, count, lanes), lambda i: (0, 0, 0)),
        ],
        out_shape=[
            jax.ShapeDtypeStruct((tokens, width), BF16),
            jax.ShapeDtypeStruct((tokens, keyval.shape[1]), BF16),
            jax.ShapeDtypeStruct((ep_count, count, lanes), F32),
        ],
        scratch_shapes=[
            pltpu.VMEM((window, HEAD), F32),
            pltpu.VMEM((window, HEAD), F32),
            pltpu.VMEM((kv_heads, window, 2 * HEAD), BF16),
            pltpu.VMEM((REACH, kv_heads, tokens, 2 * HEAD), BF16),
            pltpu.VMEM((count, ep_count, lanes), F32),
            pltpu.VMEM((ep_count, count, lanes), F32),
            pltpu.VMEM((ep_count, count, lanes), F32),
            pltpu.SemaphoreType.DMA((REACH, kv_heads)),
            pltpu.SemaphoreType.DMA((REACH, kv_heads)),
            pltpu.SemaphoreType.DMA((count - 1,)),
            pltpu.SemaphoreType.DMA((count - 1,)),
            pltpu.SemaphoreType.DMA((ep_count - 1,)),
            pltpu.SemaphoreType.DMA((ep_count - 1,)),
        ],
        compiler_params=pltpu.CompilerParams(
            collective_id=1, has_side_effects=True, vmem_limit_bytes=60 * MB
        ),
        cost_estimate=cost(8 * tokens * width * window, 10 * MB),
        name="finish",
    )(query, grad, prob, keyval, keyval, products)


def gather_rows(slots, blocks_ref, rows):
    pieces = BLOCK // slots
    span = PER_GROUP * slots
    moved = dot(to_rows(slots, 1), blocks_ref[...]).astype(BF16)
    place = pl.ds(pl.multiple_of(pl.program_id(0) * span, span), span)
    for p in range(pieces):
        rows[p, place, :] = moved[p * span : (p + 1) * span, :]


def gate_rows(half, slots, slots_ref, gates_ref):
    tokens, experts = slots_ref.shape
    count = experts * slots
    spread = (iota((experts, count), 0) == iota((experts, count), 1) // slots).astype(F32)
    spread = spread.astype(BF16)
    slot = dot(slots_ref[...].astype(BF16), spread)
    gate = dot(gates_ref[...].astype(BF16), spread)
    own = (half * slots + iota((tokens, count), 1) % slots).astype(F32)
    return jnp.where(slot == own, gate, 0.0).astype(BF16)


def combine_first_kernel(halves, slots_ref, gates_ref, blocks_ref, acc_ref, rows):
    slots = CAP // halves
    gather_rows(slots, blocks_ref, rows)

    @pl.when(pl.program_id(0) == pl.num_programs(0) - 1)
    def _():
        gate = gate_rows(0, slots, slots_ref, gates_ref)
        for p in range(rows.shape[0]):
            acc_ref[p] = dot(gate, rows[p])


def combine_last_kernel(
    halves, slots_ref, gates_ref, blocks_ref, gain_ref, rinv_ref, first_hbm, grad_out_hbm,
    hidden_hbm, grad_ref, rows, acc, first_ref, grad_out_ref, hidden_ref, sem,
):
    step = pl.program_id(0)
    tokens, width = hidden_ref.shape
    loads = [
        pltpu.make_async_copy(source, target, sem.at[i])
        for i, (source, target) in enumerate(
            [(first_hbm, first_ref), (grad_out_hbm, grad_out_ref), (hidden_hbm, hidden_ref)]
        )
    ]

    @pl.when(step == 0)
    def _():
        for load in loads:
            load.start()

    slots = CAP // halves
    pieces, _, piece = acc.shape
    gather_rows(slots, blocks_ref, rows)

    @pl.when(step == pl.num_programs(0) - 1)
    def _():
        gate = gate_rows(halves - 1, slots, slots_ref, gates_ref)
        for load in loads:
            load.wait()
        rinv = rinv_ref[...]
        mean = jnp.zeros((tokens, 1), F32)
        for p in range(pieces):
            cols = slice(p * piece, (p + 1) * piece)
            scaled = (dot(gate, rows[p]) + first_ref[p]) * gain_ref[:, cols]
            acc[p] = scaled
            mean = mean + jnp.sum(hidden_ref[:, cols].astype(F32) * scaled, axis=1, keepdims=True)
        mean = mean / width * (rinv * rinv * rinv)
        for p in range(pieces):
            cols = slice(p * piece, (p + 1) * piece)
            grad = (
                grad_out_ref[:, cols].astype(F32)
                + rinv * acc[p]
                - hidden_ref[:, cols].astype(F32) * mean
            )
            grad_ref[:, cols] = grad.astype(BF16)


def combine_first(slots, gates, blocks, halves):
    tokens, experts = slots.shape
    total, piece = blocks.shape
    pieces = BLOCK * halves // CAP
    whole = lambda shape: pl.BlockSpec(shape, lambda i: (0,) * len(shape))
    return pl.pallas_call(
        functools.partial(combine_first_kernel, halves),
        grid=(total // GROUP,),
        in_specs=[
            whole(slots.shape),
            whole(gates.shape),
            pl.BlockSpec((GROUP, piece), lambda i: (i, 0)),
        ],
        out_specs=whole((pieces, tokens, piece)),
        out_shape=jax.ShapeDtypeStruct((pieces, tokens, piece), F32),
        scratch_shapes=[pltpu.VMEM((pieces, experts * CAP // halves, piece), BF16)],
        compiler_params=params(60),
        cost_estimate=cost(1, 1),
        name="combine_first",
    )(slots, gates, blocks)


def combine_last(slots, gates, blocks, first, gain, grad_out, hidden, rinv, halves):
    tokens, width = hidden.shape
    total, piece = blocks.shape
    whole = lambda shape: pl.BlockSpec(shape, lambda i: (0, 0))
    return pl.pallas_call(
        functools.partial(combine_last_kernel, halves),
        grid=(total // GROUP,),
        in_specs=[
            whole(slots.shape),
            whole(gates.shape),
            pl.BlockSpec((GROUP, piece), lambda i: (i, 0)),
            whole(gain.shape),
            whole(rinv.shape),
        ]
        + [pl.BlockSpec(memory_space=pl.ANY)] * 3,
        out_specs=whole((tokens, width)),
        out_shape=jax.ShapeDtypeStruct((tokens, width), BF16),
        scratch_shapes=[
            pltpu.VMEM((first.shape[0], slots.shape[1] * CAP // halves, piece), BF16),
            pltpu.VMEM(first.shape, F32),
            pltpu.VMEM(first.shape, F32),
            pltpu.VMEM(grad_out.shape, BF16),
            pltpu.VMEM(hidden.shape, BF16),
            pltpu.SemaphoreType.DMA((3,)),
        ],
        compiler_params=params(60),
        cost_estimate=cost(2 * total * tokens * width, 8 * MB),
        name="combine_last",
    )(slots, gates, blocks, gain, rinv, first, grad_out, hidden)


def expert_kernel(
    slots, blocks_hbm, base_hbm, low_ref, high_ref, scale_ref, grad_hidden_ref,
    out_hbm, inputs_hbm, units_ref, low_act_ref, grad_linear_ref, back_ref, products_ref, mag_ref,
    blocks, base, inputs, linear, out_rows, in_sem, base_sem, row_sem, out_sem,
):
    groups = blocks.shape[0] // GROUP
    piece = blocks.shape[1]
    pieces = BLOCK // slots
    span = PER_GROUP * slots
    ffw = base.shape[2]
    depth = base.shape[1]
    tile = 256
    tiles = ffw // tile
    rank = high_ref.shape[1]

    def load_blocks(g):
        rows = pl.ds(pl.multiple_of(g * GROUP, GROUP), GROUP)
        return pltpu.make_async_copy(blocks_hbm.at[rows], blocks.at[rows], in_sem.at[g])

    def load_base(n):
        cols = pl.ds(pl.multiple_of((n % tiles) * tile, tile), tile)
        j = n // tiles
        return pltpu.make_async_copy(
            base_hbm.at[j, :, cols], base.at[j, :, cols], base_sem.at[n]
        )

    def store_rows(g):
        rows = pl.ds(pl.multiple_of(g * GROUP, GROUP), GROUP)
        return pltpu.make_async_copy(out_rows.at[rows], out_hbm.at[rows], out_sem.at[g])

    for g in range(groups):
        load_blocks(g).start()
    for n in range(2 * tiles):
        load_base(n).start()

    permute = to_rows(slots, 1)

    def unpack_group(g, _):
        load_blocks(g).wait()
        rows = dot(permute, blocks[pl.ds(pl.multiple_of(g * GROUP, GROUP), GROUP), :]).astype(BF16)
        place = pl.ds(pl.multiple_of(g * span, span), span)
        for p in range(pieces):
            inputs[place, p * piece : (p + 1) * piece] = rows[p * span : (p + 1) * span, :]
        return 0

    lax.fori_loop(0, groups, unpack_group, 0)
    keep = pltpu.make_async_copy(inputs, inputs_hbm, row_sem)
    keep.start()

    low_act_ref[...] = dot(inputs[...], low_ref[...]).astype(BF16)

    def forward(n, _):
        load_base(n).wait()
        j = n // tiles
        cols = pl.ds(pl.multiple_of((n % tiles) * tile, tile), tile)
        linear[j, :, cols] = dot(inputs[...], base[j, :, cols])
        return 0

    lax.fori_loop(0, 2 * tiles, forward, 0)

    for n in range(tiles):
        cols = slice(n * tile, (n + 1) * tile)
        gate_linear = linear[0, :, cols] + dot(low_act_ref[:, :rank], high_ref[0, :, cols])
        up_linear = linear[1, :, cols] + dot(low_act_ref[:, rank:], high_ref[1, :, cols])
        gate_scale = scale_ref[0:1, cols]
        up_scale = scale_ref[1:2, cols]
        gate = gate_linear * gate_scale
        up = up_linear * up_scale
        sigmoid = 1.0 / (1.0 + jnp.exp(-gate))
        active = gate * sigmoid
        units = (active * up).astype(BF16)
        units_ref[:, cols] = units
        grad_hidden = grad_hidden_ref[:, cols]
        part = jnp.sum(units.astype(F32) * grad_hidden, axis=1, keepdims=True)
        if n == 0:
            products_ref[...] = part
        else:
            products_ref[...] += part
        grad_gate = grad_hidden * up * sigmoid * (1.0 + gate * (1.0 - sigmoid))
        grad_up = grad_hidden * active
        mag_ref[0:1, cols] = jnp.sum(grad_gate * gate_linear, axis=0, keepdims=True)
        mag_ref[1:2, cols] = jnp.sum(grad_up * up_linear, axis=0, keepdims=True)
        grad_linear_ref[0, :, cols] = (grad_gate * gate_scale).astype(BF16)
        grad_linear_ref[1, :, cols] = (grad_up * up_scale).astype(BF16)

    for j in range(2):
        back_ref[:, j * rank : (j + 1) * rank] = contract(
            grad_linear_ref[j], high_ref[j], 1, 1
        ).astype(BF16)

    keep.wait()

    def backward(n, _):
        rows = pl.ds(pl.multiple_of(n * tile, tile), tile)
        grad = contract(grad_linear_ref[0], base[0, rows, :], 1, 1)
        grad = grad + contract(grad_linear_ref[1], base[1, rows, :], 1, 1)
        grad = grad + contract(back_ref[...], low_ref[rows, :], 1, 1)
        inputs[:, rows] = grad.astype(BF16)
        return 0

    lax.fori_loop(0, depth // tile, backward, 0)

    arrange = to_blocks(slots, 1)

    def pack_group(g, _):
        place = pl.ds(pl.multiple_of(g * span, span), span)
        stack = jnp.concatenate(
            [inputs[place, p * piece : (p + 1) * piece] for p in range(pieces)], axis=0
        )
        rows = pl.ds(pl.multiple_of(g * GROUP, GROUP), GROUP)
        out_rows[rows, :] = dot(arrange, stack).astype(BF16)
        store_rows(g).start()
        return 0

    lax.fori_loop(0, groups, pack_group, 0)
    for g in range(groups):
        store_rows(g).wait()


def expert(slots, blocks, base, low, high, scale, grad_hidden):
    total, piece = blocks.shape
    branches, depth, ffw = base.shape
    count = total * slots // BLOCK
    rank2 = low.shape[1]
    groups = total // GROUP
    vmem = pl.BlockSpec(memory_space=pltpu.VMEM)
    hbm = pl.BlockSpec(memory_space=pl.ANY)
    return pl.pallas_call(
        functools.partial(expert_kernel, slots),
        in_specs=[hbm, hbm, vmem, vmem, vmem, vmem],
        out_specs=[hbm, hbm, vmem, vmem, vmem, vmem, vmem, vmem],
        out_shape=[
            jax.ShapeDtypeStruct((total, piece), BF16),
            jax.ShapeDtypeStruct((count, depth), BF16),
            jax.ShapeDtypeStruct((count, ffw), BF16),
            jax.ShapeDtypeStruct((count, rank2), BF16),
            jax.ShapeDtypeStruct((branches, count, ffw), BF16),
            jax.ShapeDtypeStruct((count, rank2), BF16),
            jax.ShapeDtypeStruct((count, 1), F32),
            jax.ShapeDtypeStruct((branches, ffw), F32),
        ],
        scratch_shapes=[
            pltpu.VMEM((total, piece), BF16),
            pltpu.VMEM(base.shape, BF16),
            pltpu.VMEM((count, depth), BF16),
            pltpu.VMEM((branches, count, ffw), F32),
            pltpu.VMEM((total, piece), BF16),
            pltpu.SemaphoreType.DMA((groups,)),
            pltpu.SemaphoreType.DMA((2 * ffw // 256,)),
            pltpu.SemaphoreType.DMA,
            pltpu.SemaphoreType.DMA((groups,)),
        ],
        compiler_params=params(56),
        cost_estimate=cost(4 * count * depth * ffw * branches, 30 * MB),
        name="expert",
    )(blocks, base, low, high, scale, grad_hidden)


def expert_grads_kernel(
    halves, cotangent_ref, scale_ref, base_ref, high_ref, units_ref, low_out_ref, back_low_ref,
    *rest
):
    inputs = rest[:halves]
    low_acts, grad_linears, backs = (
        rest[halves : 2 * halves], rest[2 * halves : 3 * halves], rest[3 * halves : 4 * halves]
    )
    mag_ref, high_grad_ref, low_in_ref, low_grad_ref, high_in_ref, low_down, low_down_t, back_t = (
        rest[4 * halves :]
    )
    count = units_ref.shape[0] // halves
    rank = low_out_ref.shape[1]

    @pl.when(pl.program_id(0) == 0)
    def _():
        low = dot(units_ref[...], low_out_ref[...])
        low_down[...] = low.astype(BF16)
        low_down_t[...] = low.T.astype(BF16)
        low_grad_ref[...] = dot(back_low_ref[...].astype(F32).T.astype(BF16), units_ref[...])
        high_in_ref[...] = jnp.zeros_like(high_in_ref)
        for h in range(halves):
            back_t[h] = backs[h][...].astype(F32).T.astype(BF16)
            low_act_t = low_acts[h][...].astype(F32).T.astype(BF16)
            for j in range(2):
                high_in_ref[j] += dot(low_act_t[j * rank : (j + 1) * rank], grad_linears[h][j])

    mag = jnp.zeros((1, base_ref.shape[1]), F32)
    low_in = jnp.zeros(low_in_ref.shape, F32)
    for h in range(halves):
        rows = slice(h * count, (h + 1) * count)
        linear = dot(units_ref[rows, :], base_ref[...]) + dot(low_down[rows, :], high_ref[...])
        mag = mag + jnp.sum(linear * cotangent_ref[rows, :].astype(F32), axis=0, keepdims=True)
        low_in = low_in + dot(back_t[h], inputs[h][...])
    mag_ref[...] = mag
    low_in_ref[...] = low_in
    grad = (cotangent_ref[...].astype(F32) * scale_ref[...]).astype(BF16)
    high_grad_ref[...] = dot(low_down_t[...], grad)


def expert_grads(
    cotangent, scale, base, high, units, low_out, back_low, inputs, low_acts, grad_linears,
    backs,
):
    halves = len(inputs)
    ffw, width = base.shape
    count, rank = back_low.shape
    tile = 512
    whole = lambda array: pl.BlockSpec(array.shape, lambda i: (0,) * array.ndim)
    part = lambda rows: pl.BlockSpec((rows, tile), lambda i: (0, i))
    fixed = [units, low_out, back_low]
    return pl.pallas_call(
        functools.partial(expert_grads_kernel, halves),
        grid=(width // tile,),
        in_specs=[part(count), part(1), part(ffw), part(rank)]
        + [whole(array) for array in fixed]
        + [part(count // halves)] * halves
        + [whole(array) for array in low_acts + grad_linears + backs],
        out_specs=[
            part(1),
            part(rank),
            part(2 * rank),
            pl.BlockSpec((rank, ffw), lambda i: (0, 0)),
            pl.BlockSpec((2, rank, ffw), lambda i: (0, 0, 0)),
        ],
        out_shape=[
            jax.ShapeDtypeStruct((1, width), F32),
            jax.ShapeDtypeStruct((rank, width), F32),
            jax.ShapeDtypeStruct((2 * rank, width), F32),
            jax.ShapeDtypeStruct((rank, ffw), F32),
            jax.ShapeDtypeStruct((2, rank, ffw), F32),
        ],
        scratch_shapes=[
            pltpu.VMEM((count, rank), BF16),
            pltpu.VMEM((rank, count), BF16),
            pltpu.VMEM((halves, 2 * rank, count // halves), BF16),
        ],
        compiler_params=params(60),
        cost_estimate=cost(1, 1),
        name="expert_grads",
    )(cotangent, scale, base, high, *fixed, *inputs, *low_acts, *grad_linears, *backs)


def square_norm(base, low, high):
    merged = base.astype(F32) + dot(low, high)
    return jnp.sqrt(jnp.sum(merged * merged, axis=0))


def shards(
    query, keyval, doc_lengths, norm_gain, router_logits, expert_ids, grad_out,
    base_in, low_in, high_in, mag_in, base_out, low_out, high_out, mag_out,
):
    query, local_kv, grad_out = query[0], keyval[0], grad_out[0]
    base_in, low_in, high_in, mag_in = base_in[0], low_in[0], high_in[0], mag_in[0]
    base_out, low_out, high_out, mag_out = base_out[0], low_out[0], high_out[0], mag_out[0]
    ids = expert_ids[0]
    tokens, width = query.shape
    top = ids.shape[1]
    experts = lax.axis_size("ctx") * lax.axis_size("ep")
    axes = ("ctx", "ep")
    gain = norm_gain[None, :]
    halves = 2
    slots_each = CAP // halves
    ctx_count = lax.axis_size("ctx")

    def exchange(blocks):
        split = blocks.reshape(experts, BLOCK, blocks.shape[1])
        moved = lax.all_to_all(split, axes, split_axis=0, concat_axis=0, tiled=True)
        return moved.reshape(blocks.shape)

    named = jnp.zeros((experts, tokens), jnp.bool_)
    each = jnp.arange(experts, dtype=jnp.int32)[:, None]
    for k in range(top):
        named = named | (ids[:, k][None, :] == each)
    earlier = jnp.arange(tokens)[:, None] < jnp.arange(tokens)[None, :]
    before = dot(named.astype(BF16), earlier.astype(BF16))
    slots = jnp.where(named, before, -1.0)

    seen, outgoing_grad = open_exchange(local_kv, slots, grad_out, ctx_count)
    first = lax.axis_index("ctx") * tokens
    place = jnp.concatenate(
        [
            jnp.stack([first - REACH * tokens, first]).astype(jnp.int32),
            jnp.cumsum(doc_lengths[0]).astype(jnp.int32),
        ]
    )

    arrived_grad = exchange(outgoing_grad)

    prob, hidden = attend(place, query, seen)
    *outgoing, rinv = dispatch(slots, hidden, gain, True, halves)

    norm_in = jnp.stack([square_norm(base_in[j], low_in[j], high_in[j]) for j in range(2)])
    scale_in = mag_in / norm_in
    norm_out = square_norm(base_out, low_out, high_out)
    scale_out = mag_out / norm_out
    cotangent = unpack(arrived_grad, halves).reshape(experts * CAP, width)
    grad_linear_out = (cotangent.astype(F32) * scale_out).astype(BF16)
    back_low = contract(grad_linear_out, high_out, 1, 1).astype(BF16)
    grad_hidden = contract(grad_linear_out, base_out, 1, 1) + contract(back_low, low_out, 1, 1)
    low_pair = jnp.concatenate([low_in[0], low_in[1]], axis=1)
    arrived = [exchange(outgoing[0])]
    second, grad_hidden, scale_in, low_pair, _ = lax.optimization_barrier(
        (outgoing[1], grad_hidden, scale_in, low_pair, arrived[0])
    )
    arrived.append(exchange(second))

    rows_each = experts * slots_each
    returned, results = [], []
    for h in range(halves):
        outgoing_rows, *result = expert(
            slots_each, arrived[h], base_in, low_pair, high_in, scale_in,
            grad_hidden[h * rows_each : (h + 1) * rows_each],
        )
        returned.append(exchange(outgoing_rows))
        results.append(result)
    results, first_returned = lax.optimization_barrier((results, returned[0]))
    returned[0] = first_returned
    inputs, units, low_acts, grad_linears, backs, products, mag_sums = zip(*results)

    mag_sum, grad_high_out, low_in_t, low_out_t, grad_high_in = expert_grads(
        cotangent, scale_out[None, :], base_out, high_out, jnp.concatenate(units, axis=0), low_out,
        back_low, inputs, low_acts, grad_linears, backs,
    )
    grad_mag_out = mag_sum[0] / norm_out
    grad_low_out = low_out_t.T
    grad_low_in = low_in_t.reshape(2, -1, width).transpose(0, 2, 1)
    grad_mag_in = sum(mag_sums) / norm_in
    products = jnp.concatenate(
        [part.astype(BF16).astype(F32).reshape(experts, slots_each) for part in products], axis=1
    )
    products = jnp.pad(products, ((0, 0), (0, HEAD - CAP))).reshape(ctx_count, -1, HEAD)

    logits, hidden = lax.optimization_barrier((router_logits[0], hidden))
    gate_expo = jnp.exp(logits - jnp.max(logits, axis=-1, keepdims=True))
    gates = gate_expo / jnp.sum(gate_expo, axis=-1, keepdims=True)
    dense_gates = jnp.zeros((tokens, experts), F32)
    chosen = [ids[:, k : k + 1] == each.reshape(1, experts) for k in range(top)]
    for k in range(top):
        dense_gates = dense_gates + jnp.where(chosen[k], gates[:, k : k + 1], 0.0)
    token_slots = slots.T
    partial = combine_first(token_slots, dense_gates, returned[0], halves)
    grad_heads = combine_last(
        token_slots, dense_gates, returned[1], partial, gain, grad_out, hidden, rinv, halves
    )
    grad_query, grad_keyval, arrived_products = finish(query, grad_heads, prob, seen, products)
    returned_products = arrived_products.transpose(1, 0, 2).reshape(experts, HEAD)
    dense_products = jnp.zeros((tokens, experts), F32)
    for r in range(CAP):
        dense_products = dense_products + jnp.where(
            token_slots == r, returned_products[:, r][None, :], 0.0
        )
    grad_gate = jnp.stack(
        [jnp.sum(jnp.where(chosen[k], dense_products, 0.0), axis=1) for k in range(top)], axis=1
    )
    grad_logits = gates * (grad_gate - jnp.sum(gates * grad_gate, axis=-1, keepdims=True))

    return (
        grad_query[None],
        grad_keyval[None],
        grad_logits[None],
        grad_low_in[None],
        grad_high_in[None],
        grad_mag_in[None],
        grad_low_out[None],
        grad_high_out[None],
        grad_mag_out[None],
    )


def solution(mesh):
    rows = P("ep", "ctx", None)
    own = lambda extra: P(("ctx", "ep"), *([None] * extra))
    in_specs = (
        rows, rows, P("ep", None), P(), rows, rows, rows,
        own(3), own(3), own(3), own(2), own(2), own(2), own(2), own(1),
    )
    out_specs = (rows, rows, rows, own(3), own(3), own(2), own(2), own(2), own(1))
    return jax.shard_map(shards, mesh=mesh, in_specs=in_specs, out_specs=out_specs, check_vma=False)
```

```python
import functools

import jax
import jax.numpy as jnp
from jax import lax
from jax.experimental import pallas as pl
from jax.experimental.pallas import tpu as pltpu
from jax.sharding import PartitionSpec as P

F32 = jnp.float32
BF16 = jnp.bfloat16
MESH = pl.DeviceIdType.MESH
HEAD = 128
NEGATIVE = -1e30
EPSILON = 1e-06
CAP = 4
BLOCK = 16
GROUP = 256
PER_GROUP = GROUP // BLOCK
REACH = 4
MB = 1 << 20


def params(megabytes):
    return pltpu.CompilerParams(vmem_limit_bytes=megabytes * MB)


def cost(flops, size, transcendentals=0):
    return pl.CostEstimate(flops=flops, bytes_accessed=size, transcendentals=transcendentals)


def iota(shape, dim):
    return lax.broadcasted_iota(jnp.int32, shape, dim)


def dot(left, right):
    return jnp.dot(left, right, preferred_element_type=F32)


def contract(left, right, left_dim, right_dim):
    return lax.dot_general(
        left, right, (((left_dim,), (right_dim,)), ((), ())), preferred_element_type=F32
    )


def is_row(row, col, slots, halves):
    pieces = BLOCK // (slots * halves)
    span = PER_GROUP * slots * halves
    return (
        (row // span == (col // (slots * halves)) % pieces)
        & ((row // (PER_GROUP * slots)) % halves == (col // slots) % halves)
        & ((row // slots) % PER_GROUP == col // BLOCK)
        & (row % slots == col % slots)
    )


def to_rows(slots, halves):
    same = is_row(iota((GROUP, GROUP), 0), iota((GROUP, GROUP), 1), slots, halves)
    return same.astype(F32).astype(BF16)


def to_blocks(slots, halves):
    same = is_row(iota((GROUP, GROUP), 1), iota((GROUP, GROUP), 0), slots, halves)
    return same.astype(F32).astype(BF16)


def dispatch_kernel(with_norm, slots_ref, rows_ref, gain_ref, *rest):
    outs, rinv_ref, stack = rest[:-2], rest[-2], rest[-1]
    tokens, width = rows_ref.shape
    slots = CAP // len(outs)
    pieces = BLOCK // slots
    piece = width // pieces

    @pl.when(pl.program_id(0) == 0)
    def _():
        if with_norm:
            square = jnp.zeros((tokens, 1), F32)
            for p in range(pieces):
                part = rows_ref[:, p * piece : (p + 1) * piece].astype(F32)
                square = square + jnp.sum(part * part, axis=1, keepdims=True)
            rinv = lax.rsqrt(square / width + EPSILON)
        else:
            rinv = jnp.ones((tokens, 1), F32)
        rinv_ref[...] = rinv
        for p in range(pieces):
            cols = slice(p * piece, (p + 1) * piece)
            part = rows_ref[:, cols]
            if with_norm:
                part = (part.astype(F32) * rinv * gain_ref[:, cols]).astype(BF16)
            stack[p * tokens : (p + 1) * tokens, :] = part

    spread = (iota((GROUP, PER_GROUP), 0) // BLOCK == iota((GROUP, PER_GROUP), 1)).astype(F32)
    slot = dot(spread.astype(BF16), slots_ref[...].astype(BF16))
    row = iota((GROUP, tokens), 0)
    for half, out_ref in enumerate(outs):
        hit = slot == (half * slots + row % slots).astype(F32)
        parts = []
        for p in range(pieces):
            own = hit & ((row // slots) % pieces == p)
            parts.append(jnp.where(own, 1.0, 0.0).astype(BF16))
        out_ref[...] = dot(jnp.concatenate(parts, axis=1), stack[...]).astype(BF16)


def dispatch(slots, rows, gain, with_norm, halves):
    experts, tokens = slots.shape
    width = rows.shape[1]
    total = experts * BLOCK
    pieces = BLOCK * halves // CAP
    piece = width // pieces
    whole = lambda shape: pl.BlockSpec(shape, lambda i: (0, 0))
    return pl.pallas_call(
        functools.partial(dispatch_kernel, with_norm),
        grid=(total // GROUP,),
        in_specs=[
            pl.BlockSpec((PER_GROUP, tokens), lambda i: (i, 0)),
            whole((tokens, width)),
            whole((1, width)),
        ],
        out_specs=[pl.BlockSpec((GROUP, piece), lambda i: (i, 0))] * halves + [whole((tokens, 1))],
        out_shape=[jax.ShapeDtypeStruct((total, piece), BF16)] * halves
        + [jax.ShapeDtypeStruct((tokens, 1), F32)],
        scratch_shapes=[pltpu.VMEM((pieces * tokens, piece), BF16)],
        compiler_params=params(60),
        cost_estimate=cost(2 * total * tokens * width * halves, 10 * MB),
        name="dispatch",
    )(slots, rows, gain)


def unpack_kernel(halves, blocks_ref, out_ref):
    piece = blocks_ref.shape[1]
    slots = CAP // halves
    pieces = BLOCK // CAP
    rows = dot(to_rows(slots, halves), blocks_ref[...]).astype(BF16)
    count = PER_GROUP * slots
    for p in range(pieces):
        for half in range(halves):
            first = (p * halves + half) * count
            out_ref[half, :, p * piece : (p + 1) * piece] = rows[first : first + count, :]


def unpack(blocks, halves):
    total, piece = blocks.shape
    pieces = BLOCK // CAP
    count = total // pieces // halves
    return pl.pallas_call(
        functools.partial(unpack_kernel, halves),
        grid=(total // GROUP,),
        in_specs=[pl.BlockSpec((GROUP, piece), lambda i: (i, 0))],
        out_specs=pl.BlockSpec(
            (halves, GROUP // pieces // halves, pieces * piece), lambda i: (0, i, 0)
        ),
        out_shape=jax.ShapeDtypeStruct((halves, count, pieces * piece), BF16),
        compiler_params=params(60),
        cost_estimate=cost(2 * total * GROUP * piece, 8 * MB),
        name="unpack",
    )(blocks)


def open_kernel(
    count, own_ref, slots_ref, rows_ref, seen_ref, out_hbm, stack, blocks, send_sem, recv_sem,
    own_sem, out_sem,
):
    tokens, width = rows_ref.shape
    pieces = BLOCK // CAP
    piece = width // pieces
    groups = blocks.shape[0] // GROUP
    me = lax.axis_index("ctx")
    core = me % 2
    other = me + 1 - 2 * core

    def slot(j):
        return seen_ref.at[pl.ds((REACH - j) * tokens, tokens)]

    def copy(source, j, target, index):
        return pltpu.make_async_remote_copy(
            src_ref=source,
            dst_ref=slot(j),
            send_sem=send_sem.at[index],
            recv_sem=recv_sem.at[index],
            device_id={"ctx": target},
            device_id_type=MESH,
        )

    near = copy(own_ref, 2, me + 2, 0)
    far = copy(own_ref, 4, me + 4, 1)
    beside = copy(own_ref, 1, other, 2)
    near_even = copy(slot(2), 3, other, 3)
    near_odd = copy(slot(2), 1, other, 3)
    far_odd = copy(slot(4), 3, other, 4)

    keep = pltpu.make_async_copy(own_ref, slot(0), own_sem)
    keep.start()
    barrier = pltpu.get_barrier_semaphore()
    peers = 1
    for offset in (2, 4, -2, -4):
        present = (me + offset >= 0) & (me + offset < count)
        peers = peers + present.astype(jnp.int32)

        @pl.when(present)
        def _():
            pl.semaphore_signal(
                barrier, inc=1, device_id={"ctx": me + offset}, device_id_type=MESH
            )

    pl.semaphore_signal(barrier, inc=1, device_id={"ctx": other}, device_id_type=MESH)
    pl.semaphore_wait(barrier, peers)

    @pl.when(me + 4 < count)
    def _():
        far.start()

    @pl.when(me + 2 < count)
    def _():
        near.start()

    @pl.when(core == 0)
    def _():
        beside.start()

    for j in range(1, REACH + 1):

        @pl.when(me < j)
        def _():
            seen_ref[(REACH - j) * tokens : (REACH - j + 1) * tokens, :] = jnp.zeros(
                own_ref.shape, own_ref.dtype
            )

    for p in range(pieces):
        stack[p * tokens : (p + 1) * tokens, :] = rows_ref[:, p * piece : (p + 1) * piece]
    spread = (iota((GROUP, PER_GROUP), 0) // BLOCK == iota((GROUP, PER_GROUP), 1)).astype(F32)
    spread = spread.astype(BF16)
    row = iota((GROUP, tokens), 0)

    def store(g):
        rows = pl.ds(pl.multiple_of(g * GROUP, GROUP), GROUP)
        return pltpu.make_async_copy(blocks.at[rows], out_hbm.at[rows], out_sem.at[g])

    def pick(g, _):
        named = slots_ref[pl.ds(pl.multiple_of(g * PER_GROUP, PER_GROUP), PER_GROUP), :]
        hit = dot(spread, named.astype(BF16)) == (row % CAP).astype(F32)
        parts = []
        for p in range(pieces):
            own = hit & ((row // CAP) % pieces == p)
            parts.append(jnp.where(own, 1.0, 0.0).astype(BF16))
        rows = pl.ds(pl.multiple_of(g * GROUP, GROUP), GROUP)
        blocks[rows, :] = dot(jnp.concatenate(parts, axis=1), stack[...]).astype(BF16)
        store(g).start()
        return 0

    lax.fori_loop(0, groups, pick, 0)

    @pl.when(me >= 2)
    def _():
        near.wait_recv()

        @pl.when(core == 0)
        def _():
            near_even.start()

        @pl.when(core == 1)
        def _():
            near_odd.start()

    @pl.when(me >= 4)
    def _():
        far.wait_recv()

        @pl.when(core == 1)
        def _():
            far_odd.start()

    @pl.when(core == 1)
    def _():
        beside.wait_recv()

    @pl.when(core == 0)
    def _():
        beside.wait_send()

    @pl.when(me >= 2)
    def _():
        near_even.wait_send()
        near_even.wait_recv()

    @pl.when((me >= 4) & (core == 1))
    def _():
        far_odd.wait_send()

    @pl.when((me >= 4) & (core == 0))
    def _():
        far_odd.wait_recv()

    @pl.when(me + 4 < count)
    def _():
        far.wait_send()

    @pl.when(me + 2 < count)
    def _():
        near.wait_send()

    keep.wait()
    for g in range(groups):
        store(g).wait()


def open_exchange(own, slots, rows, count):
    experts, tokens = slots.shape
    total = experts * BLOCK
    piece = rows.shape[1] * CAP // BLOCK
    vmem = pl.BlockSpec(memory_space=pltpu.VMEM)
    return pl.pallas_call(
        functools.partial(open_kernel, count),
        in_specs=[vmem] * 3,
        out_specs=[vmem, pl.BlockSpec(memory_space=pl.ANY)],
        out_shape=[
            jax.ShapeDtypeStruct(((REACH + 1) * tokens, own.shape[1]), own.dtype),
            jax.ShapeDtypeStruct((total, piece), BF16),
        ],
        scratch_shapes=[
            pltpu.VMEM((BLOCK // CAP * tokens, piece), BF16),
            pltpu.VMEM((total, piece), BF16),
            pltpu.SemaphoreType.DMA((5,)),
            pltpu.SemaphoreType.DMA((5,)),
            pltpu.SemaphoreType.DMA,
            pltpu.SemaphoreType.DMA((total // GROUP,)),
        ],
        compiler_params=pltpu.CompilerParams(
            collective_id=0, has_side_effects=True, vmem_limit_bytes=60 * MB
        ),
        name="open_exchange",
    )(own, slots, rows)


def visible(place_ref, window, tokens):
    kpos = place_ref[0] + iota((window, tokens), 0)
    qpos = place_ref[1] + iota((window, tokens), 1)
    kdoc = jnp.zeros((window, tokens), jnp.int32)
    qdoc = jnp.zeros((window, tokens), jnp.int32)
    for d in range(4):
        end = place_ref[2 + d]
        kdoc = kdoc + (kpos >= end).astype(jnp.int32)
        qdoc = qdoc + (qpos >= end).astype(jnp.int32)
    return (kpos >= 0) & (kpos <= qpos) & (kdoc == qdoc)


def stack_heads(ref, heads):
    return jnp.concatenate([ref[:, h * HEAD : (h + 1) * HEAD] for h in range(heads)], axis=0)


def head_pair(ref, h):
    return jnp.concatenate(
        [ref[:, h * HEAD : (h + 1) * HEAD], ref[:, (h + 1) * HEAD : (h + 2) * HEAD]], axis=0
    )


def attend_kernel(heads, per_kv, place_ref, query_ref, keyval_ref, prob_ref, out_ref, bias):
    tokens = query_ref.shape[0]
    window = keyval_ref.shape[0]
    step = pl.program_id(0)
    half = keyval_ref.shape[1] // 2
    scale = HEAD ** (-0.5)

    @pl.when(step == 0)
    def _():
        hidden = jnp.where(visible(place_ref, window, tokens), 0.0, NEGATIVE)
        bias[:, :tokens] = hidden
        bias[:, tokens:] = hidden

    for m in range(half // HEAD):

        @pl.when(step // (per_kv // heads) == m)
        def _():
            keys = keyval_ref[:, m * HEAD : (m + 1) * HEAD]
            values_t = keyval_ref[:, half + m * HEAD : half + (m + 1) * HEAD].T
            for h in range(0, heads, 2):
                raw = contract(keys, head_pair(query_ref, h), 1, 1) * scale + bias[...]
                peak = jnp.max(raw, axis=0, keepdims=True)
                expo = jnp.exp(raw - peak)
                total = jnp.sum(expo, axis=0, keepdims=True)
                prob = (expo * (1.0 / total)).astype(BF16)
                prob_ref[0, :, h * tokens : (h + 2) * tokens] = prob
                mixed = dot(values_t, prob).T.astype(BF16)
                out_ref[:, h * HEAD : (h + 1) * HEAD] = mixed[:tokens]
                out_ref[:, (h + 1) * HEAD : (h + 2) * HEAD] = mixed[tokens:]


def attend(place, query, keyval):
    tokens, width = query.shape
    window = keyval.shape[0]
    kv_heads = keyval.shape[1] // 2 // HEAD
    per_kv = width // HEAD // kv_heads
    heads = 8
    steps = width // HEAD // heads
    return pl.pallas_call(
        functools.partial(attend_kernel, heads, per_kv),
        grid=(steps,),
        in_specs=[
            pl.BlockSpec(memory_space=pltpu.SMEM),
            pl.BlockSpec((tokens, heads * HEAD), lambda i: (0, i)),
            pl.BlockSpec(keyval.shape, lambda i: (0, 0)),
        ],
        out_specs=[
            pl.BlockSpec((1, window, heads * tokens), lambda i: (i, 0, 0)),
            pl.BlockSpec((tokens, heads * HEAD), lambda i: (0, i)),
        ],
        out_shape=[
            jax.ShapeDtypeStruct((steps, window, heads * tokens), BF16),
            jax.ShapeDtypeStruct((tokens, width), BF16),
        ],
        scratch_shapes=[pltpu.VMEM((window, 2 * tokens), F32)],
        compiler_params=params(60),
        cost_estimate=cost(4 * tokens * width * window, 9 * MB, tokens * width * window // HEAD),
        name="attend",
    )(place, query, keyval)


def finish_kernel(
    heads, steps_per_kv, count, ep_count, query_ref, grad_ref, prob_ref, keys_ref, values_ref,
    products_ref, grad_query_ref, grad_keyval_ref, returned_ref,
    key_sum, value_sum, terms, landed, gathered, turned, arrived,
    send_sem, recv_sem, ctx_send, ctx_recv, ep_send, ep_recv,
):
    step = pl.program_id(0)
    last = pl.num_programs(0) - 1
    tokens = query_ref.shape[0]
    half = grad_keyval_ref.shape[1] // 2
    scale = HEAD ** (-0.5)
    me = lax.axis_index("ctx")
    place = lax.axis_index("ep")
    barrier = pltpu.get_barrier_semaphore()

    def send_terms(j, m, part):
        return pltpu.make_async_remote_copy(
            src_ref=terms.at[m, part, pl.ds((REACH - j) * tokens, tokens)],
            dst_ref=landed.at[j - 1, m, part],
            send_sem=send_sem.at[j - 1, m, part],
            recv_sem=recv_sem.at[j - 1, m, part],
            device_id={"ctx": me - j},
            device_id_type=MESH,
        )

    def send_part(part, total):
        for m in range(landed.shape[1]):

            @pl.when(step == (m + 1) * steps_per_kv - 1)
            def _():
                terms[m, part] = total().astype(BF16)
                for j in range(REACH, 0, -1):

                    @pl.when(me >= j)
                    def _():
                        send_terms(j, m, part).start()

    def along_ctx(d):
        target = (me + d) % count
        return pltpu.make_async_remote_copy(
            src_ref=products_ref.at[target],
            dst_ref=gathered.at[me],
            send_sem=ctx_send.at[d - 1],
            recv_sem=ctx_recv.at[d - 1],
            device_id={"ctx": target},
            device_id_type=MESH,
        )

    def along_ep(d):
        target = (place + d) % ep_count
        return pltpu.make_async_remote_copy(
            src_ref=turned.at[target],
            dst_ref=arrived.at[place],
            send_sem=ep_send.at[d - 1],
            recv_sem=ep_recv.at[d - 1],
            device_id={"ep": target},
            device_id_type=MESH,
        )

    @pl.when(step == 0)
    def _():
        for d in range(1, count):
            pl.semaphore_signal(
                barrier, inc=1, device_id={"ctx": (me + d) % count}, device_id_type=MESH
            )
        for d in range(1, ep_count):
            pl.semaphore_signal(
                barrier, inc=1, device_id={"ep": (place + d) % ep_count}, device_id_type=MESH
            )
        gathered[me] = products_ref[me]

    @pl.when(step == 1)
    def _():
        pl.semaphore_wait(barrier, count + ep_count - 2)
        for d in range(1, count):
            along_ctx(d).start()

    @pl.when(step == last - 1)
    def _():
        for d in range(1, count):
            along_ctx(d).wait_recv()
        for c in range(count):
            turned[:, c, :] = gathered[c]
        arrived[place] = turned[place]
        for d in range(1, ep_count):
            along_ep(d).start()

    @pl.when(step % steps_per_kv == 0)
    def _():
        key_sum[...] = jnp.zeros_like(key_sum)
        value_sum[...] = jnp.zeros_like(value_sum)

    grad = stack_heads(grad_ref, heads)
    prob = prob_ref[0]
    value_sum[...] += dot(prob, grad)
    send_part(1, lambda: value_sum[...])
    wide = prob.astype(F32)
    moved = wide * contract(values_ref[...], grad, 1, 1)
    delta = jnp.sum(moved, axis=0, keepdims=True)
    dscore = (moved - wide * delta).astype(BF16)
    key_sum[...] += dot(dscore, stack_heads(query_ref, heads))
    send_part(0, lambda: key_sum[...] * scale)
    grad_query = dot(keys_ref[...].T, dscore).T.astype(BF16)
    for h in range(heads):
        grad_query_ref[:, h * HEAD : (h + 1) * HEAD] = grad_query[h * tokens : (h + 1) * tokens]

    @pl.when(step == last)
    def _():
        for d in range(1, count):
            along_ctx(d).wait_send()
        for d in range(1, ep_count):
            along_ep(d).wait_send()
            along_ep(d).wait_recv()
        returned_ref[...] = arrived[...]
        for m in range(landed.shape[1]):
            for part in (1, 0):
                for j in range(1, REACH + 1):

                    @pl.when(me + j < count)
                    def _():
                        send_terms(j, m, part).wait_recv()

                    @pl.when(me + j >= count)
                    def _():
                        landed[j - 1, m, part] = jnp.zeros(landed.shape[3:], landed.dtype)

                total = terms[m, part, REACH * tokens :, :].astype(F32)
                for j in range(REACH):
                    total = total + landed[j, m, part].astype(F32)
                first = part * half + m * HEAD
                grad_keyval_ref[:, first : first + HEAD] = total.astype(BF16)
                for j in range(1, REACH + 1):

                    @pl.when(me >= j)
                    def _():
                        send_terms(j, m, part).wait_send()


def finish(query, grad, prob, keyval, products):
    tokens, width = query.shape
    window = keyval.shape[0]
    count, ep_count, lanes = products.shape
    kv_heads = keyval.shape[1] // 2 // HEAD
    heads = prob.shape[2] // tokens
    steps = prob.shape[0]
    steps_per_kv = steps // kv_heads
    rows = pl.BlockSpec((tokens, heads * HEAD), lambda i: (0, i))
    return pl.pallas_call(
        functools.partial(finish_kernel, heads, steps_per_kv, count, ep_count),
        grid=(steps,),
        in_specs=[
            rows,
            rows,
            pl.BlockSpec((1,) + prob.shape[1:], lambda i: (i, 0, 0)),
            pl.BlockSpec((window, HEAD), lambda i: (0, i // steps_per_kv)),
            pl.BlockSpec((window, HEAD), lambda i: (0, kv_heads + i // steps_per_kv)),
            pl.BlockSpec(products.shape, lambda i: (0, 0, 0)),
        ],
        out_specs=[
            rows,
            pl.BlockSpec((tokens, keyval.shape[1]), lambda i: (0, 0)),
            pl.BlockSpec((ep_count, count, lanes), lambda i: (0, 0, 0)),
        ],
        out_shape=[
            jax.ShapeDtypeStruct((tokens, width), BF16),
            jax.ShapeDtypeStruct((tokens, keyval.shape[1]), BF16),
            jax.ShapeDtypeStruct((ep_count, count, lanes), F32),
        ],
        scratch_shapes=[
            pltpu.VMEM((window, HEAD), F32),
            pltpu.VMEM((window, HEAD), F32),
            pltpu.VMEM((kv_heads, 2, window, HEAD), BF16),
            pltpu.VMEM((REACH, kv_heads, 2, tokens, HEAD), BF16),
            pltpu.VMEM((count, ep_count, lanes), F32),
            pltpu.VMEM((ep_count, count, lanes), F32),
            pltpu.VMEM((ep_count, count, lanes), F32),
            pltpu.SemaphoreType.DMA((REACH, kv_heads, 2)),
            pltpu.SemaphoreType.DMA((REACH, kv_heads, 2)),
            pltpu.SemaphoreType.DMA((count - 1,)),
            pltpu.SemaphoreType.DMA((count - 1,)),
            pltpu.SemaphoreType.DMA((ep_count - 1,)),
            pltpu.SemaphoreType.DMA((ep_count - 1,)),
        ],
        compiler_params=pltpu.CompilerParams(
            collective_id=1, has_side_effects=True, vmem_limit_bytes=60 * MB
        ),
        cost_estimate=cost(8 * tokens * width * window, 10 * MB),
        name="finish",
    )(query, grad, prob, keyval, keyval, products)


def gather_rows(slots, blocks_ref, rows, order):
    pieces = BLOCK // slots
    span = PER_GROUP * slots
    groups = blocks_ref.shape[0] // GROUP

    @pl.when(pl.program_id(0) == 0)
    def _():
        order[...] = to_rows(slots, 1)

    for g in range(groups):
        moved = dot(order[...], blocks_ref[g * GROUP : (g + 1) * GROUP, :]).astype(BF16)
        place = pl.ds(pl.multiple_of((pl.program_id(0) * groups + g) * span, span), span)
        for p in range(pieces):
            rows[p, place, :] = moved[p * span : (p + 1) * span, :]


def gate_rows(half, slots, slots_ref, gates_ref):
    tokens, experts = slots_ref.shape
    count = experts * slots
    spread = (iota((experts, count), 0) == iota((experts, count), 1) // slots).astype(F32)
    spread = spread.astype(BF16)
    slot = dot(slots_ref[...].astype(BF16), spread)
    gate = dot(gates_ref[...].astype(BF16), spread)
    own = (half * slots + iota((tokens, count), 1) % slots).astype(F32)
    return jnp.where(slot == own, gate, 0.0).astype(BF16)


def combine_first_kernel(halves, slots_ref, gates_ref, blocks_ref, acc_ref, rows, order):
    slots = CAP // halves
    gather_rows(slots, blocks_ref, rows, order)

    @pl.when(pl.program_id(0) == pl.num_programs(0) - 1)
    def _():
        gate = gate_rows(0, slots, slots_ref, gates_ref)
        for p in range(rows.shape[0]):
            acc_ref[p] = dot(gate, rows[p])


def combine_last_kernel(
    halves, slots_ref, gates_ref, blocks_ref, gain_ref, rinv_ref, first_hbm, grad_out_hbm,
    hidden_hbm, grad_ref, rows, order, acc, first_ref, grad_out_ref, hidden_ref, sem,
):
    step = pl.program_id(0)
    tokens, width = hidden_ref.shape
    loads = [
        pltpu.make_async_copy(source, target, sem.at[i])
        for i, (source, target) in enumerate(
            [(first_hbm, first_ref), (grad_out_hbm, grad_out_ref), (hidden_hbm, hidden_ref)]
        )
    ]

    @pl.when(step == 0)
    def _():
        for load in loads:
            load.start()

    slots = CAP // halves
    pieces, _, piece = acc.shape
    gather_rows(slots, blocks_ref, rows, order)

    @pl.when(step == pl.num_programs(0) - 1)
    def _():
        gate = gate_rows(halves - 1, slots, slots_ref, gates_ref)
        for load in loads:
            load.wait()
        rinv = rinv_ref[...]
        mean = jnp.zeros((tokens, 1), F32)
        for p in range(pieces):
            cols = slice(p * piece, (p + 1) * piece)
            scaled = (dot(gate, rows[p]) + first_ref[p]) * gain_ref[:, cols]
            acc[p] = scaled
            mean = mean + jnp.sum(hidden_ref[:, cols].astype(F32) * scaled, axis=1, keepdims=True)
        mean = mean / width * (rinv * rinv * rinv)
        for p in range(pieces):
            cols = slice(p * piece, (p + 1) * piece)
            grad = (
                grad_out_ref[:, cols].astype(F32)
                + rinv * acc[p]
                - hidden_ref[:, cols].astype(F32) * mean
            )
            grad_ref[:, cols] = grad.astype(BF16)


def combine_first(slots, gates, blocks, halves):
    tokens, experts = slots.shape
    total, piece = blocks.shape
    pieces = BLOCK * halves // CAP
    whole = lambda shape: pl.BlockSpec(shape, lambda i: (0,) * len(shape))
    return pl.pallas_call(
        functools.partial(combine_first_kernel, halves),
        grid=(total // (4 * GROUP),),
        in_specs=[
            whole(slots.shape),
            whole(gates.shape),
            pl.BlockSpec((4 * GROUP, piece), lambda i: (i, 0)),
        ],
        out_specs=whole((pieces, tokens, piece)),
        out_shape=jax.ShapeDtypeStruct((pieces, tokens, piece), F32),
        scratch_shapes=[
            pltpu.VMEM((pieces, experts * CAP // halves, piece), BF16),
            pltpu.VMEM((GROUP, GROUP), BF16),
        ],
        compiler_params=params(60),
        cost_estimate=cost(1, 1),
        name="combine_first",
    )(slots, gates, blocks)


def combine_last(slots, gates, blocks, first, gain, grad_out, hidden, rinv, halves):
    tokens, width = hidden.shape
    total, piece = blocks.shape
    whole = lambda shape: pl.BlockSpec(shape, lambda i: (0, 0))
    return pl.pallas_call(
        functools.partial(combine_last_kernel, halves),
        grid=(total // (4 * GROUP),),
        in_specs=[
            whole(slots.shape),
            whole(gates.shape),
            pl.BlockSpec((4 * GROUP, piece), lambda i: (i, 0)),
            whole(gain.shape),
            whole(rinv.shape),
        ]
        + [pl.BlockSpec(memory_space=pl.ANY)] * 3,
        out_specs=whole((tokens, width)),
        out_shape=jax.ShapeDtypeStruct((tokens, width), BF16),
        scratch_shapes=[
            pltpu.VMEM((first.shape[0], slots.shape[1] * CAP // halves, piece), BF16),
            pltpu.VMEM((GROUP, GROUP), BF16),
            pltpu.VMEM(first.shape, F32),
            pltpu.VMEM(first.shape, F32),
            pltpu.VMEM(grad_out.shape, BF16),
            pltpu.VMEM(hidden.shape, BF16),
            pltpu.SemaphoreType.DMA((3,)),
        ],
        compiler_params=params(60),
        cost_estimate=cost(2 * total * tokens * width, 8 * MB),
        name="combine_last",
    )(slots, gates, blocks, gain, rinv, first, grad_out, hidden)


def expert_kernel(
    slots, blocks_hbm, base_hbm, low_ref, high_ref, scale_ref, grad_hidden_ref,
    out_hbm, inputs_hbm, units_ref, low_act_ref, grad_linear_ref, back_ref, products_ref, mag_ref,
    blocks, base, inputs, linear, out_rows, in_sem, base_sem, row_sem, out_sem,
):
    groups = blocks.shape[0] // GROUP
    piece = blocks.shape[1]
    pieces = BLOCK // slots
    span = PER_GROUP * slots
    ffw = base.shape[2]
    depth = base.shape[1]
    tile = 256
    tiles = ffw // tile
    rank = high_ref.shape[1]

    def load_blocks(g):
        rows = pl.ds(pl.multiple_of(g * GROUP, GROUP), GROUP)
        return pltpu.make_async_copy(blocks_hbm.at[rows], blocks.at[rows], in_sem.at[g])

    def load_base(n):
        cols = pl.ds(pl.multiple_of((n % tiles) * tile, tile), tile)
        j = n // tiles
        return pltpu.make_async_copy(
            base_hbm.at[j, :, cols], base.at[j, :, cols], base_sem.at[n]
        )

    def store_rows(g):
        rows = pl.ds(pl.multiple_of(g * GROUP, GROUP), GROUP)
        return pltpu.make_async_copy(out_rows.at[rows], out_hbm.at[rows], out_sem.at[g])

    for g in range(groups):
        load_blocks(g).start()
    for n in range(2 * tiles):
        load_base(n).start()

    permute = to_rows(slots, 1)

    def unpack_group(g, _):
        load_blocks(g).wait()
        rows = dot(permute, blocks[pl.ds(pl.multiple_of(g * GROUP, GROUP), GROUP), :]).astype(BF16)
        place = pl.ds(pl.multiple_of(g * span, span), span)
        for p in range(pieces):
            inputs[place, p * piece : (p + 1) * piece] = rows[p * span : (p + 1) * span, :]
        return 0

    lax.fori_loop(0, groups, unpack_group, 0)
    keep = pltpu.make_async_copy(inputs, inputs_hbm, row_sem)
    keep.start()

    low_act_ref[...] = dot(inputs[...], low_ref[...]).astype(BF16)

    def forward(n, _):
        load_base(n).wait()
        j = n // tiles
        cols = pl.ds(pl.multiple_of((n % tiles) * tile, tile), tile)
        linear[j, :, cols] = dot(inputs[...], base[j, :, cols])
        return 0

    lax.fori_loop(0, 2 * tiles, forward, 0)

    for n in range(tiles):
        cols = slice(n * tile, (n + 1) * tile)
        gate_linear = linear[0, :, cols] + dot(low_act_ref[:, :rank], high_ref[0, :, cols])
        up_linear = linear[1, :, cols] + dot(low_act_ref[:, rank:], high_ref[1, :, cols])
        gate_scale = scale_ref[0:1, cols]
        up_scale = scale_ref[1:2, cols]
        gate = gate_linear * gate_scale
        up = up_linear * up_scale
        sigmoid = 1.0 / (1.0 + jnp.exp(-gate))
        active = gate * sigmoid
        units = (active * up).astype(BF16)
        units_ref[:, cols] = units
        grad_hidden = grad_hidden_ref[:, cols]
        part = jnp.sum(units.astype(F32) * grad_hidden, axis=1, keepdims=True)
        if n == 0:
            products_ref[...] = part
        else:
            products_ref[...] += part
        grad_gate = grad_hidden * up * sigmoid * (1.0 + gate * (1.0 - sigmoid))
        grad_up = grad_hidden * active
        mag_ref[0:1, cols] = jnp.sum(grad_gate * gate_linear, axis=0, keepdims=True)
        mag_ref[1:2, cols] = jnp.sum(grad_up * up_linear, axis=0, keepdims=True)
        grad_linear_ref[0, :, cols] = (grad_gate * gate_scale).astype(BF16)
        grad_linear_ref[1, :, cols] = (grad_up * up_scale).astype(BF16)

    for j in range(2):
        back_ref[:, j * rank : (j + 1) * rank] = contract(
            grad_linear_ref[j], high_ref[j], 1, 1
        ).astype(BF16)

    keep.wait()

    def backward(n, _):
        rows = pl.ds(pl.multiple_of(n * tile, tile), tile)
        grad = contract(grad_linear_ref[0], base[0, rows, :], 1, 1)
        grad = grad + contract(grad_linear_ref[1], base[1, rows, :], 1, 1)
        grad = grad + contract(back_ref[...], low_ref[rows, :], 1, 1)
        inputs[:, rows] = grad.astype(BF16)
        return 0

    lax.fori_loop(0, depth // tile, backward, 0)

    arrange = to_blocks(slots, 1)

    def pack_group(g, _):
        place = pl.ds(pl.multiple_of(g * span, span), span)
        stack = jnp.concatenate(
            [inputs[place, p * piece : (p + 1) * piece] for p in range(pieces)], axis=0
        )
        rows = pl.ds(pl.multiple_of(g * GROUP, GROUP), GROUP)
        out_rows[rows, :] = dot(arrange, stack).astype(BF16)
        store_rows(g).start()
        return 0

    lax.fori_loop(0, groups, pack_group, 0)
    for g in range(groups):
        store_rows(g).wait()


def expert(slots, blocks, base, low, high, scale, grad_hidden):
    total, piece = blocks.shape
    branches, depth, ffw = base.shape
    count = total * slots // BLOCK
    rank2 = low.shape[1]
    groups = total // GROUP
    vmem = pl.BlockSpec(memory_space=pltpu.VMEM)
    hbm = pl.BlockSpec(memory_space=pl.ANY)
    return pl.pallas_call(
        functools.partial(expert_kernel, slots),
        in_specs=[hbm, hbm, vmem, vmem, vmem, vmem],
        out_specs=[hbm, hbm, vmem, vmem, vmem, vmem, vmem, vmem],
        out_shape=[
            jax.ShapeDtypeStruct((total, piece), BF16),
            jax.ShapeDtypeStruct((count, depth), BF16),
            jax.ShapeDtypeStruct((count, ffw), BF16),
            jax.ShapeDtypeStruct((count, rank2), BF16),
            jax.ShapeDtypeStruct((branches, count, ffw), BF16),
            jax.ShapeDtypeStruct((count, rank2), BF16),
            jax.ShapeDtypeStruct((count, 1), F32),
            jax.ShapeDtypeStruct((branches, ffw), F32),
        ],
        scratch_shapes=[
            pltpu.VMEM((total, piece), BF16),
            pltpu.VMEM(base.shape, BF16),
            pltpu.VMEM((count, depth), BF16),
            pltpu.VMEM((branches, count, ffw), F32),
            pltpu.VMEM((total, piece), BF16),
            pltpu.SemaphoreType.DMA((groups,)),
            pltpu.SemaphoreType.DMA((2 * ffw // 256,)),
            pltpu.SemaphoreType.DMA,
            pltpu.SemaphoreType.DMA((groups,)),
        ],
        compiler_params=params(56),
        cost_estimate=cost(4 * count * depth * ffw * branches, 30 * MB),
        name="expert",
    )(blocks, base, low, high, scale, grad_hidden)


def expert_grads_kernel(
    halves, cotangent_ref, scale_ref, base_ref, high_ref, units_ref, low_out_ref, back_low_ref,
    *rest
):
    inputs = rest[:halves]
    low_acts, grad_linears, backs = (
        rest[halves : 2 * halves], rest[2 * halves : 3 * halves], rest[3 * halves : 4 * halves]
    )
    mag_ref, high_grad_ref, low_in_ref, low_grad_ref, high_in_ref, low_down, low_down_t, back_t = (
        rest[4 * halves :]
    )
    count = units_ref.shape[0] // halves
    rank = low_out_ref.shape[1]

    @pl.when(pl.program_id(0) == 0)
    def _():
        low = dot(units_ref[...], low_out_ref[...])
        low_down[...] = low.astype(BF16)
        low_down_t[...] = low.T.astype(BF16)
        low_grad_ref[...] = dot(back_low_ref[...].astype(F32).T.astype(BF16), units_ref[...])
        high_in_ref[...] = jnp.zeros_like(high_in_ref)
        for h in range(halves):
            back_t[h] = backs[h][...].astype(F32).T.astype(BF16)
            low_act_t = low_acts[h][...].astype(F32).T.astype(BF16)
            for j in range(2):
                high_in_ref[j] += dot(low_act_t[j * rank : (j + 1) * rank], grad_linears[h][j])

    mag = jnp.zeros((1, base_ref.shape[1]), F32)
    low_in = jnp.zeros(low_in_ref.shape, F32)
    for h in range(halves):
        rows = slice(h * count, (h + 1) * count)
        linear = dot(units_ref[rows, :], base_ref[...]) + dot(low_down[rows, :], high_ref[...])
        mag = mag + jnp.sum(linear * cotangent_ref[rows, :].astype(F32), axis=0, keepdims=True)
        low_in = low_in + dot(back_t[h], inputs[h][...])
    mag_ref[...] = mag
    low_in_ref[...] = low_in
    grad = (cotangent_ref[...].astype(F32) * scale_ref[...]).astype(BF16)
    high_grad_ref[...] = dot(low_down_t[...], grad)


def expert_grads(
    cotangent, scale, base, high, units, low_out, back_low, inputs, low_acts, grad_linears,
    backs,
):
    halves = len(inputs)
    ffw, width = base.shape
    count, rank = back_low.shape
    tile = 512
    whole = lambda array: pl.BlockSpec(array.shape, lambda i: (0,) * array.ndim)
    part = lambda rows: pl.BlockSpec((rows, tile), lambda i: (0, i))
    fixed = [units, low_out, back_low]
    return pl.pallas_call(
        functools.partial(expert_grads_kernel, halves),
        grid=(width // tile,),
        in_specs=[part(count), part(1), part(ffw), part(rank)]
        + [whole(array) for array in fixed]
        + [part(count // halves)] * halves
        + [whole(array) for array in low_acts + grad_linears + backs],
        out_specs=[
            part(1),
            part(rank),
            part(2 * rank),
            pl.BlockSpec((rank, ffw), lambda i: (0, 0)),
            pl.BlockSpec((2, rank, ffw), lambda i: (0, 0, 0)),
        ],
        out_shape=[
            jax.ShapeDtypeStruct((1, width), F32),
            jax.ShapeDtypeStruct((rank, width), F32),
            jax.ShapeDtypeStruct((2 * rank, width), F32),
            jax.ShapeDtypeStruct((rank, ffw), F32),
            jax.ShapeDtypeStruct((2, rank, ffw), F32),
        ],
        scratch_shapes=[
            pltpu.VMEM((count, rank), BF16),
            pltpu.VMEM((rank, count), BF16),
            pltpu.VMEM((halves, 2 * rank, count // halves), BF16),
        ],
        compiler_params=params(60),
        cost_estimate=cost(1, 1),
        name="expert_grads",
    )(cotangent, scale, base, high, *fixed, *inputs, *low_acts, *grad_linears, *backs)


def square_norm(base, low, high):
    merged = base.astype(F32) + dot(low, high)
    return jnp.sqrt(jnp.sum(merged * merged, axis=0))


def shards(
    query, keyval, doc_lengths, norm_gain, router_logits, expert_ids, grad_out,
    base_in, low_in, high_in, mag_in, base_out, low_out, high_out, mag_out,
):
    query, local_kv, grad_out = query[0], keyval[0], grad_out[0]
    base_in, low_in, high_in, mag_in = base_in[0], low_in[0], high_in[0], mag_in[0]
    base_out, low_out, high_out, mag_out = base_out[0], low_out[0], high_out[0], mag_out[0]
    ids = expert_ids[0]
    tokens, width = query.shape
    top = ids.shape[1]
    experts = lax.axis_size("ctx") * lax.axis_size("ep")
    axes = ("ctx", "ep")
    gain = norm_gain[None, :]
    halves = 2
    slots_each = CAP // halves
    ctx_count = lax.axis_size("ctx")

    def exchange(blocks):
        split = blocks.reshape(experts, BLOCK, blocks.shape[1])
        moved = lax.all_to_all(split, axes, split_axis=0, concat_axis=0, tiled=True)
        return moved.reshape(blocks.shape)

    named = jnp.zeros((experts, tokens), jnp.bool_)
    each = jnp.arange(experts, dtype=jnp.int32)[:, None]
    for k in range(top):
        named = named | (ids[:, k][None, :] == each)
    earlier = jnp.arange(tokens)[:, None] < jnp.arange(tokens)[None, :]
    before = dot(named.astype(BF16), earlier.astype(BF16))
    slots = jnp.where(named, before, -1.0)

    seen, outgoing_grad = open_exchange(local_kv, slots, grad_out, ctx_count)
    first = lax.axis_index("ctx") * tokens
    place = jnp.concatenate(
        [
            jnp.stack([first - REACH * tokens, first]).astype(jnp.int32),
            jnp.cumsum(doc_lengths[0]).astype(jnp.int32),
        ]
    )

    arrived_grad = exchange(outgoing_grad)

    prob, hidden = attend(place, query, seen)
    *outgoing, rinv = dispatch(slots, hidden, gain, True, halves)

    logits, hidden = lax.optimization_barrier((router_logits[0], hidden))
    gate_expo = jnp.exp(logits - jnp.max(logits, axis=-1, keepdims=True))
    gates = gate_expo / jnp.sum(gate_expo, axis=-1, keepdims=True)
    dense_gates = jnp.zeros((tokens, experts), F32)
    chosen = [ids[:, k : k + 1] == each.reshape(1, experts) for k in range(top)]
    for k in range(top):
        dense_gates = dense_gates + jnp.where(chosen[k], gates[:, k : k + 1], 0.0)
    token_slots = slots.T

    norm_in = jnp.stack([square_norm(base_in[j], low_in[j], high_in[j]) for j in range(2)])
    scale_in = mag_in / norm_in
    norm_out = square_norm(base_out, low_out, high_out)
    scale_out = mag_out / norm_out
    cotangent = unpack(arrived_grad, halves).reshape(experts * CAP, width)
    grad_linear_out = (cotangent.astype(F32) * scale_out).astype(BF16)
    back_low = contract(grad_linear_out, high_out, 1, 1).astype(BF16)
    grad_hidden = contract(grad_linear_out, base_out, 1, 1) + contract(back_low, low_out, 1, 1)
    low_pair = jnp.concatenate([low_in[0], low_in[1]], axis=1)
    arrived = [exchange(outgoing[0])]
    second, grad_hidden, scale_in, low_pair, dense_gates, token_slots, _ = lax.optimization_barrier(
        (outgoing[1], grad_hidden, scale_in, low_pair, dense_gates, token_slots, arrived[0])
    )
    arrived.append(exchange(second))

    rows_each = experts * slots_each
    returned, results = [], []
    for h in range(halves):
        outgoing_rows, *result = expert(
            slots_each, arrived[h], base_in, low_pair, high_in, scale_in,
            grad_hidden[h * rows_each : (h + 1) * rows_each],
        )
        returned.append(exchange(outgoing_rows))
        results.append(result)
    results, first_returned = lax.optimization_barrier((results, returned[0]))
    returned[0] = first_returned
    inputs, units, low_acts, grad_linears, backs, products, mag_sums = zip(*results)

    mag_sum, grad_high_out, low_in_t, low_out_t, grad_high_in = expert_grads(
        cotangent, scale_out[None, :], base_out, high_out, jnp.concatenate(units, axis=0), low_out,
        back_low, inputs, low_acts, grad_linears, backs,
    )
    grad_mag_out = mag_sum[0] / norm_out
    grad_low_out = low_out_t.T
    grad_low_in = low_in_t.reshape(2, -1, width).transpose(0, 2, 1)
    grad_mag_in = sum(mag_sums) / norm_in
    products = jnp.concatenate(
        [part.astype(BF16).astype(F32).reshape(experts, slots_each) for part in products], axis=1
    )
    products = jnp.pad(products, ((0, 0), (0, HEAD - CAP))).reshape(ctx_count, -1, HEAD)

    partial = combine_first(token_slots, dense_gates, returned[0], halves)
    grad_heads = combine_last(
        token_slots, dense_gates, returned[1], partial, gain, grad_out, hidden, rinv, halves
    )
    grad_query, grad_keyval, arrived_products = finish(query, grad_heads, prob, seen, products)
    grad_query = (grad_query.astype(F32) * HEAD ** (-0.5)).astype(BF16)
    returned_products = arrived_products.transpose(1, 0, 2).reshape(experts, HEAD)
    dense_products = jnp.zeros((tokens, experts), F32)
    for r in range(CAP):
        dense_products = dense_products + jnp.where(
            token_slots == r, returned_products[:, r][None, :], 0.0
        )
    grad_gate = jnp.stack(
        [jnp.sum(jnp.where(chosen[k], dense_products, 0.0), axis=1) for k in range(top)], axis=1
    )
    grad_logits = gates * (grad_gate - jnp.sum(gates * grad_gate, axis=-1, keepdims=True))

    return (
        grad_query[None],
        grad_keyval[None],
        grad_logits[None],
        grad_low_in[None],
        grad_high_in[None],
        grad_mag_in[None],
        grad_low_out[None],
        grad_high_out[None],
        grad_mag_out[None],
    )


def solution(mesh):
    rows = P("ep", "ctx", None)
    own = lambda extra: P(("ctx", "ep"), *([None] * extra))
    in_specs = (
        rows, rows, P("ep", None), P(), rows, rows, rows,
        own(3), own(3), own(3), own(2), own(2), own(2), own(2), own(1),
    )
    out_specs = (rows, rows, rows, own(3), own(3), own(2), own(2), own(2), own(1))
    return jax.shard_map(shards, mesh=mesh, in_specs=in_specs, out_specs=out_specs, check_vma=False)
```

```python
import functools

import jax
import jax.numpy as jnp
from jax import lax
from jax.experimental import pallas as pl
from jax.experimental.pallas import tpu as pltpu
from jax.sharding import PartitionSpec as P

F32 = jnp.float32
BF16 = jnp.bfloat16
MESH = pl.DeviceIdType.MESH
HEAD = 128
NEGATIVE = -1e30
EPSILON = 1e-06
CAP = 4
BLOCK = 16
GROUP = 256
PER_GROUP = GROUP // BLOCK
REACH = 4
MB = 1 << 20


def params(megabytes):
    return pltpu.CompilerParams(vmem_limit_bytes=megabytes * MB)


def cost(flops, size, transcendentals=0):
    return pl.CostEstimate(flops=flops, bytes_accessed=size, transcendentals=transcendentals)


def iota(shape, dim):
    return lax.broadcasted_iota(jnp.int32, shape, dim)


def dot(left, right):
    return jnp.dot(left, right, preferred_element_type=F32)


def contract(left, right, left_dim, right_dim):
    return lax.dot_general(
        left, right, (((left_dim,), (right_dim,)), ((), ())), preferred_element_type=F32
    )


def is_row(row, col, slots, halves):
    pieces = BLOCK // (slots * halves)
    span = PER_GROUP * slots * halves
    return (
        (row // span == (col // (slots * halves)) % pieces)
        & ((row // (PER_GROUP * slots)) % halves == (col // slots) % halves)
        & ((row // slots) % PER_GROUP == col // BLOCK)
        & (row % slots == col % slots)
    )


def to_rows(slots, halves):
    same = is_row(iota((GROUP, GROUP), 0), iota((GROUP, GROUP), 1), slots, halves)
    return same.astype(F32).astype(BF16)


def to_blocks(slots, halves):
    same = is_row(iota((GROUP, GROUP), 1), iota((GROUP, GROUP), 0), slots, halves)
    return same.astype(F32).astype(BF16)


def dispatch_kernel(with_norm, slots_ref, rows_ref, gain_ref, *rest):
    outs, rinv_ref, stack = rest[:-2], rest[-2], rest[-1]
    tokens, width = rows_ref.shape
    slots = CAP // len(outs)
    pieces = BLOCK // slots
    piece = width // pieces

    @pl.when(pl.program_id(0) == 0)
    def _():
        if with_norm:
            square = jnp.zeros((tokens, 1), F32)
            for p in range(pieces):
                part = rows_ref[:, p * piece : (p + 1) * piece].astype(F32)
                square = square + jnp.sum(part * part, axis=1, keepdims=True)
            rinv = lax.rsqrt(square / width + EPSILON)
        else:
            rinv = jnp.ones((tokens, 1), F32)
        rinv_ref[...] = rinv
        for p in range(pieces):
            cols = slice(p * piece, (p + 1) * piece)
            part = rows_ref[:, cols]
            if with_norm:
                part = (part.astype(F32) * rinv * gain_ref[:, cols]).astype(BF16)
            stack[p * tokens : (p + 1) * tokens, :] = part

    spread = (iota((GROUP, PER_GROUP), 0) // BLOCK == iota((GROUP, PER_GROUP), 1)).astype(F32)
    slot = dot(spread.astype(BF16), slots_ref[...].astype(BF16))
    row = iota((GROUP, tokens), 0)
    for half, out_ref in enumerate(outs):
        hit = slot == (half * slots + row % slots).astype(F32)
        parts = []
        for p in range(pieces):
            own = hit & ((row // slots) % pieces == p)
            parts.append(jnp.where(own, 1.0, 0.0).astype(BF16))
        out_ref[...] = dot(jnp.concatenate(parts, axis=1), stack[...]).astype(BF16)


def dispatch(slots, rows, gain, with_norm, halves):
    experts, tokens = slots.shape
    width = rows.shape[1]
    total = experts * BLOCK
    pieces = BLOCK * halves // CAP
    piece = width // pieces
    whole = lambda shape: pl.BlockSpec(shape, lambda i: (0, 0))
    return pl.pallas_call(
        functools.partial(dispatch_kernel, with_norm),
        grid=(total // GROUP,),
        in_specs=[
            pl.BlockSpec((PER_GROUP, tokens), lambda i: (i, 0)),
            whole((tokens, width)),
            whole((1, width)),
        ],
        out_specs=[pl.BlockSpec((GROUP, piece), lambda i: (i, 0))] * halves + [whole((tokens, 1))],
        out_shape=[jax.ShapeDtypeStruct((total, piece), BF16)] * halves
        + [jax.ShapeDtypeStruct((tokens, 1), F32)],
        scratch_shapes=[pltpu.VMEM((pieces * tokens, piece), BF16)],
        compiler_params=params(60),
        cost_estimate=cost(2 * total * tokens * width * halves, 10 * MB),
        name="dispatch",
    )(slots, rows, gain)


def unpack_kernel(halves, blocks_ref, out_ref):
    piece = blocks_ref.shape[1]
    slots = CAP // halves
    pieces = BLOCK // CAP
    rows = dot(to_rows(slots, halves), blocks_ref[...]).astype(BF16)
    count = PER_GROUP * slots
    for p in range(pieces):
        for half in range(halves):
            first = (p * halves + half) * count
            out_ref[half, :, p * piece : (p + 1) * piece] = rows[first : first + count, :]


def unpack(blocks, halves):
    total, piece = blocks.shape
    pieces = BLOCK // CAP
    count = total // pieces // halves
    return pl.pallas_call(
        functools.partial(unpack_kernel, halves),
        grid=(total // GROUP,),
        in_specs=[pl.BlockSpec((GROUP, piece), lambda i: (i, 0))],
        out_specs=pl.BlockSpec(
            (halves, GROUP // pieces // halves, pieces * piece), lambda i: (0, i, 0)
        ),
        out_shape=jax.ShapeDtypeStruct((halves, count, pieces * piece), BF16),
        compiler_params=params(60),
        cost_estimate=cost(2 * total * GROUP * piece, 8 * MB),
        name="unpack",
    )(blocks)


def open_kernel(
    count, own_ref, slots_ref, rows_ref, seen_ref, out_hbm, stack, blocks, wanted, masks,
    send_sem, recv_sem, own_sem, out_sem,
):
    tokens, width = rows_ref.shape
    pieces = BLOCK // CAP
    piece = width // pieces
    groups = blocks.shape[0] // GROUP
    me = lax.axis_index("ctx")
    core = me % 2
    other = me + 1 - 2 * core

    def slot(j):
        return seen_ref.at[pl.ds((REACH - j) * tokens, tokens)]

    def copy(source, j, target, index):
        return pltpu.make_async_remote_copy(
            src_ref=source,
            dst_ref=slot(j),
            send_sem=send_sem.at[index],
            recv_sem=recv_sem.at[index],
            device_id={"ctx": target},
            device_id_type=MESH,
        )

    near = copy(own_ref, 2, me + 2, 0)
    far = copy(own_ref, 4, me + 4, 1)
    beside = copy(own_ref, 1, other, 2)
    near_even = copy(slot(2), 3, other, 3)
    near_odd = copy(slot(2), 1, other, 3)
    far_odd = copy(slot(4), 3, other, 4)

    keep = pltpu.make_async_copy(own_ref, slot(0), own_sem)
    keep.start()
    barrier = pltpu.get_barrier_semaphore()
    peers = 1
    for offset in (2, 4, -2, -4):
        present = (me + offset >= 0) & (me + offset < count)
        peers = peers + present.astype(jnp.int32)

        @pl.when(present)
        def _():
            pl.semaphore_signal(
                barrier, inc=1, device_id={"ctx": me + offset}, device_id_type=MESH
            )

    pl.semaphore_signal(barrier, inc=1, device_id={"ctx": other}, device_id_type=MESH)
    pl.semaphore_wait(barrier, peers)

    @pl.when(me + 4 < count)
    def _():
        far.start()

    @pl.when(me + 2 < count)
    def _():
        near.start()

    @pl.when(core == 0)
    def _():
        beside.start()

    for j in range(1, REACH + 1):

        @pl.when(me < j)
        def _():
            seen_ref[(REACH - j) * tokens : (REACH - j + 1) * tokens, :] = jnp.zeros(
                own_ref.shape, own_ref.dtype
            )

    for p in range(pieces):
        stack[p * tokens : (p + 1) * tokens, :] = rows_ref[:, p * piece : (p + 1) * piece]
    spread = (iota((GROUP, PER_GROUP), 0) // BLOCK == iota((GROUP, PER_GROUP), 1)).astype(F32)
    spread = spread.astype(BF16)
    row = iota((GROUP, tokens), 0)
    wanted[...] = (row % CAP).astype(F32)
    for p in range(pieces):
        own = (row // CAP) % pieces == p
        masks[:, p * tokens : (p + 1) * tokens] = own.astype(F32).astype(BF16)

    def store(g):
        rows = pl.ds(pl.multiple_of(g * GROUP, GROUP), GROUP)
        return pltpu.make_async_copy(blocks.at[rows], out_hbm.at[rows], out_sem.at[g])

    def pick(g, _):
        named = slots_ref[pl.ds(pl.multiple_of(g * PER_GROUP, PER_GROUP), PER_GROUP), :]
        hit = jnp.where(dot(spread, named.astype(BF16)) == wanted[...], 1.0, 0.0).astype(BF16)
        picker = jnp.concatenate([hit] * pieces, axis=1) * masks[...]
        rows = pl.ds(pl.multiple_of(g * GROUP, GROUP), GROUP)
        blocks[rows, :] = dot(picker, stack[...]).astype(BF16)
        store(g).start()
        return 0

    lax.fori_loop(0, groups // 2, pick, 0)

    @pl.when(me >= 2)
    def _():
        near.wait_recv()

        @pl.when(core == 0)
        def _():
            near_even.start()

        @pl.when(core == 1)
        def _():
            near_odd.start()

    lax.fori_loop(groups // 2, groups, pick, 0)

    @pl.when(me >= 4)
    def _():
        far.wait_recv()

        @pl.when(core == 1)
        def _():
            far_odd.start()

    @pl.when(core == 1)
    def _():
        beside.wait_recv()

    @pl.when(core == 0)
    def _():
        beside.wait_send()

    @pl.when(me >= 2)
    def _():
        near_even.wait_send()
        near_even.wait_recv()

    @pl.when((me >= 4) & (core == 1))
    def _():
        far_odd.wait_send()

    @pl.when((me >= 4) & (core == 0))
    def _():
        far_odd.wait_recv()

    @pl.when(me + 4 < count)
    def _():
        far.wait_send()

    @pl.when(me + 2 < count)
    def _():
        near.wait_send()

    keep.wait()
    for g in range(groups):
        store(g).wait()


def open_exchange(own, slots, rows, count):
    experts, tokens = slots.shape
    total = experts * BLOCK
    piece = rows.shape[1] * CAP // BLOCK
    vmem = pl.BlockSpec(memory_space=pltpu.VMEM)
    return pl.pallas_call(
        functools.partial(open_kernel, count),
        in_specs=[vmem] * 3,
        out_specs=[vmem, pl.BlockSpec(memory_space=pl.ANY)],
        out_shape=[
            jax.ShapeDtypeStruct(((REACH + 1) * tokens, own.shape[1]), own.dtype),
            jax.ShapeDtypeStruct((total, piece), BF16),
        ],
        scratch_shapes=[
            pltpu.VMEM((BLOCK // CAP * tokens, piece), BF16),
            pltpu.VMEM((total, piece), BF16),
            pltpu.VMEM((GROUP, tokens), F32),
            pltpu.VMEM((GROUP, BLOCK // CAP * tokens), BF16),
            pltpu.SemaphoreType.DMA((5,)),
            pltpu.SemaphoreType.DMA((5,)),
            pltpu.SemaphoreType.DMA,
            pltpu.SemaphoreType.DMA((total // GROUP,)),
        ],
        compiler_params=pltpu.CompilerParams(
            collective_id=0, has_side_effects=True, vmem_limit_bytes=60 * MB
        ),
        name="open_exchange",
    )(own, slots, rows)


def visible(place_ref, window, tokens):
    kpos = place_ref[0] + iota((window, tokens), 0)
    qpos = place_ref[1] + iota((window, tokens), 1)
    kdoc = jnp.zeros((window, tokens), jnp.int32)
    qdoc = jnp.zeros((window, tokens), jnp.int32)
    for d in range(4):
        end = place_ref[2 + d]
        kdoc = kdoc + (kpos >= end).astype(jnp.int32)
        qdoc = qdoc + (qpos >= end).astype(jnp.int32)
    return (kpos >= 0) & (kpos <= qpos) & (kdoc == qdoc)


def stack_heads(ref, heads):
    return jnp.concatenate([ref[:, h * HEAD : (h + 1) * HEAD] for h in range(heads)], axis=0)


def head_pair(ref, h):
    return jnp.concatenate(
        [ref[:, h * HEAD : (h + 1) * HEAD], ref[:, (h + 1) * HEAD : (h + 2) * HEAD]], axis=0
    )


def attend_kernel(heads, per_kv, place_ref, query_ref, keyval_ref, prob_ref, out_ref, bias):
    tokens = query_ref.shape[0]
    window = keyval_ref.shape[0]
    step = pl.program_id(0)
    half = keyval_ref.shape[1] // 2
    scale = HEAD ** (-0.5)

    @pl.when(step == 0)
    def _():
        hidden = jnp.where(visible(place_ref, window, tokens), 0.0, NEGATIVE)
        bias[:, :tokens] = hidden
        bias[:, tokens:] = hidden

    for m in range(half // HEAD):

        @pl.when(step // (per_kv // heads) == m)
        def _():
            keys = keyval_ref[:, m * HEAD : (m + 1) * HEAD]
            values_t = keyval_ref[:, half + m * HEAD : half + (m + 1) * HEAD].T
            for h in range(0, heads, 2):
                raw = contract(keys, head_pair(query_ref, h), 1, 1) * scale + bias[...]
                peak = jnp.max(raw, axis=0, keepdims=True)
                expo = jnp.exp(raw - peak)
                total = jnp.sum(expo, axis=0, keepdims=True)
                prob = (expo * (1.0 / total)).astype(BF16)
                prob_ref[0, :, h * tokens : (h + 2) * tokens] = prob
                mixed = dot(values_t, prob).T.astype(BF16)
                out_ref[:, h * HEAD : (h + 1) * HEAD] = mixed[:tokens]
                out_ref[:, (h + 1) * HEAD : (h + 2) * HEAD] = mixed[tokens:]


def attend(place, query, keyval):
    tokens, width = query.shape
    window = keyval.shape[0]
    kv_heads = keyval.shape[1] // 2 // HEAD
    per_kv = width // HEAD // kv_heads
    heads = 8
    steps = width // HEAD // heads
    return pl.pallas_call(
        functools.partial(attend_kernel, heads, per_kv),
        grid=(steps,),
        in_specs=[
            pl.BlockSpec(memory_space=pltpu.SMEM),
            pl.BlockSpec((tokens, heads * HEAD), lambda i: (0, i)),
            pl.BlockSpec(keyval.shape, lambda i: (0, 0)),
        ],
        out_specs=[
            pl.BlockSpec((1, window, heads * tokens), lambda i: (i, 0, 0)),
            pl.BlockSpec((tokens, heads * HEAD), lambda i: (0, i)),
        ],
        out_shape=[
            jax.ShapeDtypeStruct((steps, window, heads * tokens), BF16),
            jax.ShapeDtypeStruct((tokens, width), BF16),
        ],
        scratch_shapes=[pltpu.VMEM((window, 2 * tokens), F32)],
        compiler_params=params(60),
        cost_estimate=cost(4 * tokens * width * window, 9 * MB, tokens * width * window // HEAD),
        name="attend",
    )(place, query, keyval)


def finish_kernel(
    heads, steps_per_kv, count, ep_count, query_ref, grad_ref, prob_ref, keys_ref, values_ref,
    products_ref, grad_query_ref, grad_keyval_ref, returned_ref,
    key_sum, value_sum, terms, landed, gathered, turned, arrived,
    send_sem, recv_sem, ctx_send, ctx_recv, ep_send, ep_recv,
):
    step = pl.program_id(0)
    last = pl.num_programs(0) - 1
    tokens = query_ref.shape[0]
    half = grad_keyval_ref.shape[1] // 2
    scale = HEAD ** (-0.5)
    me = lax.axis_index("ctx")
    place = lax.axis_index("ep")
    barrier = pltpu.get_barrier_semaphore()

    def send_terms(j, m, part):
        return pltpu.make_async_remote_copy(
            src_ref=terms.at[m, part, pl.ds((REACH - j) * tokens, tokens)],
            dst_ref=landed.at[j - 1, m, part],
            send_sem=send_sem.at[j - 1, m, part],
            recv_sem=recv_sem.at[j - 1, m, part],
            device_id={"ctx": me - j},
            device_id_type=MESH,
        )

    def send_part(part, total):
        for m in range(landed.shape[1]):

            @pl.when(step == (m + 1) * steps_per_kv - 1)
            def _():
                terms[m, part] = total().astype(BF16)
                for j in range(REACH, 0, -1):

                    @pl.when(me >= j)
                    def _():
                        send_terms(j, m, part).start()

    def along_ctx(d):
        target = (me + d) % count
        return pltpu.make_async_remote_copy(
            src_ref=products_ref.at[target],
            dst_ref=gathered.at[me],
            send_sem=ctx_send.at[d - 1],
            recv_sem=ctx_recv.at[d - 1],
            device_id={"ctx": target},
            device_id_type=MESH,
        )

    def along_ep(d):
        target = (place + d) % ep_count
        return pltpu.make_async_remote_copy(
            src_ref=turned.at[target],
            dst_ref=arrived.at[place],
            send_sem=ep_send.at[d - 1],
            recv_sem=ep_recv.at[d - 1],
            device_id={"ep": target},
            device_id_type=MESH,
        )

    @pl.when(step == 0)
    def _():
        for d in range(1, count):
            pl.semaphore_signal(
                barrier, inc=1, device_id={"ctx": (me + d) % count}, device_id_type=MESH
            )
        for d in range(1, ep_count):
            pl.semaphore_signal(
                barrier, inc=1, device_id={"ep": (place + d) % ep_count}, device_id_type=MESH
            )
        gathered[me] = products_ref[me]

    @pl.when(step == 1)
    def _():
        pl.semaphore_wait(barrier, count + ep_count - 2)
        for d in range(1, count):
            along_ctx(d).start()

    @pl.when(step == last - 1)
    def _():
        for d in range(1, count):
            along_ctx(d).wait_recv()
        for c in range(count):
            turned[:, c, :] = gathered[c]
        arrived[place] = turned[place]
        for d in range(1, ep_count):
            along_ep(d).start()

    @pl.when(step % steps_per_kv == 0)
    def _():
        key_sum[...] = jnp.zeros_like(key_sum)
        value_sum[...] = jnp.zeros_like(value_sum)

    grad = stack_heads(grad_ref, heads)
    prob = prob_ref[0]
    value_sum[...] += dot(prob, grad)
    send_part(1, lambda: value_sum[...])
    wide = prob.astype(F32)
    moved = wide * contract(values_ref[...], grad, 1, 1)
    delta = jnp.sum(moved, axis=0, keepdims=True)
    dscore = (moved - wide * delta).astype(BF16)
    key_sum[...] += dot(dscore, stack_heads(query_ref, heads))
    send_part(0, lambda: key_sum[...] * scale)
    grad_query = dot(keys_ref[...].T, dscore).T.astype(BF16)
    for h in range(heads):
        grad_query_ref[:, h * HEAD : (h + 1) * HEAD] = grad_query[h * tokens : (h + 1) * tokens]

    @pl.when(step == last)
    def _():
        for d in range(1, count):
            along_ctx(d).wait_send()
        for d in range(1, ep_count):
            along_ep(d).wait_send()
            along_ep(d).wait_recv()
        by_expert = jnp.concatenate([arrived[:, c, :] for c in range(count)], axis=0)
        returned_ref[...] = by_expert.T[: returned_ref.shape[0], :]
        for m in range(landed.shape[1]):
            for part in (1, 0):
                for j in range(1, REACH + 1):

                    @pl.when(me + j < count)
                    def _():
                        send_terms(j, m, part).wait_recv()

                    @pl.when(me + j >= count)
                    def _():
                        landed[j - 1, m, part] = jnp.zeros(landed.shape[3:], landed.dtype)

                total = terms[m, part, REACH * tokens :, :].astype(F32)
                for j in range(REACH):
                    total = total + landed[j, m, part].astype(F32)
                first = part * half + m * HEAD
                grad_keyval_ref[:, first : first + HEAD] = total.astype(BF16)
                for j in range(1, REACH + 1):

                    @pl.when(me >= j)
                    def _():
                        send_terms(j, m, part).wait_send()


def finish(query, grad, prob, keyval, products):
    tokens, width = query.shape
    window = keyval.shape[0]
    count, ep_count, lanes = products.shape
    kv_heads = keyval.shape[1] // 2 // HEAD
    heads = prob.shape[2] // tokens
    steps = prob.shape[0]
    steps_per_kv = steps // kv_heads
    rows = pl.BlockSpec((tokens, heads * HEAD), lambda i: (0, i))
    return pl.pallas_call(
        functools.partial(finish_kernel, heads, steps_per_kv, count, ep_count),
        grid=(steps,),
        in_specs=[
            rows,
            rows,
            pl.BlockSpec((1,) + prob.shape[1:], lambda i: (i, 0, 0)),
            pl.BlockSpec((window, HEAD), lambda i: (0, i // steps_per_kv)),
            pl.BlockSpec((window, HEAD), lambda i: (0, kv_heads + i // steps_per_kv)),
            pl.BlockSpec(products.shape, lambda i: (0, 0, 0)),
        ],
        out_specs=[
            rows,
            pl.BlockSpec((tokens, keyval.shape[1]), lambda i: (0, 0)),
            pl.BlockSpec((8, count * ep_count), lambda i: (0, 0)),
        ],
        out_shape=[
            jax.ShapeDtypeStruct((tokens, width), BF16),
            jax.ShapeDtypeStruct((tokens, keyval.shape[1]), BF16),
            jax.ShapeDtypeStruct((8, count * ep_count), F32),
        ],
        scratch_shapes=[
            pltpu.VMEM((window, HEAD), F32),
            pltpu.VMEM((window, HEAD), F32),
            pltpu.VMEM((kv_heads, 2, window, HEAD), BF16),
            pltpu.VMEM((REACH, kv_heads, 2, tokens, HEAD), BF16),
            pltpu.VMEM((count, ep_count, lanes), F32),
            pltpu.VMEM((ep_count, count, lanes), F32),
            pltpu.VMEM((ep_count, count, lanes), F32),
            pltpu.SemaphoreType.DMA((REACH, kv_heads, 2)),
            pltpu.SemaphoreType.DMA((REACH, kv_heads, 2)),
            pltpu.SemaphoreType.DMA((count - 1,)),
            pltpu.SemaphoreType.DMA((count - 1,)),
            pltpu.SemaphoreType.DMA((ep_count - 1,)),
            pltpu.SemaphoreType.DMA((ep_count - 1,)),
        ],
        compiler_params=pltpu.CompilerParams(
            collective_id=1, has_side_effects=True, vmem_limit_bytes=50 * MB
        ),
        cost_estimate=cost(8 * tokens * width * window, 10 * MB),
        name="finish",
    )(query, grad, prob, keyval, keyval, products)


def gather_rows(slots, blocks_ref, rows, order):
    pieces = BLOCK // slots
    span = PER_GROUP * slots
    groups = blocks_ref.shape[0] // GROUP

    @pl.when(pl.program_id(0) == 0)
    def _():
        order[...] = to_rows(slots, 1)

    for g in range(groups):
        moved = dot(order[...], blocks_ref[g * GROUP : (g + 1) * GROUP, :]).astype(BF16)
        place = pl.ds(pl.multiple_of((pl.program_id(0) * groups + g) * span, span), span)
        for p in range(pieces):
            rows[p, place, :] = moved[p * span : (p + 1) * span, :]


def gate_rows(half, slots, slots_ref, gates_ref):
    tokens, experts = slots_ref.shape
    count = experts * slots
    spread = (iota((experts, count), 0) == iota((experts, count), 1) // slots).astype(F32)
    spread = spread.astype(BF16)
    slot = dot(slots_ref[...].astype(BF16), spread)
    gate = dot(gates_ref[...].astype(BF16), spread)
    own = (half * slots + iota((tokens, count), 1) % slots).astype(F32)
    return jnp.where(slot == own, gate, 0.0).astype(BF16)


def combine_first_kernel(halves, slots_ref, gates_ref, blocks_ref, acc_ref, rows, order):
    slots = CAP // halves
    gather_rows(slots, blocks_ref, rows, order)

    @pl.when(pl.program_id(0) == pl.num_programs(0) - 1)
    def _():
        gate = gate_rows(0, slots, slots_ref, gates_ref)
        for p in range(rows.shape[0]):
            acc_ref[p] = dot(gate, rows[p])


def combine_last_kernel(
    halves, slots_ref, gates_ref, blocks_ref, gain_ref, rinv_ref, first_hbm, grad_out_hbm,
    hidden_hbm, grad_ref, rows, order, acc, first_ref, grad_out_ref, hidden_ref, sem,
):
    step = pl.program_id(0)
    tokens, width = hidden_ref.shape
    loads = [
        pltpu.make_async_copy(source, target, sem.at[i])
        for i, (source, target) in enumerate(
            [(first_hbm, first_ref), (grad_out_hbm, grad_out_ref), (hidden_hbm, hidden_ref)]
        )
    ]

    @pl.when(step == 0)
    def _():
        for load in loads:
            load.start()

    slots = CAP // halves
    pieces, _, piece = acc.shape
    gather_rows(slots, blocks_ref, rows, order)

    @pl.when(step == pl.num_programs(0) - 1)
    def _():
        gate = gate_rows(halves - 1, slots, slots_ref, gates_ref)
        for load in loads:
            load.wait()
        rinv = rinv_ref[...]
        mean = jnp.zeros((tokens, 1), F32)
        for p in range(pieces):
            cols = slice(p * piece, (p + 1) * piece)
            scaled = (dot(gate, rows[p]) + first_ref[p]) * gain_ref[:, cols]
            acc[p] = scaled
            mean = mean + jnp.sum(hidden_ref[:, cols].astype(F32) * scaled, axis=1, keepdims=True)
        mean = mean / width * (rinv * rinv * rinv)
        for p in range(pieces):
            cols = slice(p * piece, (p + 1) * piece)
            grad = (
                grad_out_ref[:, cols].astype(F32)
                + rinv * acc[p]
                - hidden_ref[:, cols].astype(F32) * mean
            )
            grad_ref[:, cols] = grad.astype(BF16)


def combine_first(slots, gates, blocks, halves):
    tokens, experts = slots.shape
    total, piece = blocks.shape
    pieces = BLOCK * halves // CAP
    whole = lambda shape: pl.BlockSpec(shape, lambda i: (0,) * len(shape))
    return pl.pallas_call(
        functools.partial(combine_first_kernel, halves),
        grid=(total // (4 * GROUP),),
        in_specs=[
            whole(slots.shape),
            whole(gates.shape),
            pl.BlockSpec((4 * GROUP, piece), lambda i: (i, 0)),
        ],
        out_specs=whole((pieces, tokens, piece)),
        out_shape=jax.ShapeDtypeStruct((pieces, tokens, piece), F32),
        scratch_shapes=[
            pltpu.VMEM((pieces, experts * CAP // halves, piece), BF16),
            pltpu.VMEM((GROUP, GROUP), BF16),
        ],
        compiler_params=params(60),
        cost_estimate=cost(1, 1),
        name="combine_first",
    )(slots, gates, blocks)


def combine_last(slots, gates, blocks, first, gain, grad_out, hidden, rinv, halves):
    tokens, width = hidden.shape
    total, piece = blocks.shape
    whole = lambda shape: pl.BlockSpec(shape, lambda i: (0, 0))
    return pl.pallas_call(
        functools.partial(combine_last_kernel, halves),
        grid=(total // (4 * GROUP),),
        in_specs=[
            whole(slots.shape),
            whole(gates.shape),
            pl.BlockSpec((4 * GROUP, piece), lambda i: (i, 0)),
            whole(gain.shape),
            whole(rinv.shape),
        ]
        + [pl.BlockSpec(memory_space=pl.ANY)] * 3,
        out_specs=whole((tokens, width)),
        out_shape=jax.ShapeDtypeStruct((tokens, width), BF16),
        scratch_shapes=[
            pltpu.VMEM((first.shape[0], slots.shape[1] * CAP // halves, piece), BF16),
            pltpu.VMEM((GROUP, GROUP), BF16),
            pltpu.VMEM(first.shape, F32),
            pltpu.VMEM(first.shape, F32),
            pltpu.VMEM(grad_out.shape, BF16),
            pltpu.VMEM(hidden.shape, BF16),
            pltpu.SemaphoreType.DMA((3,)),
        ],
        compiler_params=params(50),
        cost_estimate=cost(2 * total * tokens * width, 8 * MB),
        name="combine_last",
    )(slots, gates, blocks, gain, rinv, first, grad_out, hidden)


def expert_kernel(
    slots, blocks_hbm, base_hbm, low_ref, high_ref, scale_ref, grad_hidden_ref,
    out_hbm, inputs_hbm, units_ref, low_act_ref, grad_linear_ref, back_ref, products_ref, mag_ref,
    blocks, base, inputs, linear, out_rows, in_sem, base_sem, row_sem, out_sem,
):
    groups = blocks.shape[0] // GROUP
    piece = blocks.shape[1]
    pieces = BLOCK // slots
    span = PER_GROUP * slots
    ffw = base.shape[2]
    depth = base.shape[1]
    tile = 256
    tiles = ffw // tile
    rank = high_ref.shape[1]

    def load_blocks(g):
        rows = pl.ds(pl.multiple_of(g * GROUP, GROUP), GROUP)
        return pltpu.make_async_copy(blocks_hbm.at[rows], blocks.at[rows], in_sem.at[g])

    def load_base(n):
        cols = pl.ds(pl.multiple_of((n % tiles) * tile, tile), tile)
        j = n // tiles
        return pltpu.make_async_copy(
            base_hbm.at[j, :, cols], base.at[j, :, cols], base_sem.at[n]
        )

    def store_rows(g):
        rows = pl.ds(pl.multiple_of(g * GROUP, GROUP), GROUP)
        return pltpu.make_async_copy(out_rows.at[rows], out_hbm.at[rows], out_sem.at[g])

    for g in range(groups):
        load_blocks(g).start()
    for n in range(2 * tiles):
        load_base(n).start()

    permute = to_rows(slots, 1)

    def unpack_group(g, _):
        load_blocks(g).wait()
        rows = dot(permute, blocks[pl.ds(pl.multiple_of(g * GROUP, GROUP), GROUP), :]).astype(BF16)
        place = pl.ds(pl.multiple_of(g * span, span), span)
        for p in range(pieces):
            inputs[place, p * piece : (p + 1) * piece] = rows[p * span : (p + 1) * span, :]
        return 0

    lax.fori_loop(0, groups, unpack_group, 0)
    keep = pltpu.make_async_copy(inputs, inputs_hbm, row_sem)
    keep.start()

    low_act_ref[...] = dot(inputs[...], low_ref[...]).astype(BF16)

    def forward(n, _):
        load_base(n).wait()
        j = n // tiles
        cols = pl.ds(pl.multiple_of((n % tiles) * tile, tile), tile)
        linear[j, :, cols] = dot(inputs[...], base[j, :, cols])
        return 0

    lax.fori_loop(0, 2 * tiles, forward, 0)

    for n in range(tiles):
        cols = slice(n * tile, (n + 1) * tile)
        gate_linear = linear[0, :, cols] + dot(low_act_ref[:, :rank], high_ref[0, :, cols])
        up_linear = linear[1, :, cols] + dot(low_act_ref[:, rank:], high_ref[1, :, cols])
        gate_scale = scale_ref[0:1, cols]
        up_scale = scale_ref[1:2, cols]
        gate = gate_linear * gate_scale
        up = up_linear * up_scale
        sigmoid = 1.0 / (1.0 + jnp.exp(-gate))
        active = gate * sigmoid
        units = (active * up).astype(BF16)
        units_ref[:, cols] = units
        grad_hidden = grad_hidden_ref[:, cols]
        part = jnp.sum(units.astype(F32) * grad_hidden, axis=1, keepdims=True)
        if n == 0:
            products_ref[...] = part
        else:
            products_ref[...] += part
        grad_gate = grad_hidden * up * sigmoid * (1.0 + gate * (1.0 - sigmoid))
        grad_up = grad_hidden * active
        mag_ref[0:1, cols] = jnp.sum(grad_gate * gate_linear, axis=0, keepdims=True)
        mag_ref[1:2, cols] = jnp.sum(grad_up * up_linear, axis=0, keepdims=True)
        grad_linear_ref[0, :, cols] = (grad_gate * gate_scale).astype(BF16)
        grad_linear_ref[1, :, cols] = (grad_up * up_scale).astype(BF16)

    for j in range(2):
        back_ref[:, j * rank : (j + 1) * rank] = contract(
            grad_linear_ref[j], high_ref[j], 1, 1
        ).astype(BF16)

    keep.wait()

    def backward(n, _):
        rows = pl.ds(pl.multiple_of(n * tile, tile), tile)
        grad = contract(grad_linear_ref[0], base[0, rows, :], 1, 1)
        grad = grad + contract(grad_linear_ref[1], base[1, rows, :], 1, 1)
        grad = grad + contract(back_ref[...], low_ref[rows, :], 1, 1)
        inputs[:, rows] = grad.astype(BF16)
        return 0

    lax.fori_loop(0, depth // tile, backward, 0)

    arrange = to_blocks(slots, 1)

    def pack_group(g, _):
        place = pl.ds(pl.multiple_of(g * span, span), span)
        stack = jnp.concatenate(
            [inputs[place, p * piece : (p + 1) * piece] for p in range(pieces)], axis=0
        )
        rows = pl.ds(pl.multiple_of(g * GROUP, GROUP), GROUP)
        out_rows[rows, :] = dot(arrange, stack).astype(BF16)
        store_rows(g).start()
        return 0

    lax.fori_loop(0, groups, pack_group, 0)
    for g in range(groups):
        store_rows(g).wait()


def expert(slots, blocks, base, low, high, scale, grad_hidden):
    total, piece = blocks.shape
    branches, depth, ffw = base.shape
    count = total * slots // BLOCK
    rank2 = low.shape[1]
    groups = total // GROUP
    vmem = pl.BlockSpec(memory_space=pltpu.VMEM)
    hbm = pl.BlockSpec(memory_space=pl.ANY)
    return pl.pallas_call(
        functools.partial(expert_kernel, slots),
        in_specs=[hbm, hbm, vmem, vmem, vmem, vmem],
        out_specs=[hbm, hbm, vmem, vmem, vmem, vmem, vmem, vmem],
        out_shape=[
            jax.ShapeDtypeStruct((total, piece), BF16),
            jax.ShapeDtypeStruct((count, depth), BF16),
            jax.ShapeDtypeStruct((count, ffw), BF16),
            jax.ShapeDtypeStruct((count, rank2), BF16),
            jax.ShapeDtypeStruct((branches, count, ffw), BF16),
            jax.ShapeDtypeStruct((count, rank2), BF16),
            jax.ShapeDtypeStruct((count, 1), F32),
            jax.ShapeDtypeStruct((branches, ffw), F32),
        ],
        scratch_shapes=[
            pltpu.VMEM((total, piece), BF16),
            pltpu.VMEM(base.shape, BF16),
            pltpu.VMEM((count, depth), BF16),
            pltpu.VMEM((branches, count, ffw), F32),
            pltpu.VMEM((total, piece), BF16),
            pltpu.SemaphoreType.DMA((groups,)),
            pltpu.SemaphoreType.DMA((2 * ffw // 256,)),
            pltpu.SemaphoreType.DMA,
            pltpu.SemaphoreType.DMA((groups,)),
        ],
        compiler_params=params(56),
        cost_estimate=cost(4 * count * depth * ffw * branches, 30 * MB),
        name="expert",
    )(blocks, base, low, high, scale, grad_hidden)


def expert_grads_kernel(
    halves, cotangent_ref, scale_ref, base_ref, high_ref, units_ref, low_out_ref, back_low_ref,
    *rest
):
    inputs = rest[:halves]
    low_acts, grad_linears, backs = (
        rest[halves : 2 * halves], rest[2 * halves : 3 * halves], rest[3 * halves : 4 * halves]
    )
    mag_ref, high_grad_ref, low_in_ref, low_grad_ref, high_in_ref, low_down, low_down_t, back_t = (
        rest[4 * halves :]
    )
    count = units_ref.shape[0] // halves
    rank = low_out_ref.shape[1]

    @pl.when(pl.program_id(0) == 0)
    def _():
        low = dot(units_ref[...], low_out_ref[...])
        low_down[...] = low.astype(BF16)
        low_down_t[...] = low.T.astype(BF16)
        low_grad_ref[...] = dot(back_low_ref[...].astype(F32).T.astype(BF16), units_ref[...])
        high_in_ref[...] = jnp.zeros_like(high_in_ref)
        for h in range(halves):
            back_t[h] = backs[h][...].astype(F32).T.astype(BF16)
            low_act_t = low_acts[h][...].astype(F32).T.astype(BF16)
            for j in range(2):
                high_in_ref[j] += dot(low_act_t[j * rank : (j + 1) * rank], grad_linears[h][j])

    mag = jnp.zeros((1, base_ref.shape[1]), F32)
    low_in = jnp.zeros(low_in_ref.shape, F32)
    for h in range(halves):
        rows = slice(h * count, (h + 1) * count)
        linear = dot(units_ref[rows, :], base_ref[...]) + dot(low_down[rows, :], high_ref[...])
        mag = mag + jnp.sum(linear * cotangent_ref[rows, :].astype(F32), axis=0, keepdims=True)
        low_in = low_in + dot(back_t[h], inputs[h][...])
    mag_ref[...] = mag
    low_in_ref[...] = low_in
    grad = (cotangent_ref[...].astype(F32) * scale_ref[...]).astype(BF16)
    high_grad_ref[...] = dot(low_down_t[...], grad)


def expert_grads(
    cotangent, scale, base, high, units, low_out, back_low, inputs, low_acts, grad_linears,
    backs,
):
    halves = len(inputs)
    ffw, width = base.shape
    count, rank = back_low.shape
    tile = 512
    whole = lambda array: pl.BlockSpec(array.shape, lambda i: (0,) * array.ndim)
    part = lambda rows: pl.BlockSpec((rows, tile), lambda i: (0, i))
    fixed = [units, low_out, back_low]
    return pl.pallas_call(
        functools.partial(expert_grads_kernel, halves),
        grid=(width // tile,),
        in_specs=[part(count), part(1), part(ffw), part(rank)]
        + [whole(array) for array in fixed]
        + [part(count // halves)] * halves
        + [whole(array) for array in low_acts + grad_linears + backs],
        out_specs=[
            part(1),
            part(rank),
            part(2 * rank),
            pl.BlockSpec((rank, ffw), lambda i: (0, 0)),
            pl.BlockSpec((2, rank, ffw), lambda i: (0, 0, 0)),
        ],
        out_shape=[
            jax.ShapeDtypeStruct((1, width), F32),
            jax.ShapeDtypeStruct((rank, width), F32),
            jax.ShapeDtypeStruct((2 * rank, width), F32),
            jax.ShapeDtypeStruct((rank, ffw), F32),
            jax.ShapeDtypeStruct((2, rank, ffw), F32),
        ],
        scratch_shapes=[
            pltpu.VMEM((count, rank), BF16),
            pltpu.VMEM((rank, count), BF16),
            pltpu.VMEM((halves, 2 * rank, count // halves), BF16),
        ],
        compiler_params=params(60),
        cost_estimate=cost(1, 1),
        name="expert_grads",
    )(cotangent, scale, base, high, *fixed, *inputs, *low_acts, *grad_linears, *backs)


def square_norm(base, low, high):
    merged = base.astype(F32) + dot(low, high)
    return jnp.sqrt(jnp.sum(merged * merged, axis=0))


def shards(
    query, keyval, doc_lengths, norm_gain, router_logits, expert_ids, grad_out,
    base_in, low_in, high_in, mag_in, base_out, low_out, high_out, mag_out,
):
    query, local_kv, grad_out = query[0], keyval[0], grad_out[0]
    base_in, low_in, high_in, mag_in = base_in[0], low_in[0], high_in[0], mag_in[0]
    base_out, low_out, high_out, mag_out = base_out[0], low_out[0], high_out[0], mag_out[0]
    ids = expert_ids[0]
    tokens, width = query.shape
    top = ids.shape[1]
    experts = lax.axis_size("ctx") * lax.axis_size("ep")
    axes = ("ctx", "ep")
    gain = norm_gain[None, :]
    halves = 2
    slots_each = CAP // halves
    ctx_count = lax.axis_size("ctx")

    def exchange(blocks):
        split = blocks.reshape(experts, BLOCK, blocks.shape[1])
        moved = lax.all_to_all(split, axes, split_axis=0, concat_axis=0, tiled=True)
        return moved.reshape(blocks.shape)

    named = jnp.zeros((experts, tokens), jnp.bool_)
    each = jnp.arange(experts, dtype=jnp.int32)[:, None]
    for k in range(top):
        named = named | (ids[:, k][None, :] == each)
    earlier = jnp.arange(tokens)[:, None] < jnp.arange(tokens)[None, :]
    before = dot(named.astype(BF16), earlier.astype(BF16))
    slots = jnp.where(named, before, -1.0)

    seen, outgoing_grad = open_exchange(local_kv, slots, grad_out, ctx_count)
    first = lax.axis_index("ctx") * tokens
    place = jnp.concatenate(
        [
            jnp.stack([first - REACH * tokens, first]).astype(jnp.int32),
            jnp.cumsum(doc_lengths[0]).astype(jnp.int32),
        ]
    )

    arrived_grad = exchange(outgoing_grad)

    prob, hidden = attend(place, query, seen)
    *outgoing, rinv = dispatch(slots, hidden, gain, True, halves)

    logits, hidden = lax.optimization_barrier((router_logits[0], hidden))
    gate_expo = jnp.exp(logits - jnp.max(logits, axis=-1, keepdims=True))
    gates = gate_expo / jnp.sum(gate_expo, axis=-1, keepdims=True)
    dense_gates = jnp.zeros((tokens, experts), F32)
    chosen = [ids[:, k : k + 1] == each.reshape(1, experts) for k in range(top)]
    for k in range(top):
        dense_gates = dense_gates + jnp.where(chosen[k], gates[:, k : k + 1], 0.0)
    token_slots = slots.T

    norm_in = jnp.stack([square_norm(base_in[j], low_in[j], high_in[j]) for j in range(2)])
    scale_in = mag_in / norm_in
    norm_out = square_norm(base_out, low_out, high_out)
    scale_out = mag_out / norm_out
    cotangent = unpack(arrived_grad, halves).reshape(experts * CAP, width)
    grad_linear_out = (cotangent.astype(F32) * scale_out).astype(BF16)
    back_low = contract(grad_linear_out, high_out, 1, 1).astype(BF16)
    grad_hidden = contract(grad_linear_out, base_out, 1, 1) + contract(back_low, low_out, 1, 1)
    low_pair = jnp.concatenate([low_in[0], low_in[1]], axis=1)
    arrived = [exchange(outgoing[0])]
    second, grad_hidden, scale_in, low_pair, dense_gates, token_slots, _ = lax.optimization_barrier(
        (outgoing[1], grad_hidden, scale_in, low_pair, dense_gates, token_slots, arrived[0])
    )
    arrived.append(exchange(second))

    rows_each = experts * slots_each
    returned, results = [], []
    for h in range(halves):
        outgoing_rows, *result = expert(
            slots_each, arrived[h], base_in, low_pair, high_in, scale_in,
            grad_hidden[h * rows_each : (h + 1) * rows_each],
        )
        returned.append(exchange(outgoing_rows))
        results.append(result)
    results, first_returned = lax.optimization_barrier((results, returned[0]))
    returned[0] = first_returned
    inputs, units, low_acts, grad_linears, backs, products, mag_sums = zip(*results)

    mag_sum, grad_high_out, low_in_t, low_out_t, grad_high_in = expert_grads(
        cotangent, scale_out[None, :], base_out, high_out, jnp.concatenate(units, axis=0), low_out,
        back_low, inputs, low_acts, grad_linears, backs,
    )
    grad_mag_out = mag_sum[0] / norm_out
    grad_low_out = low_out_t.T
    grad_low_in = low_in_t.reshape(2, -1, width).transpose(0, 2, 1)
    grad_mag_in = sum(mag_sums) / norm_in
    products = jnp.concatenate(
        [part.astype(BF16).astype(F32).reshape(experts, slots_each) for part in products], axis=1
    )
    products = jnp.pad(products, ((0, 0), (0, HEAD - CAP))).reshape(ctx_count, -1, HEAD)

    partial = combine_first(token_slots, dense_gates, returned[0], halves)
    grad_heads = combine_last(
        token_slots, dense_gates, returned[1], partial, gain, grad_out, hidden, rinv, halves
    )
    grad_query, grad_keyval, arrived_products = finish(query, grad_heads, prob, seen, products)
    grad_query = (grad_query.astype(F32) * HEAD ** (-0.5)).astype(BF16)
    dense_products = jnp.zeros((tokens, experts), F32)
    for r in range(CAP):
        dense_products = dense_products + jnp.where(
            token_slots == r, arrived_products[r][None, :], 0.0
        )
    grad_gate = jnp.stack(
        [jnp.sum(jnp.where(chosen[k], dense_products, 0.0), axis=1) for k in range(top)], axis=1
    )
    grad_logits = gates * (grad_gate - jnp.sum(gates * grad_gate, axis=-1, keepdims=True))

    return (
        grad_query[None],
        grad_keyval[None],
        grad_logits[None],
        grad_low_in[None],
        grad_high_in[None],
        grad_mag_in[None],
        grad_low_out[None],
        grad_high_out[None],
        grad_mag_out[None],
    )


def solution(mesh):
    rows = P("ep", "ctx", None)
    own = lambda extra: P(("ctx", "ep"), *([None] * extra))
    in_specs = (
        rows, rows, P("ep", None), P(), rows, rows, rows,
        own(3), own(3), own(3), own(2), own(2), own(2), own(2), own(1),
    )
    out_specs = (rows, rows, rows, own(3), own(3), own(2), own(2), own(2), own(1))
    return jax.shard_map(shards, mesh=mesh, in_specs=in_specs, out_specs=out_specs, check_vma=False)
```

```python
import functools

import jax
import jax.numpy as jnp
from jax import lax
from jax.experimental import pallas as pl
from jax.experimental.pallas import tpu as pltpu
from jax.sharding import PartitionSpec as P

F32 = jnp.float32
BF16 = jnp.bfloat16
MESH = pl.DeviceIdType.MESH
HEAD = 128
NEGATIVE = -1e30
EPSILON = 1e-06
CAP = 4
BLOCK = 16
GROUP = 256
PER_GROUP = GROUP // BLOCK
REACH = 4
MB = 1 << 20


def params(megabytes):
    return pltpu.CompilerParams(vmem_limit_bytes=megabytes * MB)


def cost(flops, size, transcendentals=0):
    return pl.CostEstimate(flops=flops, bytes_accessed=size, transcendentals=transcendentals)


def iota(shape, dim):
    return lax.broadcasted_iota(jnp.int32, shape, dim)


def dot(left, right):
    return jnp.dot(left, right, preferred_element_type=F32)


def contract(left, right, left_dim, right_dim):
    return lax.dot_general(
        left, right, (((left_dim,), (right_dim,)), ((), ())), preferred_element_type=F32
    )


def is_row(row, col, slots, halves):
    pieces = BLOCK // (slots * halves)
    span = PER_GROUP * slots * halves
    return (
        (row // span == (col // (slots * halves)) % pieces)
        & ((row // (PER_GROUP * slots)) % halves == (col // slots) % halves)
        & ((row // slots) % PER_GROUP == col // BLOCK)
        & (row % slots == col % slots)
    )


def to_rows(slots, halves):
    same = is_row(iota((GROUP, GROUP), 0), iota((GROUP, GROUP), 1), slots, halves)
    return same.astype(F32).astype(BF16)


def to_blocks(slots, halves):
    same = is_row(iota((GROUP, GROUP), 1), iota((GROUP, GROUP), 0), slots, halves)
    return same.astype(F32).astype(BF16)


def dispatch_kernel(with_norm, slots_ref, rows_ref, gain_ref, *rest):
    outs, rinv_ref, stack = rest[:-2], rest[-2], rest[-1]
    tokens, width = rows_ref.shape
    slots = CAP // len(outs)
    pieces = BLOCK // slots
    piece = width // pieces

    @pl.when(pl.program_id(0) == 0)
    def _():
        if with_norm:
            square = jnp.zeros((tokens, 1), F32)
            for p in range(pieces):
                part = rows_ref[:, p * piece : (p + 1) * piece].astype(F32)
                square = square + jnp.sum(part * part, axis=1, keepdims=True)
            rinv = lax.rsqrt(square / width + EPSILON)
        else:
            rinv = jnp.ones((tokens, 1), F32)
        rinv_ref[...] = rinv
        for p in range(pieces):
            cols = slice(p * piece, (p + 1) * piece)
            part = rows_ref[:, cols]
            if with_norm:
                part = (part.astype(F32) * rinv * gain_ref[:, cols]).astype(BF16)
            stack[p * tokens : (p + 1) * tokens, :] = part

    spread = (iota((GROUP, PER_GROUP), 0) // BLOCK == iota((GROUP, PER_GROUP), 1)).astype(F32)
    slot = dot(spread.astype(BF16), slots_ref[...].astype(BF16))
    row = iota((GROUP, tokens), 0)
    for half, out_ref in enumerate(outs):
        hit = slot == (half * slots + row % slots).astype(F32)
        parts = []
        for p in range(pieces):
            own = hit & ((row // slots) % pieces == p)
            parts.append(jnp.where(own, 1.0, 0.0).astype(BF16))
        out_ref[...] = dot(jnp.concatenate(parts, axis=1), stack[...]).astype(BF16)


def dispatch(slots, rows, gain, with_norm, halves):
    experts, tokens = slots.shape
    width = rows.shape[1]
    total = experts * BLOCK
    pieces = BLOCK * halves // CAP
    piece = width // pieces
    whole = lambda shape: pl.BlockSpec(shape, lambda i: (0, 0))
    return pl.pallas_call(
        functools.partial(dispatch_kernel, with_norm),
        grid=(total // GROUP,),
        in_specs=[
            pl.BlockSpec((PER_GROUP, tokens), lambda i: (i, 0)),
            whole((tokens, width)),
            whole((1, width)),
        ],
        out_specs=[pl.BlockSpec((GROUP, piece), lambda i: (i, 0))] * halves + [whole((tokens, 1))],
        out_shape=[jax.ShapeDtypeStruct((total, piece), BF16)] * halves
        + [jax.ShapeDtypeStruct((tokens, 1), F32)],
        scratch_shapes=[pltpu.VMEM((pieces * tokens, piece), BF16)],
        compiler_params=params(60),
        cost_estimate=cost(2 * total * tokens * width * halves, 10 * MB),
        name="dispatch",
    )(slots, rows, gain)


def unpack_kernel(halves, blocks_ref, out_ref):
    piece = blocks_ref.shape[1]
    slots = CAP // halves
    pieces = BLOCK // CAP
    rows = dot(to_rows(slots, halves), blocks_ref[...]).astype(BF16)
    count = PER_GROUP * slots
    for p in range(pieces):
        for half in range(halves):
            first = (p * halves + half) * count
            out_ref[half, :, p * piece : (p + 1) * piece] = rows[first : first + count, :]


def unpack(blocks, halves):
    total, piece = blocks.shape
    pieces = BLOCK // CAP
    count = total // pieces // halves
    return pl.pallas_call(
        functools.partial(unpack_kernel, halves),
        grid=(total // GROUP,),
        in_specs=[pl.BlockSpec((GROUP, piece), lambda i: (i, 0))],
        out_specs=pl.BlockSpec(
            (halves, GROUP // pieces // halves, pieces * piece), lambda i: (0, i, 0)
        ),
        out_shape=jax.ShapeDtypeStruct((halves, count, pieces * piece), BF16),
        compiler_params=params(60),
        cost_estimate=cost(2 * total * GROUP * piece, 8 * MB),
        name="unpack",
    )(blocks)


def open_kernel(
    count, own_ref, ids_ref, rows_ref, seen_ref, out_hbm, slots_ref, token_slots_ref, stack, blocks, wanted, masks,
    send_sem, recv_sem, own_sem, out_sem,
):
    tokens, width = rows_ref.shape
    pieces = BLOCK // CAP
    piece = width // pieces
    groups = blocks.shape[0] // GROUP
    me = lax.axis_index("ctx")
    core = me % 2
    other = me + 1 - 2 * core

    def slot(j):
        return seen_ref.at[pl.ds((REACH - j) * tokens, tokens)]

    def copy(source, j, target, index):
        return pltpu.make_async_remote_copy(
            src_ref=source,
            dst_ref=slot(j),
            send_sem=send_sem.at[index],
            recv_sem=recv_sem.at[index],
            device_id={"ctx": target},
            device_id_type=MESH,
        )

    near = copy(own_ref, 2, me + 2, 0)
    far = copy(own_ref, 4, me + 4, 1)
    beside = copy(own_ref, 1, other, 2)
    near_even = copy(slot(2), 3, other, 3)
    near_odd = copy(slot(2), 1, other, 3)
    far_odd = copy(slot(4), 3, other, 4)

    keep = pltpu.make_async_copy(own_ref, slot(0), own_sem)
    keep.start()
    barrier = pltpu.get_barrier_semaphore()
    peers = 1
    for offset in (2, 4, -2, -4):
        present = (me + offset >= 0) & (me + offset < count)
        peers = peers + present.astype(jnp.int32)

        @pl.when(present)
        def _():
            pl.semaphore_signal(
                barrier, inc=1, device_id={"ctx": me + offset}, device_id_type=MESH
            )

    pl.semaphore_signal(barrier, inc=1, device_id={"ctx": other}, device_id_type=MESH)

    experts = slots_ref.shape[0]
    named = jnp.zeros((tokens, experts), F32)
    for k in range(ids_ref.shape[1]):
        named = named + (ids_ref[:, k : k + 1] == iota((tokens, experts), 1)).astype(F32)
    earlier = (iota((tokens, tokens), 1) < iota((tokens, tokens), 0)).astype(F32).astype(BF16)
    token_slots = jnp.where(named > 0.0, dot(earlier, named.astype(BF16)), -1.0)
    token_slots_ref[...] = token_slots
    slots_ref[...] = token_slots.T

    pl.semaphore_wait(barrier, peers)

    @pl.when(me + 4 < count)
    def _():
        far.start()

    @pl.when(me + 2 < count)
    def _():
        near.start()

    @pl.when(core == 0)
    def _():
        beside.start()

    for j in range(1, REACH + 1):

        @pl.when(me < j)
        def _():
            seen_ref[(REACH - j) * tokens : (REACH - j + 1) * tokens, :] = jnp.zeros(
                own_ref.shape, own_ref.dtype
            )

    for p in range(pieces):
        stack[p * tokens : (p + 1) * tokens, :] = rows_ref[:, p * piece : (p + 1) * piece]
    spread = (iota((GROUP, PER_GROUP), 0) // BLOCK == iota((GROUP, PER_GROUP), 1)).astype(F32)
    spread = spread.astype(BF16)
    row = iota((GROUP, tokens), 0)
    wanted[...] = (row % CAP).astype(F32)
    for p in range(pieces):
        own = (row // CAP) % pieces == p
        masks[:, p * tokens : (p + 1) * tokens] = own.astype(F32).astype(BF16)

    def store(g):
        rows = pl.ds(pl.multiple_of(g * GROUP, GROUP), GROUP)
        return pltpu.make_async_copy(blocks.at[rows], out_hbm.at[rows], out_sem.at[g])

    def pick(g, _):
        named = slots_ref[pl.ds(pl.multiple_of(g * PER_GROUP, PER_GROUP), PER_GROUP), :]
        hit = jnp.where(dot(spread, named.astype(BF16)) == wanted[...], 1.0, 0.0).astype(BF16)
        picker = jnp.concatenate([hit] * pieces, axis=1) * masks[...]
        rows = pl.ds(pl.multiple_of(g * GROUP, GROUP), GROUP)
        blocks[rows, :] = dot(picker, stack[...]).astype(BF16)
        store(g).start()
        return 0

    lax.fori_loop(0, groups // 2, pick, 0)

    @pl.when(me >= 2)
    def _():
        near.wait_recv()

        @pl.when(core == 0)
        def _():
            near_even.start()

        @pl.when(core == 1)
        def _():
            near_odd.start()

    lax.fori_loop(groups // 2, groups, pick, 0)

    @pl.when(me >= 4)
    def _():
        far.wait_recv()

        @pl.when(core == 1)
        def _():
            far_odd.start()

    @pl.when(core == 1)
    def _():
        beside.wait_recv()

    @pl.when(core == 0)
    def _():
        beside.wait_send()

    @pl.when(me >= 2)
    def _():
        near_even.wait_send()
        near_even.wait_recv()

    @pl.when((me >= 4) & (core == 1))
    def _():
        far_odd.wait_send()

    @pl.when((me >= 4) & (core == 0))
    def _():
        far_odd.wait_recv()

    @pl.when(me + 4 < count)
    def _():
        far.wait_send()

    @pl.when(me + 2 < count)
    def _():
        near.wait_send()

    keep.wait()
    for g in range(groups):
        store(g).wait()


def open_exchange(own, ids, rows, experts, count):
    tokens = ids.shape[0]
    total = experts * BLOCK
    piece = rows.shape[1] * CAP // BLOCK
    vmem = pl.BlockSpec(memory_space=pltpu.VMEM)
    return pl.pallas_call(
        functools.partial(open_kernel, count),
        in_specs=[vmem] * 3,
        out_specs=[vmem, pl.BlockSpec(memory_space=pl.ANY), vmem, vmem],
        out_shape=[
            jax.ShapeDtypeStruct(((REACH + 1) * tokens, own.shape[1]), own.dtype),
            jax.ShapeDtypeStruct((total, piece), BF16),
            jax.ShapeDtypeStruct((experts, tokens), F32),
            jax.ShapeDtypeStruct((tokens, experts), F32),
        ],
        scratch_shapes=[
            pltpu.VMEM((BLOCK // CAP * tokens, piece), BF16),
            pltpu.VMEM((total, piece), BF16),
            pltpu.VMEM((GROUP, tokens), F32),
            pltpu.VMEM((GROUP, BLOCK // CAP * tokens), BF16),
            pltpu.SemaphoreType.DMA((5,)),
            pltpu.SemaphoreType.DMA((5,)),
            pltpu.SemaphoreType.DMA,
            pltpu.SemaphoreType.DMA((total // GROUP,)),
        ],
        compiler_params=pltpu.CompilerParams(
            collective_id=0, has_side_effects=True, vmem_limit_bytes=60 * MB
        ),
        name="open_exchange",
    )(own, ids, rows)


def visible(place_ref, window, tokens):
    kpos = place_ref[0] + iota((window, tokens), 0)
    qpos = place_ref[1] + iota((window, tokens), 1)
    kdoc = jnp.zeros((window, tokens), jnp.int32)
    qdoc = jnp.zeros((window, tokens), jnp.int32)
    for d in range(4):
        end = place_ref[2 + d]
        kdoc = kdoc + (kpos >= end).astype(jnp.int32)
        qdoc = qdoc + (qpos >= end).astype(jnp.int32)
    return (kpos >= 0) & (kpos <= qpos) & (kdoc == qdoc)


def stack_heads(ref, heads):
    return jnp.concatenate([ref[:, h * HEAD : (h + 1) * HEAD] for h in range(heads)], axis=0)


def head_pair(ref, h):
    return jnp.concatenate(
        [ref[:, h * HEAD : (h + 1) * HEAD], ref[:, (h + 1) * HEAD : (h + 2) * HEAD]], axis=0
    )


def attend_kernel(heads, per_kv, place_ref, query_ref, keyval_ref, prob_ref, out_ref, bias):
    tokens = query_ref.shape[0]
    window = keyval_ref.shape[0]
    step = pl.program_id(0)
    half = keyval_ref.shape[1] // 2
    scale = HEAD ** (-0.5)

    @pl.when(step == 0)
    def _():
        hidden = jnp.where(visible(place_ref, window, tokens), 0.0, NEGATIVE)
        bias[:, :tokens] = hidden
        bias[:, tokens:] = hidden

    for m in range(half // HEAD):

        @pl.when(step // (per_kv // heads) == m)
        def _():
            keys = keyval_ref[:, m * HEAD : (m + 1) * HEAD]
            values_t = keyval_ref[:, half + m * HEAD : half + (m + 1) * HEAD].T
            for h in range(0, heads, 2):
                raw = contract(keys, head_pair(query_ref, h), 1, 1) * scale + bias[...]
                peak = jnp.max(raw, axis=0, keepdims=True)
                expo = jnp.exp(raw - peak)
                total = jnp.sum(expo, axis=0, keepdims=True)
                prob = (expo * (1.0 / total)).astype(BF16)
                prob_ref[0, :, h * tokens : (h + 2) * tokens] = prob
                mixed = dot(values_t, prob).T.astype(BF16)
                out_ref[:, h * HEAD : (h + 1) * HEAD] = mixed[:tokens]
                out_ref[:, (h + 1) * HEAD : (h + 2) * HEAD] = mixed[tokens:]


def attend(place, query, keyval):
    tokens, width = query.shape
    window = keyval.shape[0]
    kv_heads = keyval.shape[1] // 2 // HEAD
    per_kv = width // HEAD // kv_heads
    heads = 8
    steps = width // HEAD // heads
    return pl.pallas_call(
        functools.partial(attend_kernel, heads, per_kv),
        grid=(steps,),
        in_specs=[
            pl.BlockSpec(memory_space=pltpu.SMEM),
            pl.BlockSpec((tokens, heads * HEAD), lambda i: (0, i)),
            pl.BlockSpec(keyval.shape, lambda i: (0, 0)),
        ],
        out_specs=[
            pl.BlockSpec((1, window, heads * tokens), lambda i: (i, 0, 0)),
            pl.BlockSpec((tokens, heads * HEAD), lambda i: (0, i)),
        ],
        out_shape=[
            jax.ShapeDtypeStruct((steps, window, heads * tokens), BF16),
            jax.ShapeDtypeStruct((tokens, width), BF16),
        ],
        scratch_shapes=[pltpu.VMEM((window, 2 * tokens), F32)],
        compiler_params=params(60),
        cost_estimate=cost(4 * tokens * width * window, 9 * MB, tokens * width * window // HEAD),
        name="attend",
    )(place, query, keyval)


def finish_kernel(
    heads, steps_per_kv, count, ep_count, query_ref, grad_ref, prob_ref, keys_ref, values_ref,
    products_ref, grad_query_ref, grad_keyval_ref, returned_ref,
    key_sum, value_sum, terms, landed, gathered, turned, arrived,
    send_sem, recv_sem, ctx_send, ctx_recv, ep_send, ep_recv,
):
    step = pl.program_id(0)
    last = pl.num_programs(0) - 1
    tokens = query_ref.shape[0]
    half = grad_keyval_ref.shape[1] // 2
    scale = HEAD ** (-0.5)
    me = lax.axis_index("ctx")
    place = lax.axis_index("ep")
    barrier = pltpu.get_barrier_semaphore()

    def send_terms(j, m, part):
        return pltpu.make_async_remote_copy(
            src_ref=terms.at[m, part, pl.ds((REACH - j) * tokens, tokens)],
            dst_ref=landed.at[j - 1, m, part],
            send_sem=send_sem.at[j - 1, m, part],
            recv_sem=recv_sem.at[j - 1, m, part],
            device_id={"ctx": me - j},
            device_id_type=MESH,
        )

    def send_part(part, total):
        for m in range(landed.shape[1]):

            @pl.when(step == (m + 1) * steps_per_kv - 1)
            def _():
                terms[m, part] = total().astype(BF16)
                for j in range(REACH, 0, -1):

                    @pl.when(me >= j)
                    def _():
                        send_terms(j, m, part).start()

    def along_ctx(d):
        target = (me + d) % count
        return pltpu.make_async_remote_copy(
            src_ref=products_ref.at[target],
            dst_ref=gathered.at[me],
            send_sem=ctx_send.at[d - 1],
            recv_sem=ctx_recv.at[d - 1],
            device_id={"ctx": target},
            device_id_type=MESH,
        )

    def along_ep(d):
        target = (place + d) % ep_count
        return pltpu.make_async_remote_copy(
            src_ref=turned.at[target],
            dst_ref=arrived.at[place],
            send_sem=ep_send.at[d - 1],
            recv_sem=ep_recv.at[d - 1],
            device_id={"ep": target},
            device_id_type=MESH,
        )

    @pl.when(step == 0)
    def _():
        for d in range(1, count):
            pl.semaphore_signal(
                barrier, inc=1, device_id={"ctx": (me + d) % count}, device_id_type=MESH
            )
        for d in range(1, ep_count):
            pl.semaphore_signal(
                barrier, inc=1, device_id={"ep": (place + d) % ep_count}, device_id_type=MESH
            )
        gathered[me] = products_ref[me]

    @pl.when(step == 1)
    def _():
        pl.semaphore_wait(barrier, count + ep_count - 2)
        for d in range(1, count):
            along_ctx(d).start()

    @pl.when(step == last - 1)
    def _():
        for d in range(1, count):
            along_ctx(d).wait_recv()
        for c in range(count):
            turned[:, c, :] = gathered[c]
        arrived[place] = turned[place]
        for d in range(1, ep_count):
            along_ep(d).start()

    @pl.when(step % steps_per_kv == 0)
    def _():
        key_sum[...] = jnp.zeros_like(key_sum)
        value_sum[...] = jnp.zeros_like(value_sum)

    grad = stack_heads(grad_ref, heads)
    prob = prob_ref[0]
    value_sum[...] += dot(prob, grad)
    send_part(1, lambda: value_sum[...])
    wide = prob.astype(F32)
    moved = wide * contract(values_ref[...], grad, 1, 1)
    delta = jnp.sum(moved, axis=0, keepdims=True)
    dscore = (moved - wide * delta).astype(BF16)
    key_sum[...] += dot(dscore, stack_heads(query_ref, heads))
    send_part(0, lambda: key_sum[...] * scale)
    grad_query = dot(keys_ref[...].T, dscore).T.astype(BF16)
    for h in range(heads):
        grad_query_ref[:, h * HEAD : (h + 1) * HEAD] = grad_query[h * tokens : (h + 1) * tokens]

    @pl.when(step == last)
    def _():
        for d in range(1, count):
            along_ctx(d).wait_send()
        for d in range(1, ep_count):
            along_ep(d).wait_send()
            along_ep(d).wait_recv()
        by_expert = jnp.concatenate([arrived[:, c, :] for c in range(count)], axis=0)
        returned_ref[...] = by_expert.T[: returned_ref.shape[0], :]
        for m in range(landed.shape[1]):
            for part in (1, 0):
                for j in range(1, REACH + 1):

                    @pl.when(me + j < count)
                    def _():
                        send_terms(j, m, part).wait_recv()

                    @pl.when(me + j >= count)
                    def _():
                        landed[j - 1, m, part] = jnp.zeros(landed.shape[3:], landed.dtype)

                total = terms[m, part, REACH * tokens :, :].astype(F32)
                for j in range(REACH):
                    total = total + landed[j, m, part].astype(F32)
                first = part * half + m * HEAD
                grad_keyval_ref[:, first : first + HEAD] = total.astype(BF16)
                for j in range(1, REACH + 1):

                    @pl.when(me >= j)
                    def _():
                        send_terms(j, m, part).wait_send()


def finish(query, grad, prob, keyval, products):
    tokens, width = query.shape
    window = keyval.shape[0]
    count, ep_count, lanes = products.shape
    kv_heads = keyval.shape[1] // 2 // HEAD
    heads = prob.shape[2] // tokens
    steps = prob.shape[0]
    steps_per_kv = steps // kv_heads
    rows = pl.BlockSpec((tokens, heads * HEAD), lambda i: (0, i))
    return pl.pallas_call(
        functools.partial(finish_kernel, heads, steps_per_kv, count, ep_count),
        grid=(steps,),
        in_specs=[
            rows,
            rows,
            pl.BlockSpec((1,) + prob.shape[1:], lambda i: (i, 0, 0)),
            pl.BlockSpec((window, HEAD), lambda i: (0, i // steps_per_kv)),
            pl.BlockSpec((window, HEAD), lambda i: (0, kv_heads + i // steps_per_kv)),
            pl.BlockSpec(products.shape, lambda i: (0, 0, 0)),
        ],
        out_specs=[
            rows,
            pl.BlockSpec((tokens, keyval.shape[1]), lambda i: (0, 0)),
            pl.BlockSpec((8, count * ep_count), lambda i: (0, 0)),
        ],
        out_shape=[
            jax.ShapeDtypeStruct((tokens, width), BF16),
            jax.ShapeDtypeStruct((tokens, keyval.shape[1]), BF16),
            jax.ShapeDtypeStruct((8, count * ep_count), F32),
        ],
        scratch_shapes=[
            pltpu.VMEM((window, HEAD), F32),
            pltpu.VMEM((window, HEAD), F32),
            pltpu.VMEM((kv_heads, 2, window, HEAD), BF16),
            pltpu.VMEM((REACH, kv_heads, 2, tokens, HEAD), BF16),
            pltpu.VMEM((count, ep_count, lanes), F32),
            pltpu.VMEM((ep_count, count, lanes), F32),
            pltpu.VMEM((ep_count, count, lanes), F32),
            pltpu.SemaphoreType.DMA((REACH, kv_heads, 2)),
            pltpu.SemaphoreType.DMA((REACH, kv_heads, 2)),
            pltpu.SemaphoreType.DMA((count - 1,)),
            pltpu.SemaphoreType.DMA((count - 1,)),
            pltpu.SemaphoreType.DMA((ep_count - 1,)),
            pltpu.SemaphoreType.DMA((ep_count - 1,)),
        ],
        compiler_params=pltpu.CompilerParams(
            collective_id=1, has_side_effects=True, vmem_limit_bytes=50 * MB
        ),
        cost_estimate=cost(8 * tokens * width * window, 10 * MB),
        name="finish",
    )(query, grad, prob, keyval, keyval, products)


def gather_rows(slots, blocks_ref, rows, order):
    pieces = BLOCK // slots
    span = PER_GROUP * slots
    groups = blocks_ref.shape[0] // GROUP

    @pl.when(pl.program_id(0) == 0)
    def _():
        order[...] = to_rows(slots, 1)

    for g in range(groups):
        moved = dot(order[...], blocks_ref[g * GROUP : (g + 1) * GROUP, :]).astype(BF16)
        place = pl.ds(pl.multiple_of((pl.program_id(0) * groups + g) * span, span), span)
        for p in range(pieces):
            rows[p, place, :] = moved[p * span : (p + 1) * span, :]


def gate_rows(half, slots, slots_ref, gates_ref):
    tokens, experts = slots_ref.shape
    count = experts * slots
    spread = (iota((experts, count), 0) == iota((experts, count), 1) // slots).astype(F32)
    spread = spread.astype(BF16)
    slot = dot(slots_ref[...].astype(BF16), spread)
    gate = dot(gates_ref[...].astype(BF16), spread)
    own = (half * slots + iota((tokens, count), 1) % slots).astype(F32)
    return jnp.where(slot == own, gate, 0.0).astype(BF16)


def combine_first_kernel(halves, slots_ref, gates_ref, blocks_ref, acc_ref, rows, order):
    slots = CAP // halves
    gather_rows(slots, blocks_ref, rows, order)

    @pl.when(pl.program_id(0) == pl.num_programs(0) - 1)
    def _():
        gate = gate_rows(0, slots, slots_ref, gates_ref)
        for p in range(rows.shape[0]):
            acc_ref[p] = dot(gate, rows[p])


def combine_last_kernel(
    halves, slots_ref, gates_ref, blocks_ref, gain_ref, rinv_ref, first_hbm, grad_out_hbm,
    hidden_hbm, grad_ref, rows, order, acc, first_ref, grad_out_ref, hidden_ref, sem,
):
    step = pl.program_id(0)
    tokens, width = hidden_ref.shape
    loads = [
        pltpu.make_async_copy(source, target, sem.at[i])
        for i, (source, target) in enumerate(
            [(first_hbm, first_ref), (grad_out_hbm, grad_out_ref), (hidden_hbm, hidden_ref)]
        )
    ]

    @pl.when(step == 0)
    def _():
        for load in loads:
            load.start()

    slots = CAP // halves
    pieces, _, piece = acc.shape
    gather_rows(slots, blocks_ref, rows, order)

    @pl.when(step == pl.num_programs(0) - 1)
    def _():
        gate = gate_rows(halves - 1, slots, slots_ref, gates_ref)
        for load in loads:
            load.wait()
        rinv = rinv_ref[...]
        mean = jnp.zeros((tokens, 1), F32)
        for p in range(pieces):
            cols = slice(p * piece, (p + 1) * piece)
            scaled = (dot(gate, rows[p]) + first_ref[p]) * gain_ref[:, cols]
            acc[p] = scaled
            mean = mean + jnp.sum(hidden_ref[:, cols].astype(F32) * scaled, axis=1, keepdims=True)
        mean = mean / width * (rinv * rinv * rinv)
        for p in range(pieces):
            cols = slice(p * piece, (p + 1) * piece)
            grad = (
                grad_out_ref[:, cols].astype(F32)
                + rinv * acc[p]
                - hidden_ref[:, cols].astype(F32) * mean
            )
            grad_ref[:, cols] = grad.astype(BF16)


def combine_first(slots, gates, blocks, halves):
    tokens, experts = slots.shape
    total, piece = blocks.shape
    pieces = BLOCK * halves // CAP
    whole = lambda shape: pl.BlockSpec(shape, lambda i: (0,) * len(shape))
    return pl.pallas_call(
        functools.partial(combine_first_kernel, halves),
        grid=(total // (4 * GROUP),),
        in_specs=[
            whole(slots.shape),
            whole(gates.shape),
            pl.BlockSpec((4 * GROUP, piece), lambda i: (i, 0)),
        ],
        out_specs=whole((pieces, tokens, piece)),
        out_shape=jax.ShapeDtypeStruct((pieces, tokens, piece), F32),
        scratch_shapes=[
            pltpu.VMEM((pieces, experts * CAP // halves, piece), BF16),
            pltpu.VMEM((GROUP, GROUP), BF16),
        ],
        compiler_params=params(60),
        cost_estimate=cost(1, 1),
        name="combine_first",
    )(slots, gates, blocks)


def combine_last(slots, gates, blocks, first, gain, grad_out, hidden, rinv, halves):
    tokens, width = hidden.shape
    total, piece = blocks.shape
    whole = lambda shape: pl.BlockSpec(shape, lambda i: (0, 0))
    return pl.pallas_call(
        functools.partial(combine_last_kernel, halves),
        grid=(total // (4 * GROUP),),
        in_specs=[
            whole(slots.shape),
            whole(gates.shape),
            pl.BlockSpec((4 * GROUP, piece), lambda i: (i, 0)),
            whole(gain.shape),
            whole(rinv.shape),
        ]
        + [pl.BlockSpec(memory_space=pl.ANY)] * 3,
        out_specs=whole((tokens, width)),
        out_shape=jax.ShapeDtypeStruct((tokens, width), BF16),
        scratch_shapes=[
            pltpu.VMEM((first.shape[0], slots.shape[1] * CAP // halves, piece), BF16),
            pltpu.VMEM((GROUP, GROUP), BF16),
            pltpu.VMEM(first.shape, F32),
            pltpu.VMEM(first.shape, F32),
            pltpu.VMEM(grad_out.shape, BF16),
            pltpu.VMEM(hidden.shape, BF16),
            pltpu.SemaphoreType.DMA((3,)),
        ],
        compiler_params=params(50),
        cost_estimate=cost(2 * total * tokens * width, 8 * MB),
        name="combine_last",
    )(slots, gates, blocks, gain, rinv, first, grad_out, hidden)


def expert_kernel(
    slots, blocks_hbm, base_hbm, low_ref, high_ref, scale_ref, grad_hidden_ref,
    out_hbm, inputs_hbm, units_ref, low_act_ref, grad_linear_ref, back_ref, products_ref, mag_ref,
    blocks, base, inputs, linear, out_rows, in_sem, base_sem, row_sem, out_sem,
):
    groups = blocks.shape[0] // GROUP
    piece = blocks.shape[1]
    pieces = BLOCK // slots
    span = PER_GROUP * slots
    ffw = base.shape[2]
    depth = base.shape[1]
    tile = 256
    tiles = ffw // tile
    rank = high_ref.shape[1]

    def load_blocks(g):
        rows = pl.ds(pl.multiple_of(g * GROUP, GROUP), GROUP)
        return pltpu.make_async_copy(blocks_hbm.at[rows], blocks.at[rows], in_sem.at[g])

    def load_base(n):
        cols = pl.ds(pl.multiple_of((n % tiles) * tile, tile), tile)
        j = n // tiles
        return pltpu.make_async_copy(
            base_hbm.at[j, :, cols], base.at[j, :, cols], base_sem.at[n]
        )

    def store_rows(g):
        rows = pl.ds(pl.multiple_of(g * GROUP, GROUP), GROUP)
        return pltpu.make_async_copy(out_rows.at[rows], out_hbm.at[rows], out_sem.at[g])

    for g in range(groups):
        load_blocks(g).start()
    for n in range(2 * tiles):
        load_base(n).start()

    permute = to_rows(slots, 1)

    def unpack_group(g, _):
        load_blocks(g).wait()
        rows = dot(permute, blocks[pl.ds(pl.multiple_of(g * GROUP, GROUP), GROUP), :]).astype(BF16)
        place = pl.ds(pl.multiple_of(g * span, span), span)
        for p in range(pieces):
            inputs[place, p * piece : (p + 1) * piece] = rows[p * span : (p + 1) * span, :]
        return 0

    lax.fori_loop(0, groups, unpack_group, 0)
    keep = pltpu.make_async_copy(inputs, inputs_hbm, row_sem)
    keep.start()

    low_act_ref[...] = dot(inputs[...], low_ref[...]).astype(BF16)

    def forward(n, _):
        load_base(n).wait()
        j = n // tiles
        cols = pl.ds(pl.multiple_of((n % tiles) * tile, tile), tile)
        linear[j, :, cols] = dot(inputs[...], base[j, :, cols])
        return 0

    lax.fori_loop(0, 2 * tiles, forward, 0)

    for n in range(tiles):
        cols = slice(n * tile, (n + 1) * tile)
        gate_linear = linear[0, :, cols] + dot(low_act_ref[:, :rank], high_ref[0, :, cols])
        up_linear = linear[1, :, cols] + dot(low_act_ref[:, rank:], high_ref[1, :, cols])
        gate_scale = scale_ref[0:1, cols]
        up_scale = scale_ref[1:2, cols]
        gate = gate_linear * gate_scale
        up = up_linear * up_scale
        sigmoid = 1.0 / (1.0 + jnp.exp(-gate))
        active = gate * sigmoid
        units = (active * up).astype(BF16)
        units_ref[:, cols] = units
        grad_hidden = grad_hidden_ref[:, cols]
        part = jnp.sum(units.astype(F32) * grad_hidden, axis=1, keepdims=True)
        if n == 0:
            products_ref[...] = part
        else:
            products_ref[...] += part
        grad_gate = grad_hidden * up * sigmoid * (1.0 + gate * (1.0 - sigmoid))
        grad_up = grad_hidden * active
        mag_ref[0:1, cols] = jnp.sum(grad_gate * gate_linear, axis=0, keepdims=True)
        mag_ref[1:2, cols] = jnp.sum(grad_up * up_linear, axis=0, keepdims=True)
        grad_linear_ref[0, :, cols] = (grad_gate * gate_scale).astype(BF16)
        grad_linear_ref[1, :, cols] = (grad_up * up_scale).astype(BF16)

    for j in range(2):
        back_ref[:, j * rank : (j + 1) * rank] = contract(
            grad_linear_ref[j], high_ref[j], 1, 1
        ).astype(BF16)

    keep.wait()

    def backward(n, _):
        rows = pl.ds(pl.multiple_of(n * tile, tile), tile)
        grad = contract(grad_linear_ref[0], base[0, rows, :], 1, 1)
        grad = grad + contract(grad_linear_ref[1], base[1, rows, :], 1, 1)
        grad = grad + contract(back_ref[...], low_ref[rows, :], 1, 1)
        inputs[:, rows] = grad.astype(BF16)
        return 0

    lax.fori_loop(0, depth // tile, backward, 0)

    arrange = to_blocks(slots, 1)

    def pack_group(g, _):
        place = pl.ds(pl.multiple_of(g * span, span), span)
        stack = jnp.concatenate(
            [inputs[place, p * piece : (p + 1) * piece] for p in range(pieces)], axis=0
        )
        rows = pl.ds(pl.multiple_of(g * GROUP, GROUP), GROUP)
        out_rows[rows, :] = dot(arrange, stack).astype(BF16)
        store_rows(g).start()
        return 0

    lax.fori_loop(0, groups, pack_group, 0)
    for g in range(groups):
        store_rows(g).wait()


def expert(slots, blocks, base, low, high, scale, grad_hidden):
    total, piece = blocks.shape
    branches, depth, ffw = base.shape
    count = total * slots // BLOCK
    rank2 = low.shape[1]
    groups = total // GROUP
    vmem = pl.BlockSpec(memory_space=pltpu.VMEM)
    hbm = pl.BlockSpec(memory_space=pl.ANY)
    return pl.pallas_call(
        functools.partial(expert_kernel, slots),
        in_specs=[hbm, hbm, vmem, vmem, vmem, vmem],
        out_specs=[hbm, hbm, vmem, vmem, vmem, vmem, vmem, vmem],
        out_shape=[
            jax.ShapeDtypeStruct((total, piece), BF16),
            jax.ShapeDtypeStruct((count, depth), BF16),
            jax.ShapeDtypeStruct((count, ffw), BF16),
            jax.ShapeDtypeStruct((count, rank2), BF16),
            jax.ShapeDtypeStruct((branches, count, ffw), BF16),
            jax.ShapeDtypeStruct((count, rank2), BF16),
            jax.ShapeDtypeStruct((count, 1), F32),
            jax.ShapeDtypeStruct((branches, ffw), F32),
        ],
        scratch_shapes=[
            pltpu.VMEM((total, piece), BF16),
            pltpu.VMEM(base.shape, BF16),
            pltpu.VMEM((count, depth), BF16),
            pltpu.VMEM((branches, count, ffw), F32),
            pltpu.VMEM((total, piece), BF16),
            pltpu.SemaphoreType.DMA((groups,)),
            pltpu.SemaphoreType.DMA((2 * ffw // 256,)),
            pltpu.SemaphoreType.DMA,
            pltpu.SemaphoreType.DMA((groups,)),
        ],
        compiler_params=params(56),
        cost_estimate=cost(4 * count * depth * ffw * branches, 30 * MB),
        name="expert",
    )(blocks, base, low, high, scale, grad_hidden)


def expert_grads_kernel(
    halves, cotangent_ref, scale_ref, base_ref, high_ref, units_ref, low_out_ref, back_low_ref,
    *rest
):
    inputs = rest[:halves]
    low_acts, grad_linears, backs = (
        rest[halves : 2 * halves], rest[2 * halves : 3 * halves], rest[3 * halves : 4 * halves]
    )
    mag_ref, high_grad_ref, low_in_ref, low_grad_ref, high_in_ref, low_down, low_down_t, back_t = (
        rest[4 * halves :]
    )
    count = units_ref.shape[0] // halves
    rank = low_out_ref.shape[1]

    @pl.when(pl.program_id(0) == 0)
    def _():
        low = dot(units_ref[...], low_out_ref[...])
        low_down[...] = low.astype(BF16)
        low_down_t[...] = low.T.astype(BF16)
        low_grad_ref[...] = dot(back_low_ref[...].astype(F32).T.astype(BF16), units_ref[...])
        high_in_ref[...] = jnp.zeros_like(high_in_ref)
        for h in range(halves):
            back_t[h] = backs[h][...].astype(F32).T.astype(BF16)
            low_act_t = low_acts[h][...].astype(F32).T.astype(BF16)
            for j in range(2):
                high_in_ref[j] += dot(low_act_t[j * rank : (j + 1) * rank], grad_linears[h][j])

    mag = jnp.zeros((1, base_ref.shape[1]), F32)
    low_in = jnp.zeros(low_in_ref.shape, F32)
    for h in range(halves):
        rows = slice(h * count, (h + 1) * count)
        linear = dot(units_ref[rows, :], base_ref[...]) + dot(low_down[rows, :], high_ref[...])
        mag = mag + jnp.sum(linear * cotangent_ref[rows, :].astype(F32), axis=0, keepdims=True)
        low_in = low_in + dot(back_t[h], inputs[h][...])
    mag_ref[...] = mag
    low_in_ref[...] = low_in
    grad = (cotangent_ref[...].astype(F32) * scale_ref[...]).astype(BF16)
    high_grad_ref[...] = dot(low_down_t[...], grad)


def expert_grads(
    cotangent, scale, base, high, units, low_out, back_low, inputs, low_acts, grad_linears,
    backs,
):
    halves = len(inputs)
    ffw, width = base.shape
    count, rank = back_low.shape
    tile = 512
    whole = lambda array: pl.BlockSpec(array.shape, lambda i: (0,) * array.ndim)
    part = lambda rows: pl.BlockSpec((rows, tile), lambda i: (0, i))
    fixed = [units, low_out, back_low]
    return pl.pallas_call(
        functools.partial(expert_grads_kernel, halves),
        grid=(width // tile,),
        in_specs=[part(count), part(1), part(ffw), part(rank)]
        + [whole(array) for array in fixed]
        + [part(count // halves)] * halves
        + [whole(array) for array in low_acts + grad_linears + backs],
        out_specs=[
            part(1),
            part(rank),
            part(2 * rank),
            pl.BlockSpec((rank, ffw), lambda i: (0, 0)),
            pl.BlockSpec((2, rank, ffw), lambda i: (0, 0, 0)),
        ],
        out_shape=[
            jax.ShapeDtypeStruct((1, width), F32),
            jax.ShapeDtypeStruct((rank, width), F32),
            jax.ShapeDtypeStruct((2 * rank, width), F32),
            jax.ShapeDtypeStruct((rank, ffw), F32),
            jax.ShapeDtypeStruct((2, rank, ffw), F32),
        ],
        scratch_shapes=[
            pltpu.VMEM((count, rank), BF16),
            pltpu.VMEM((rank, count), BF16),
            pltpu.VMEM((halves, 2 * rank, count // halves), BF16),
        ],
        compiler_params=params(60),
        cost_estimate=cost(1, 1),
        name="expert_grads",
    )(cotangent, scale, base, high, *fixed, *inputs, *low_acts, *grad_linears, *backs)


def square_norm(base, low, high):
    merged = base.astype(F32) + dot(low, high)
    return jnp.sqrt(jnp.sum(merged * merged, axis=0))


def shards(
    query, keyval, doc_lengths, norm_gain, router_logits, expert_ids, grad_out,
    base_in, low_in, high_in, mag_in, base_out, low_out, high_out, mag_out,
):
    query, local_kv, grad_out = query[0], keyval[0], grad_out[0]
    base_in, low_in, high_in, mag_in = base_in[0], low_in[0], high_in[0], mag_in[0]
    base_out, low_out, high_out, mag_out = base_out[0], low_out[0], high_out[0], mag_out[0]
    ids = expert_ids[0]
    tokens, width = query.shape
    top = ids.shape[1]
    experts = lax.axis_size("ctx") * lax.axis_size("ep")
    axes = ("ctx", "ep")
    gain = norm_gain[None, :]
    halves = 2
    slots_each = CAP // halves
    ctx_count = lax.axis_size("ctx")

    def exchange(blocks):
        split = blocks.reshape(experts, BLOCK, blocks.shape[1])
        moved = lax.all_to_all(split, axes, split_axis=0, concat_axis=0, tiled=True)
        return moved.reshape(blocks.shape)

    each = jnp.arange(experts, dtype=jnp.int32)[:, None]

    seen, outgoing_grad, slots, token_slots = open_exchange(
        local_kv, ids, grad_out, experts, ctx_count
    )
    first = lax.axis_index("ctx") * tokens
    place = jnp.concatenate(
        [
            jnp.stack([first - REACH * tokens, first]).astype(jnp.int32),
            jnp.cumsum(doc_lengths[0]).astype(jnp.int32),
        ]
    )

    arrived_grad = exchange(outgoing_grad)

    prob, hidden = attend(place, query, seen)
    *outgoing, rinv = dispatch(slots, hidden, gain, True, halves)

    logits, hidden = lax.optimization_barrier((router_logits[0], hidden))
    gate_expo = jnp.exp(logits - jnp.max(logits, axis=-1, keepdims=True))
    gates = gate_expo / jnp.sum(gate_expo, axis=-1, keepdims=True)
    dense_gates = jnp.zeros((tokens, experts), F32)
    chosen = [ids[:, k : k + 1] == each.reshape(1, experts) for k in range(top)]
    for k in range(top):
        dense_gates = dense_gates + jnp.where(chosen[k], gates[:, k : k + 1], 0.0)

    norm_in = jnp.stack([square_norm(base_in[j], low_in[j], high_in[j]) for j in range(2)])
    scale_in = mag_in / norm_in
    norm_out = square_norm(base_out, low_out, high_out)
    scale_out = mag_out / norm_out
    cotangent = unpack(arrived_grad, halves).reshape(experts * CAP, width)
    grad_linear_out = (cotangent.astype(F32) * scale_out).astype(BF16)
    back_low = contract(grad_linear_out, high_out, 1, 1).astype(BF16)
    grad_hidden = contract(grad_linear_out, base_out, 1, 1) + contract(back_low, low_out, 1, 1)
    low_pair = jnp.concatenate([low_in[0], low_in[1]], axis=1)
    arrived = [exchange(outgoing[0])]
    second, grad_hidden, scale_in, low_pair, dense_gates, token_slots, _ = lax.optimization_barrier(
        (outgoing[1], grad_hidden, scale_in, low_pair, dense_gates, token_slots, arrived[0])
    )
    arrived.append(exchange(second))

    rows_each = experts * slots_each
    returned, results = [], []
    for h in range(halves):
        outgoing_rows, *result = expert(
            slots_each, arrived[h], base_in, low_pair, high_in, scale_in,
            grad_hidden[h * rows_each : (h + 1) * rows_each],
        )
        returned.append(exchange(outgoing_rows))
        results.append(result)
    results, first_returned = lax.optimization_barrier((results, returned[0]))
    returned[0] = first_returned
    inputs, units, low_acts, grad_linears, backs, products, mag_sums = zip(*results)

    mag_sum, grad_high_out, low_in_t, low_out_t, grad_high_in = expert_grads(
        cotangent, scale_out[None, :], base_out, high_out, jnp.concatenate(units, axis=0), low_out,
        back_low, inputs, low_acts, grad_linears, backs,
    )
    grad_mag_out = mag_sum[0] / norm_out
    grad_low_out = low_out_t.T
    grad_low_in = low_in_t.reshape(2, -1, width).transpose(0, 2, 1)
    grad_mag_in = sum(mag_sums) / norm_in
    products = jnp.concatenate(
        [part.astype(BF16).astype(F32).reshape(experts, slots_each) for part in products], axis=1
    )
    products = jnp.pad(products, ((0, 0), (0, HEAD - CAP))).reshape(ctx_count, -1, HEAD)

    partial = combine_first(token_slots, dense_gates, returned[0], halves)
    grad_heads = combine_last(
        token_slots, dense_gates, returned[1], partial, gain, grad_out, hidden, rinv, halves
    )
    grad_query, grad_keyval, arrived_products = finish(query, grad_heads, prob, seen, products)
    grad_query = (grad_query.astype(F32) * HEAD ** (-0.5)).astype(BF16)
    dense_products = jnp.zeros((tokens, experts), F32)
    for r in range(CAP):
        dense_products = dense_products + jnp.where(
            token_slots == r, arrived_products[r][None, :], 0.0
        )
    grad_gate = jnp.stack(
        [jnp.sum(jnp.where(chosen[k], dense_products, 0.0), axis=1) for k in range(top)], axis=1
    )
    grad_logits = gates * (grad_gate - jnp.sum(gates * grad_gate, axis=-1, keepdims=True))

    return (
        grad_query[None],
        grad_keyval[None],
        grad_logits[None],
        grad_low_in[None],
        grad_high_in[None],
        grad_mag_in[None],
        grad_low_out[None],
        grad_high_out[None],
        grad_mag_out[None],
    )


def solution(mesh):
    rows = P("ep", "ctx", None)
    own = lambda extra: P(("ctx", "ep"), *([None] * extra))
    in_specs = (
        rows, rows, P("ep", None), P(), rows, rows, rows,
        own(3), own(3), own(3), own(2), own(2), own(2), own(2), own(1),
    )
    out_specs = (rows, rows, rows, own(3), own(3), own(2), own(2), own(2), own(1))
    return jax.shard_map(shards, mesh=mesh, in_specs=in_specs, out_specs=out_specs, check_vma=False)
```

```python
import functools

import jax
import jax.numpy as jnp
from jax import lax
from jax.experimental import pallas as pl
from jax.experimental.pallas import tpu as pltpu
from jax.sharding import PartitionSpec as P

F32 = jnp.float32
BF16 = jnp.bfloat16
MESH = pl.DeviceIdType.MESH
HEAD = 128
NEGATIVE = -1e30
EPSILON = 1e-06
CAP = 4
BLOCK = 16
GROUP = 256
PER_GROUP = GROUP // BLOCK
REACH = 4
MB = 1 << 20


def params(megabytes):
    return pltpu.CompilerParams(vmem_limit_bytes=megabytes * MB)


def cost(flops, size, transcendentals=0):
    return pl.CostEstimate(flops=flops, bytes_accessed=size, transcendentals=transcendentals)


def iota(shape, dim):
    return lax.broadcasted_iota(jnp.int32, shape, dim)


def dot(left, right):
    return jnp.dot(left, right, preferred_element_type=F32)


def contract(left, right, left_dim, right_dim):
    return lax.dot_general(
        left, right, (((left_dim,), (right_dim,)), ((), ())), preferred_element_type=F32
    )


def is_row(row, col, slots, halves):
    pieces = BLOCK // (slots * halves)
    span = PER_GROUP * slots * halves
    return (
        (row // span == (col // (slots * halves)) % pieces)
        & ((row // (PER_GROUP * slots)) % halves == (col // slots) % halves)
        & ((row // slots) % PER_GROUP == col // BLOCK)
        & (row % slots == col % slots)
    )


def to_rows(slots, halves):
    same = is_row(iota((GROUP, GROUP), 0), iota((GROUP, GROUP), 1), slots, halves)
    return same.astype(F32).astype(BF16)


def to_blocks(slots, halves):
    same = is_row(iota((GROUP, GROUP), 1), iota((GROUP, GROUP), 0), slots, halves)
    return same.astype(F32).astype(BF16)


def dispatch_kernel(with_norm, slots_ref, rows_ref, gain_ref, *rest):
    outs, rinv_ref, stack = rest[:-2], rest[-2], rest[-1]
    tokens, width = rows_ref.shape
    slots = CAP // len(outs)
    pieces = BLOCK // slots
    piece = width // pieces

    @pl.when(pl.program_id(0) == 0)
    def _():
        if with_norm:
            square = jnp.zeros((tokens, 1), F32)
            for p in range(pieces):
                part = rows_ref[:, p * piece : (p + 1) * piece].astype(F32)
                square = square + jnp.sum(part * part, axis=1, keepdims=True)
            rinv = lax.rsqrt(square / width + EPSILON)
        else:
            rinv = jnp.ones((tokens, 1), F32)
        rinv_ref[...] = rinv
        for p in range(pieces):
            cols = slice(p * piece, (p + 1) * piece)
            part = rows_ref[:, cols]
            if with_norm:
                part = (part.astype(F32) * rinv * gain_ref[:, cols]).astype(BF16)
            stack[p * tokens : (p + 1) * tokens, :] = part

    spread = (iota((GROUP, PER_GROUP), 0) // BLOCK == iota((GROUP, PER_GROUP), 1)).astype(F32)
    slot = dot(spread.astype(BF16), slots_ref[...].astype(BF16))
    row = iota((GROUP, tokens), 0)
    for half, out_ref in enumerate(outs):
        hit = slot == (half * slots + row % slots).astype(F32)
        parts = []
        for p in range(pieces):
            own = hit & ((row // slots) % pieces == p)
            parts.append(jnp.where(own, 1.0, 0.0).astype(BF16))
        out_ref[...] = dot(jnp.concatenate(parts, axis=1), stack[...]).astype(BF16)


def dispatch(slots, rows, gain, with_norm, halves):
    experts, tokens = slots.shape
    width = rows.shape[1]
    total = experts * BLOCK
    pieces = BLOCK * halves // CAP
    piece = width // pieces
    whole = lambda shape: pl.BlockSpec(shape, lambda i: (0, 0))
    return pl.pallas_call(
        functools.partial(dispatch_kernel, with_norm),
        grid=(total // GROUP,),
        in_specs=[
            pl.BlockSpec((PER_GROUP, tokens), lambda i: (i, 0)),
            whole((tokens, width)),
            whole((1, width)),
        ],
        out_specs=[pl.BlockSpec((GROUP, piece), lambda i: (i, 0))] * halves + [whole((tokens, 1))],
        out_shape=[jax.ShapeDtypeStruct((total, piece), BF16)] * halves
        + [jax.ShapeDtypeStruct((tokens, 1), F32)],
        scratch_shapes=[pltpu.VMEM((pieces * tokens, piece), BF16)],
        compiler_params=params(60),
        cost_estimate=cost(2 * total * tokens * width * halves, 10 * MB),
        name="dispatch",
    )(slots, rows, gain)


def unpack_kernel(halves, blocks_ref, out_ref):
    piece = blocks_ref.shape[1]
    slots = CAP // halves
    pieces = BLOCK // CAP
    rows = dot(to_rows(slots, halves), blocks_ref[...]).astype(BF16)
    count = PER_GROUP * slots
    for p in range(pieces):
        for half in range(halves):
            first = (p * halves + half) * count
            out_ref[half, :, p * piece : (p + 1) * piece] = rows[first : first + count, :]


def unpack(blocks, halves):
    total, piece = blocks.shape
    pieces = BLOCK // CAP
    count = total // pieces // halves
    return pl.pallas_call(
        functools.partial(unpack_kernel, halves),
        grid=(total // GROUP,),
        in_specs=[pl.BlockSpec((GROUP, piece), lambda i: (i, 0))],
        out_specs=pl.BlockSpec(
            (halves, GROUP // pieces // halves, pieces * piece), lambda i: (0, i, 0)
        ),
        out_shape=jax.ShapeDtypeStruct((halves, count, pieces * piece), BF16),
        compiler_params=params(60),
        cost_estimate=cost(2 * total * GROUP * piece, 8 * MB),
        name="unpack",
    )(blocks)


def open_kernel(
    count, own_ref, slots_ref, rows_ref, seen_ref, out_hbm, stack, blocks, wanted, masks,
    send_sem, recv_sem, own_sem, out_sem,
):
    tokens, width = rows_ref.shape
    pieces = BLOCK // CAP
    piece = width // pieces
    groups = blocks.shape[0] // GROUP
    me = lax.axis_index("ctx")
    core = me % 2
    other = me + 1 - 2 * core

    def slot(j):
        return seen_ref.at[pl.ds((REACH - j) * tokens, tokens)]

    def copy(source, j, target, index):
        return pltpu.make_async_remote_copy(
            src_ref=source,
            dst_ref=slot(j),
            send_sem=send_sem.at[index],
            recv_sem=recv_sem.at[index],
            device_id={"ctx": target},
            device_id_type=MESH,
        )

    near = copy(own_ref, 2, me + 2, 0)
    far = copy(own_ref, 4, me + 4, 1)
    beside = copy(own_ref, 1, other, 2)
    near_even = copy(slot(2), 3, other, 3)
    near_odd = copy(slot(2), 1, other, 3)
    far_odd = copy(slot(4), 3, other, 4)

    keep = pltpu.make_async_copy(own_ref, slot(0), own_sem)
    keep.start()
    barrier = pltpu.get_barrier_semaphore()
    peers = 1
    for offset in (2, 4, -2, -4):
        present = (me + offset >= 0) & (me + offset < count)
        peers = peers + present.astype(jnp.int32)

        @pl.when(present)
        def _():
            pl.semaphore_signal(
                barrier, inc=1, device_id={"ctx": me + offset}, device_id_type=MESH
            )

    pl.semaphore_signal(barrier, inc=1, device_id={"ctx": other}, device_id_type=MESH)
    pl.semaphore_wait(barrier, peers)

    @pl.when(me + 4 < count)
    def _():
        far.start()

    @pl.when(me + 2 < count)
    def _():
        near.start()

    @pl.when(core == 0)
    def _():
        beside.start()

    for j in range(1, REACH + 1):

        @pl.when(me < j)
        def _():
            seen_ref[(REACH - j) * tokens : (REACH - j + 1) * tokens, :] = jnp.zeros(
                own_ref.shape, own_ref.dtype
            )

    for p in range(pieces):
        stack[p * tokens : (p + 1) * tokens, :] = rows_ref[:, p * piece : (p + 1) * piece]
    spread = (iota((GROUP, PER_GROUP), 0) // BLOCK == iota((GROUP, PER_GROUP), 1)).astype(F32)
    spread = spread.astype(BF16)
    row = iota((GROUP, tokens), 0)
    wanted[...] = (row % CAP).astype(F32)
    for p in range(pieces):
        own = (row // CAP) % pieces == p
        masks[:, p * tokens : (p + 1) * tokens] = own.astype(F32).astype(BF16)

    def store(g):
        rows = pl.ds(pl.multiple_of(g * GROUP, GROUP), GROUP)
        return pltpu.make_async_copy(blocks.at[rows], out_hbm.at[rows], out_sem.at[g])

    def pick(g, _):
        named = slots_ref[pl.ds(pl.multiple_of(g * PER_GROUP, PER_GROUP), PER_GROUP), :]
        hit = jnp.where(dot(spread, named.astype(BF16)) == wanted[...], 1.0, 0.0).astype(BF16)
        picker = jnp.concatenate([hit] * pieces, axis=1) * masks[...]
        rows = pl.ds(pl.multiple_of(g * GROUP, GROUP), GROUP)
        blocks[rows, :] = dot(picker, stack[...]).astype(BF16)
        store(g).start()
        return 0

    lax.fori_loop(0, groups // 2, pick, 0)

    @pl.when(me >= 2)
    def _():
        near.wait_recv()

        @pl.when(core == 0)
        def _():
            near_even.start()

        @pl.when(core == 1)
        def _():
            near_odd.start()

    lax.fori_loop(groups // 2, groups, pick, 0)

    @pl.when(me >= 4)
    def _():
        far.wait_recv()

        @pl.when(core == 1)
        def _():
            far_odd.start()

    @pl.when(core == 1)
    def _():
        beside.wait_recv()

    @pl.when(core == 0)
    def _():
        beside.wait_send()

    @pl.when(me >= 2)
    def _():
        near_even.wait_send()
        near_even.wait_recv()

    @pl.when((me >= 4) & (core == 1))
    def _():
        far_odd.wait_send()

    @pl.when((me >= 4) & (core == 0))
    def _():
        far_odd.wait_recv()

    @pl.when(me + 4 < count)
    def _():
        far.wait_send()

    @pl.when(me + 2 < count)
    def _():
        near.wait_send()

    keep.wait()
    for g in range(groups):
        store(g).wait()


def open_exchange(own, slots, rows, count):
    experts, tokens = slots.shape
    total = experts * BLOCK
    piece = rows.shape[1] * CAP // BLOCK
    vmem = pl.BlockSpec(memory_space=pltpu.VMEM)
    return pl.pallas_call(
        functools.partial(open_kernel, count),
        in_specs=[vmem] * 3,
        out_specs=[vmem, pl.BlockSpec(memory_space=pl.ANY)],
        out_shape=[
            jax.ShapeDtypeStruct(((REACH + 1) * tokens, own.shape[1]), own.dtype),
            jax.ShapeDtypeStruct((total, piece), BF16),
        ],
        scratch_shapes=[
            pltpu.VMEM((BLOCK // CAP * tokens, piece), BF16),
            pltpu.VMEM((total, piece), BF16),
            pltpu.VMEM((GROUP, tokens), F32),
            pltpu.VMEM((GROUP, BLOCK // CAP * tokens), BF16),
            pltpu.SemaphoreType.DMA((5,)),
            pltpu.SemaphoreType.DMA((5,)),
            pltpu.SemaphoreType.DMA,
            pltpu.SemaphoreType.DMA((total // GROUP,)),
        ],
        compiler_params=pltpu.CompilerParams(
            collective_id=0, has_side_effects=True, vmem_limit_bytes=60 * MB
        ),
        name="open_exchange",
    )(own, slots, rows)


def visible(place_ref, window, tokens):
    kpos = place_ref[0] + iota((window, tokens), 0)
    qpos = place_ref[1] + iota((window, tokens), 1)
    kdoc = jnp.zeros((window, tokens), jnp.int32)
    qdoc = jnp.zeros((window, tokens), jnp.int32)
    for d in range(4):
        end = place_ref[2 + d]
        kdoc = kdoc + (kpos >= end).astype(jnp.int32)
        qdoc = qdoc + (qpos >= end).astype(jnp.int32)
    return (kpos >= 0) & (kpos <= qpos) & (kdoc == qdoc)


def stack_heads(ref, heads):
    return jnp.concatenate([ref[:, h * HEAD : (h + 1) * HEAD] for h in range(heads)], axis=0)


def head_pair(ref, h):
    return jnp.concatenate(
        [ref[:, h * HEAD : (h + 1) * HEAD], ref[:, (h + 1) * HEAD : (h + 2) * HEAD]], axis=0
    )


def attend_kernel(heads, per_kv, place_ref, query_ref, keyval_ref, prob_ref, out_ref, bias):
    tokens = query_ref.shape[0]
    window = keyval_ref.shape[0]
    step = pl.program_id(0)
    half = keyval_ref.shape[1] // 2
    scale = HEAD ** (-0.5)

    @pl.when(step == 0)
    def _():
        hidden = jnp.where(visible(place_ref, window, tokens), 0.0, NEGATIVE)
        bias[:, :tokens] = hidden
        bias[:, tokens:] = hidden

    for m in range(half // HEAD):

        @pl.when(step // (per_kv // heads) == m)
        def _():
            keys = keyval_ref[:, m * HEAD : (m + 1) * HEAD]
            values_t = keyval_ref[:, half + m * HEAD : half + (m + 1) * HEAD].T
            for h in range(0, heads, 2):
                raw = contract(keys, head_pair(query_ref, h), 1, 1) * scale + bias[...]
                peak = jnp.max(raw, axis=0, keepdims=True)
                expo = jnp.exp(raw - peak)
                total = jnp.sum(expo, axis=0, keepdims=True)
                prob = (expo * (1.0 / total)).astype(BF16)
                prob_ref[0, :, h * tokens : (h + 2) * tokens] = prob
                mixed = dot(values_t, prob).T.astype(BF16)
                out_ref[:, h * HEAD : (h + 1) * HEAD] = mixed[:tokens]
                out_ref[:, (h + 1) * HEAD : (h + 2) * HEAD] = mixed[tokens:]


def attend(place, query, keyval):
    tokens, width = query.shape
    window = keyval.shape[0]
    kv_heads = keyval.shape[1] // 2 // HEAD
    per_kv = width // HEAD // kv_heads
    heads = 8
    steps = width // HEAD // heads
    return pl.pallas_call(
        functools.partial(attend_kernel, heads, per_kv),
        grid=(steps,),
        in_specs=[
            pl.BlockSpec(memory_space=pltpu.SMEM),
            pl.BlockSpec((tokens, heads * HEAD), lambda i: (0, i)),
            pl.BlockSpec(keyval.shape, lambda i: (0, 0)),
        ],
        out_specs=[
            pl.BlockSpec((1, window, heads * tokens), lambda i: (i, 0, 0)),
            pl.BlockSpec((tokens, heads * HEAD), lambda i: (0, i)),
        ],
        out_shape=[
            jax.ShapeDtypeStruct((steps, window, heads * tokens), BF16),
            jax.ShapeDtypeStruct((tokens, width), BF16),
        ],
        scratch_shapes=[pltpu.VMEM((window, 2 * tokens), F32)],
        compiler_params=params(60),
        cost_estimate=cost(4 * tokens * width * window, 9 * MB, tokens * width * window // HEAD),
        name="attend",
    )(place, query, keyval)


def finish_kernel(
    heads, steps_per_kv, count, ep_count, query_ref, grad_ref, prob_ref, keys_ref, values_ref,
    products_ref, grad_query_ref, grad_keyval_ref, returned_ref,
    key_sum, value_sum, terms, landed, gathered, turned, arrived,
    send_sem, recv_sem, ctx_send, ctx_recv, ep_send, ep_recv,
):
    step = pl.program_id(0)
    last = pl.num_programs(0) - 1
    tokens = query_ref.shape[0]
    half = grad_keyval_ref.shape[1] // 2
    scale = HEAD ** (-0.5)
    me = lax.axis_index("ctx")
    place = lax.axis_index("ep")
    barrier = pltpu.get_barrier_semaphore()

    def send_terms(j, m, part):
        return pltpu.make_async_remote_copy(
            src_ref=terms.at[m, part, pl.ds((REACH - j) * tokens, tokens)],
            dst_ref=landed.at[j - 1, m, part],
            send_sem=send_sem.at[j - 1, m, part],
            recv_sem=recv_sem.at[j - 1, m, part],
            device_id={"ctx": me - j},
            device_id_type=MESH,
        )

    def send_part(part, total):
        for m in range(landed.shape[1]):

            @pl.when(step == (m + 1) * steps_per_kv - 1)
            def _():
                terms[m, part] = total().astype(BF16)
                for j in range(REACH, 0, -1):

                    @pl.when(me >= j)
                    def _():
                        send_terms(j, m, part).start()

    def along_ctx(d):
        target = (me + d) % count
        return pltpu.make_async_remote_copy(
            src_ref=products_ref.at[target],
            dst_ref=gathered.at[me],
            send_sem=ctx_send.at[d - 1],
            recv_sem=ctx_recv.at[d - 1],
            device_id={"ctx": target},
            device_id_type=MESH,
        )

    def along_ep(d):
        target = (place + d) % ep_count
        return pltpu.make_async_remote_copy(
            src_ref=turned.at[target],
            dst_ref=arrived.at[place],
            send_sem=ep_send.at[d - 1],
            recv_sem=ep_recv.at[d - 1],
            device_id={"ep": target},
            device_id_type=MESH,
        )

    @pl.when(step == 0)
    def _():
        for d in range(1, count):
            pl.semaphore_signal(
                barrier, inc=1, device_id={"ctx": (me + d) % count}, device_id_type=MESH
            )
        for d in range(1, ep_count):
            pl.semaphore_signal(
                barrier, inc=1, device_id={"ep": (place + d) % ep_count}, device_id_type=MESH
            )
        gathered[me] = products_ref[me]

    @pl.when(step == 1)
    def _():
        pl.semaphore_wait(barrier, count + ep_count - 2)
        for d in range(1, count):
            along_ctx(d).start()

    @pl.when(step == last - 1)
    def _():
        for d in range(1, count):
            along_ctx(d).wait_recv()
        for c in range(count):
            turned[:, c, :] = gathered[c]
        arrived[place] = turned[place]
        for d in range(1, ep_count):
            along_ep(d).start()

    @pl.when(step % steps_per_kv == 0)
    def _():
        key_sum[...] = jnp.zeros_like(key_sum)
        value_sum[...] = jnp.zeros_like(value_sum)

    grad = stack_heads(grad_ref, heads)
    prob = prob_ref[0]
    value_sum[...] += dot(prob, grad)
    send_part(1, lambda: value_sum[...])
    wide = prob.astype(F32)
    moved = wide * contract(values_ref[...], grad, 1, 1)
    delta = jnp.sum(moved, axis=0, keepdims=True)
    dscore = (moved - wide * delta).astype(BF16)
    key_sum[...] += dot(dscore, stack_heads(query_ref, heads))
    send_part(0, lambda: key_sum[...] * scale)
    grad_query = dot(keys_ref[...].T, dscore).T.astype(BF16)
    for h in range(heads):
        grad_query_ref[:, h * HEAD : (h + 1) * HEAD] = grad_query[h * tokens : (h + 1) * tokens]

    @pl.when(step == last)
    def _():
        for d in range(1, count):
            along_ctx(d).wait_send()
        for d in range(1, ep_count):
            along_ep(d).wait_send()
            along_ep(d).wait_recv()
        by_expert = jnp.concatenate([arrived[:, c, :] for c in range(count)], axis=0)
        returned_ref[...] = by_expert.T[: returned_ref.shape[0], :]
        for m in range(landed.shape[1]):
            for part in (1, 0):
                for j in range(1, REACH + 1):

                    @pl.when(me + j < count)
                    def _():
                        send_terms(j, m, part).wait_recv()

                    @pl.when(me + j >= count)
                    def _():
                        landed[j - 1, m, part] = jnp.zeros(landed.shape[3:], landed.dtype)

                total = terms[m, part, REACH * tokens :, :].astype(F32)
                for j in range(REACH):
                    total = total + landed[j, m, part].astype(F32)
                first = part * half + m * HEAD
                grad_keyval_ref[:, first : first + HEAD] = total.astype(BF16)
                for j in range(1, REACH + 1):

                    @pl.when(me >= j)
                    def _():
                        send_terms(j, m, part).wait_send()


def finish(query, grad, prob, keyval, products):
    tokens, width = query.shape
    window = keyval.shape[0]
    count, ep_count, lanes = products.shape
    kv_heads = keyval.shape[1] // 2 // HEAD
    heads = prob.shape[2] // tokens
    steps = prob.shape[0]
    steps_per_kv = steps // kv_heads
    rows = pl.BlockSpec((tokens, heads * HEAD), lambda i: (0, i))
    return pl.pallas_call(
        functools.partial(finish_kernel, heads, steps_per_kv, count, ep_count),
        grid=(steps,),
        in_specs=[
            rows,
            rows,
            pl.BlockSpec((1,) + prob.shape[1:], lambda i: (i, 0, 0)),
            pl.BlockSpec((window, HEAD), lambda i: (0, i // steps_per_kv)),
            pl.BlockSpec((window, HEAD), lambda i: (0, kv_heads + i // steps_per_kv)),
            pl.BlockSpec(products.shape, lambda i: (0, 0, 0)),
        ],
        out_specs=[
            rows,
            pl.BlockSpec((tokens, keyval.shape[1]), lambda i: (0, 0)),
            pl.BlockSpec((8, count * ep_count), lambda i: (0, 0)),
        ],
        out_shape=[
            jax.ShapeDtypeStruct((tokens, width), BF16),
            jax.ShapeDtypeStruct((tokens, keyval.shape[1]), BF16),
            jax.ShapeDtypeStruct((8, count * ep_count), F32),
        ],
        scratch_shapes=[
            pltpu.VMEM((window, HEAD), F32),
            pltpu.VMEM((window, HEAD), F32),
            pltpu.VMEM((kv_heads, 2, window, HEAD), BF16),
            pltpu.VMEM((REACH, kv_heads, 2, tokens, HEAD), BF16),
            pltpu.VMEM((count, ep_count, lanes), F32),
            pltpu.VMEM((ep_count, count, lanes), F32),
            pltpu.VMEM((ep_count, count, lanes), F32),
            pltpu.SemaphoreType.DMA((REACH, kv_heads, 2)),
            pltpu.SemaphoreType.DMA((REACH, kv_heads, 2)),
            pltpu.SemaphoreType.DMA((count - 1,)),
            pltpu.SemaphoreType.DMA((count - 1,)),
            pltpu.SemaphoreType.DMA((ep_count - 1,)),
            pltpu.SemaphoreType.DMA((ep_count - 1,)),
        ],
        compiler_params=pltpu.CompilerParams(
            collective_id=1, has_side_effects=True, vmem_limit_bytes=50 * MB
        ),
        cost_estimate=cost(8 * tokens * width * window, 10 * MB),
        name="finish",
    )(query, grad, prob, keyval, keyval, products)


def gather_rows(slots, blocks_ref, rows, order):
    pieces = BLOCK // slots
    span = PER_GROUP * slots
    groups = blocks_ref.shape[0] // GROUP

    @pl.when(pl.program_id(0) == 0)
    def _():
        order[...] = to_rows(slots, 1)

    for g in range(groups):
        moved = dot(order[...], blocks_ref[g * GROUP : (g + 1) * GROUP, :]).astype(BF16)
        place = pl.ds(pl.multiple_of((pl.program_id(0) * groups + g) * span, span), span)
        for p in range(pieces):
            rows[p, place, :] = moved[p * span : (p + 1) * span, :]


def gate_rows(half, slots, slots_ref, gates_ref):
    tokens, experts = slots_ref.shape
    count = experts * slots
    spread = (iota((experts, count), 0) == iota((experts, count), 1) // slots).astype(F32)
    spread = spread.astype(BF16)
    slot = dot(slots_ref[...].astype(BF16), spread)
    gate = dot(gates_ref[...].astype(BF16), spread)
    own = (half * slots + iota((tokens, count), 1) % slots).astype(F32)
    return jnp.where(slot == own, gate, 0.0).astype(BF16)


def combine_first_kernel(halves, slots_ref, gates_ref, blocks_ref, acc_ref, rows, order):
    slots = CAP // halves
    gather_rows(slots, blocks_ref, rows, order)

    @pl.when(pl.program_id(0) == pl.num_programs(0) - 1)
    def _():
        gate = gate_rows(0, slots, slots_ref, gates_ref)
        for p in range(rows.shape[0]):
            acc_ref[p] = dot(gate, rows[p])


def combine_last_kernel(
    halves, slots_ref, gates_ref, blocks_ref, gain_ref, rinv_ref, first_hbm, grad_out_hbm,
    hidden_hbm, grad_ref, rows, order, acc, first_ref, grad_out_ref, hidden_ref, sem,
):
    step = pl.program_id(0)
    tokens, width = hidden_ref.shape
    loads = [
        pltpu.make_async_copy(source, target, sem.at[i])
        for i, (source, target) in enumerate(
            [(first_hbm, first_ref), (grad_out_hbm, grad_out_ref), (hidden_hbm, hidden_ref)]
        )
    ]

    @pl.when(step == 0)
    def _():
        for load in loads:
            load.start()

    slots = CAP // halves
    pieces, _, piece = acc.shape
    gather_rows(slots, blocks_ref, rows, order)

    @pl.when(step == pl.num_programs(0) - 1)
    def _():
        gate = gate_rows(halves - 1, slots, slots_ref, gates_ref)
        for load in loads:
            load.wait()
        rinv = rinv_ref[...]
        mean = jnp.zeros((tokens, 1), F32)
        for p in range(pieces):
            cols = slice(p * piece, (p + 1) * piece)
            scaled = (dot(gate, rows[p]) + first_ref[p]) * gain_ref[:, cols]
            acc[p] = scaled
            mean = mean + jnp.sum(hidden_ref[:, cols].astype(F32) * scaled, axis=1, keepdims=True)
        mean = mean / width * (rinv * rinv * rinv)
        for p in range(pieces):
            cols = slice(p * piece, (p + 1) * piece)
            grad = (
                grad_out_ref[:, cols].astype(F32)
                + rinv * acc[p]
                - hidden_ref[:, cols].astype(F32) * mean
            )
            grad_ref[:, cols] = grad.astype(BF16)


def combine_first(slots, gates, blocks, halves):
    tokens, experts = slots.shape
    total, piece = blocks.shape
    pieces = BLOCK * halves // CAP
    whole = lambda shape: pl.BlockSpec(shape, lambda i: (0,) * len(shape))
    return pl.pallas_call(
        functools.partial(combine_first_kernel, halves),
        grid=(total // (4 * GROUP),),
        in_specs=[
            whole(slots.shape),
            whole(gates.shape),
            pl.BlockSpec((4 * GROUP, piece), lambda i: (i, 0)),
        ],
        out_specs=whole((pieces, tokens, piece)),
        out_shape=jax.ShapeDtypeStruct((pieces, tokens, piece), F32),
        scratch_shapes=[
            pltpu.VMEM((pieces, experts * CAP // halves, piece), BF16),
            pltpu.VMEM((GROUP, GROUP), BF16),
        ],
        compiler_params=params(60),
        cost_estimate=cost(1, 1),
        name="combine_first",
    )(slots, gates, blocks)


def combine_last(slots, gates, blocks, first, gain, grad_out, hidden, rinv, halves):
    tokens, width = hidden.shape
    total, piece = blocks.shape
    whole = lambda shape: pl.BlockSpec(shape, lambda i: (0, 0))
    return pl.pallas_call(
        functools.partial(combine_last_kernel, halves),
        grid=(total // (4 * GROUP),),
        in_specs=[
            whole(slots.shape),
            whole(gates.shape),
            pl.BlockSpec((4 * GROUP, piece), lambda i: (i, 0)),
            whole(gain.shape),
            whole(rinv.shape),
        ]
        + [pl.BlockSpec(memory_space=pl.ANY)] * 3,
        out_specs=whole((tokens, width)),
        out_shape=jax.ShapeDtypeStruct((tokens, width), BF16),
        scratch_shapes=[
            pltpu.VMEM((first.shape[0], slots.shape[1] * CAP // halves, piece), BF16),
            pltpu.VMEM((GROUP, GROUP), BF16),
            pltpu.VMEM(first.shape, F32),
            pltpu.VMEM(first.shape, F32),
            pltpu.VMEM(grad_out.shape, BF16),
            pltpu.VMEM(hidden.shape, BF16),
            pltpu.SemaphoreType.DMA((3,)),
        ],
        compiler_params=params(51),
        cost_estimate=cost(2 * total * tokens * width, 1),
        name="combine_last",
    )(slots, gates, blocks, gain, rinv, first, grad_out, hidden)


def expert_kernel(
    slots, blocks_hbm, base_hbm, low_ref, high_ref, scale_ref, grad_hidden_ref,
    out_hbm, inputs_hbm, units_ref, low_act_ref, grad_linear_ref, back_ref, products_ref, mag_ref,
    blocks, base, inputs, linear, out_rows, in_sem, base_sem, row_sem, out_sem,
):
    groups = blocks.shape[0] // GROUP
    piece = blocks.shape[1]
    pieces = BLOCK // slots
    span = PER_GROUP * slots
    ffw = base.shape[2]
    depth = base.shape[1]
    tile = 256
    tiles = ffw // tile
    rank = high_ref.shape[1]

    def load_blocks(g):
        rows = pl.ds(pl.multiple_of(g * GROUP, GROUP), GROUP)
        return pltpu.make_async_copy(blocks_hbm.at[rows], blocks.at[rows], in_sem.at[g])

    def load_base(n):
        cols = pl.ds(pl.multiple_of((n % tiles) * tile, tile), tile)
        j = n // tiles
        return pltpu.make_async_copy(
            base_hbm.at[j, :, cols], base.at[j, :, cols], base_sem.at[n]
        )

    def store_rows(g):
        rows = pl.ds(pl.multiple_of(g * GROUP, GROUP), GROUP)
        return pltpu.make_async_copy(out_rows.at[rows], out_hbm.at[rows], out_sem.at[g])

    for g in range(groups):
        load_blocks(g).start()
    for n in range(2 * tiles):
        load_base(n).start()

    permute = to_rows(slots, 1)

    def unpack_group(g, _):
        load_blocks(g).wait()
        rows = dot(permute, blocks[pl.ds(pl.multiple_of(g * GROUP, GROUP), GROUP), :]).astype(BF16)
        place = pl.ds(pl.multiple_of(g * span, span), span)
        for p in range(pieces):
            inputs[place, p * piece : (p + 1) * piece] = rows[p * span : (p + 1) * span, :]
        return 0

    lax.fori_loop(0, groups, unpack_group, 0)
    keep = pltpu.make_async_copy(inputs, inputs_hbm, row_sem)
    keep.start()

    low_act_ref[...] = dot(inputs[...], low_ref[...]).astype(BF16)

    def forward(n, _):
        load_base(n).wait()
        j = n // tiles
        cols = pl.ds(pl.multiple_of((n % tiles) * tile, tile), tile)
        linear[j, :, cols] = dot(inputs[...], base[j, :, cols])
        return 0

    lax.fori_loop(0, 2 * tiles, forward, 0)

    for n in range(tiles):
        cols = slice(n * tile, (n + 1) * tile)
        gate_linear = linear[0, :, cols] + dot(low_act_ref[:, :rank], high_ref[0, :, cols])
        up_linear = linear[1, :, cols] + dot(low_act_ref[:, rank:], high_ref[1, :, cols])
        gate_scale = scale_ref[0:1, cols]
        up_scale = scale_ref[1:2, cols]
        gate = gate_linear * gate_scale
        up = up_linear * up_scale
        sigmoid = 1.0 / (1.0 + jnp.exp(-gate))
        active = gate * sigmoid
        units = (active * up).astype(BF16)
        units_ref[:, cols] = units
        grad_hidden = grad_hidden_ref[:, cols]
        part = jnp.sum(units.astype(F32) * grad_hidden, axis=1, keepdims=True)
        if n == 0:
            products_ref[...] = part
        else:
            products_ref[...] += part
        grad_gate = grad_hidden * up * sigmoid * (1.0 + gate * (1.0 - sigmoid))
        grad_up = grad_hidden * active
        mag_ref[0:1, cols] = jnp.sum(grad_gate * gate_linear, axis=0, keepdims=True)
        mag_ref[1:2, cols] = jnp.sum(grad_up * up_linear, axis=0, keepdims=True)
        grad_linear_ref[0, :, cols] = (grad_gate * gate_scale).astype(BF16)
        grad_linear_ref[1, :, cols] = (grad_up * up_scale).astype(BF16)

    for j in range(2):
        back_ref[:, j * rank : (j + 1) * rank] = contract(
            grad_linear_ref[j], high_ref[j], 1, 1
        ).astype(BF16)

    keep.wait()

    def backward(n, _):
        rows = pl.ds(pl.multiple_of(n * tile, tile), tile)
        grad = contract(grad_linear_ref[0], base[0, rows, :], 1, 1)
        grad = grad + contract(grad_linear_ref[1], base[1, rows, :], 1, 1)
        grad = grad + contract(back_ref[...], low_ref[rows, :], 1, 1)
        inputs[:, rows] = grad.astype(BF16)
        return 0

    lax.fori_loop(0, depth // tile, backward, 0)

    arrange = to_blocks(slots, 1)

    def pack_group(g, _):
        place = pl.ds(pl.multiple_of(g * span, span), span)
        stack = jnp.concatenate(
            [inputs[place, p * piece : (p + 1) * piece] for p in range(pieces)], axis=0
        )
        rows = pl.ds(pl.multiple_of(g * GROUP, GROUP), GROUP)
        out_rows[rows, :] = dot(arrange, stack).astype(BF16)
        store_rows(g).start()
        return 0

    lax.fori_loop(0, groups, pack_group, 0)
    for g in range(groups):
        store_rows(g).wait()


def expert(slots, blocks, base, low, high, scale, grad_hidden):
    total, piece = blocks.shape
    branches, depth, ffw = base.shape
    count = total * slots // BLOCK
    rank2 = low.shape[1]
    groups = total // GROUP
    vmem = pl.BlockSpec(memory_space=pltpu.VMEM)
    hbm = pl.BlockSpec(memory_space=pl.ANY)
    return pl.pallas_call(
        functools.partial(expert_kernel, slots),
        in_specs=[hbm, hbm, vmem, vmem, vmem, vmem],
        out_specs=[hbm, hbm, vmem, vmem, vmem, vmem, vmem, vmem],
        out_shape=[
            jax.ShapeDtypeStruct((total, piece), BF16),
            jax.ShapeDtypeStruct((count, depth), BF16),
            jax.ShapeDtypeStruct((count, ffw), BF16),
            jax.ShapeDtypeStruct((count, rank2), BF16),
            jax.ShapeDtypeStruct((branches, count, ffw), BF16),
            jax.ShapeDtypeStruct((count, rank2), BF16),
            jax.ShapeDtypeStruct((count, 1), F32),
            jax.ShapeDtypeStruct((branches, ffw), F32),
        ],
        scratch_shapes=[
            pltpu.VMEM((total, piece), BF16),
            pltpu.VMEM(base.shape, BF16),
            pltpu.VMEM((count, depth), BF16),
            pltpu.VMEM((branches, count, ffw), F32),
            pltpu.VMEM((total, piece), BF16),
            pltpu.SemaphoreType.DMA((groups,)),
            pltpu.SemaphoreType.DMA((2 * ffw // 256,)),
            pltpu.SemaphoreType.DMA,
            pltpu.SemaphoreType.DMA((groups,)),
        ],
        compiler_params=params(56),
        cost_estimate=cost(4 * count * depth * ffw * branches, 30 * MB),
        name="expert",
    )(blocks, base, low, high, scale, grad_hidden)


def expert_grads_kernel(
    halves, cotangent_ref, scale_ref, base_ref, high_ref, units_ref, low_out_ref, back_low_ref,
    *rest
):
    inputs = rest[:halves]
    low_acts, grad_linears, backs = (
        rest[halves : 2 * halves], rest[2 * halves : 3 * halves], rest[3 * halves : 4 * halves]
    )
    mag_ref, high_grad_ref, low_in_ref, low_grad_ref, high_in_ref, low_down, low_down_t, back_t = (
        rest[4 * halves :]
    )
    count = units_ref.shape[0] // halves
    rank = low_out_ref.shape[1]

    @pl.when(pl.program_id(0) == 0)
    def _():
        low = dot(units_ref[...], low_out_ref[...])
        low_down[...] = low.astype(BF16)
        low_down_t[...] = low.T.astype(BF16)
        low_grad_ref[...] = dot(back_low_ref[...].astype(F32).T.astype(BF16), units_ref[...])
        high_in_ref[...] = jnp.zeros_like(high_in_ref)
        for h in range(halves):
            back_t[h] = backs[h][...].astype(F32).T.astype(BF16)
            low_act_t = low_acts[h][...].astype(F32).T.astype(BF16)
            for j in range(2):
                high_in_ref[j] += dot(low_act_t[j * rank : (j + 1) * rank], grad_linears[h][j])

    mag = jnp.zeros((1, base_ref.shape[1]), F32)
    low_in = jnp.zeros(low_in_ref.shape, F32)
    for h in range(halves):
        rows = slice(h * count, (h + 1) * count)
        linear = dot(units_ref[rows, :], base_ref[...]) + dot(low_down[rows, :], high_ref[...])
        mag = mag + jnp.sum(linear * cotangent_ref[rows, :].astype(F32), axis=0, keepdims=True)
        low_in = low_in + dot(back_t[h], inputs[h][...])
    mag_ref[...] = mag
    low_in_ref[...] = low_in
    grad = (cotangent_ref[...].astype(F32) * scale_ref[...]).astype(BF16)
    high_grad_ref[...] = dot(low_down_t[...], grad)


def expert_grads(
    cotangent, scale, base, high, units, low_out, back_low, inputs, low_acts, grad_linears,
    backs,
):
    halves = len(inputs)
    ffw, width = base.shape
    count, rank = back_low.shape
    tile = 512
    whole = lambda array: pl.BlockSpec(array.shape, lambda i: (0,) * array.ndim)
    part = lambda rows: pl.BlockSpec((rows, tile), lambda i: (0, i))
    fixed = [units, low_out, back_low]
    return pl.pallas_call(
        functools.partial(expert_grads_kernel, halves),
        grid=(width // tile,),
        in_specs=[part(count), part(1), part(ffw), part(rank)]
        + [whole(array) for array in fixed]
        + [part(count // halves)] * halves
        + [whole(array) for array in low_acts + grad_linears + backs],
        out_specs=[
            part(1),
            part(rank),
            part(2 * rank),
            pl.BlockSpec((rank, ffw), lambda i: (0, 0)),
            pl.BlockSpec((2, rank, ffw), lambda i: (0, 0, 0)),
        ],
        out_shape=[
            jax.ShapeDtypeStruct((1, width), F32),
            jax.ShapeDtypeStruct((rank, width), F32),
            jax.ShapeDtypeStruct((2 * rank, width), F32),
            jax.ShapeDtypeStruct((rank, ffw), F32),
            jax.ShapeDtypeStruct((2, rank, ffw), F32),
        ],
        scratch_shapes=[
            pltpu.VMEM((count, rank), BF16),
            pltpu.VMEM((rank, count), BF16),
            pltpu.VMEM((halves, 2 * rank, count // halves), BF16),
        ],
        compiler_params=params(60),
        cost_estimate=cost(1, 1),
        name="expert_grads",
    )(cotangent, scale, base, high, *fixed, *inputs, *low_acts, *grad_linears, *backs)


def square_norm(base, low, high):
    merged = base.astype(F32) + dot(low, high)
    return jnp.sqrt(jnp.sum(merged * merged, axis=0))


def shards(
    query, keyval, doc_lengths, norm_gain, router_logits, expert_ids, grad_out,
    base_in, low_in, high_in, mag_in, base_out, low_out, high_out, mag_out,
):
    query, local_kv, grad_out = query[0], keyval[0], grad_out[0]
    base_in, low_in, high_in, mag_in = base_in[0], low_in[0], high_in[0], mag_in[0]
    base_out, low_out, high_out, mag_out = base_out[0], low_out[0], high_out[0], mag_out[0]
    ids = expert_ids[0]
    tokens, width = query.shape
    top = ids.shape[1]
    experts = lax.axis_size("ctx") * lax.axis_size("ep")
    axes = ("ctx", "ep")
    gain = norm_gain[None, :]
    halves = 2
    slots_each = CAP // halves
    ctx_count = lax.axis_size("ctx")

    def exchange(blocks):
        split = blocks.reshape(experts, BLOCK, blocks.shape[1])
        moved = lax.all_to_all(split, axes, split_axis=0, concat_axis=0, tiled=True)
        return moved.reshape(blocks.shape)

    named = jnp.zeros((experts, tokens), jnp.bool_)
    each = jnp.arange(experts, dtype=jnp.int32)[:, None]
    for k in range(top):
        named = named | (ids[:, k][None, :] == each)
    earlier = jnp.arange(tokens)[:, None] < jnp.arange(tokens)[None, :]
    before = dot(named.astype(BF16), earlier.astype(BF16))
    slots = jnp.where(named, before, -1.0)

    seen, outgoing_grad = open_exchange(local_kv, slots, grad_out, ctx_count)
    first = lax.axis_index("ctx") * tokens
    place = jnp.concatenate(
        [
            jnp.stack([first - REACH * tokens, first]).astype(jnp.int32),
            jnp.cumsum(doc_lengths[0]).astype(jnp.int32),
        ]
    )

    arrived_grad = exchange(outgoing_grad)

    prob, hidden = attend(place, query, seen)
    *outgoing, rinv = dispatch(slots, hidden, gain, True, halves)

    logits, hidden = lax.optimization_barrier((router_logits[0], hidden))
    gate_expo = jnp.exp(logits - jnp.max(logits, axis=-1, keepdims=True))
    gates = gate_expo / jnp.sum(gate_expo, axis=-1, keepdims=True)
    dense_gates = jnp.zeros((tokens, experts), F32)
    chosen = [ids[:, k : k + 1] == each.reshape(1, experts) for k in range(top)]
    for k in range(top):
        dense_gates = dense_gates + jnp.where(chosen[k], gates[:, k : k + 1], 0.0)
    token_slots = slots.T

    norm_in = jnp.stack([square_norm(base_in[j], low_in[j], high_in[j]) for j in range(2)])
    scale_in = mag_in / norm_in
    norm_out = square_norm(base_out, low_out, high_out)
    scale_out = mag_out / norm_out
    cotangent = unpack(arrived_grad, halves).reshape(experts * CAP, width)
    grad_linear_out = (cotangent.astype(F32) * scale_out).astype(BF16)
    back_low = contract(grad_linear_out, high_out, 1, 1).astype(BF16)
    grad_hidden = contract(grad_linear_out, base_out, 1, 1) + contract(back_low, low_out, 1, 1)
    low_pair = jnp.concatenate([low_in[0], low_in[1]], axis=1)
    arrived = [exchange(outgoing[0])]
    second, grad_hidden, scale_in, low_pair, dense_gates, token_slots, _ = lax.optimization_barrier(
        (outgoing[1], grad_hidden, scale_in, low_pair, dense_gates, token_slots, arrived[0])
    )
    arrived.append(exchange(second))

    rows_each = experts * slots_each
    returned, results = [], []
    for h in range(halves):
        outgoing_rows, *result = expert(
            slots_each, arrived[h], base_in, low_pair, high_in, scale_in,
            grad_hidden[h * rows_each : (h + 1) * rows_each],
        )
        returned.append(exchange(outgoing_rows))
        results.append(result)
    results, first_returned = lax.optimization_barrier((results, returned[0]))
    returned[0] = first_returned
    inputs, units, low_acts, grad_linears, backs, products, mag_sums = zip(*results)

    mag_sum, grad_high_out, low_in_t, low_out_t, grad_high_in = expert_grads(
        cotangent, scale_out[None, :], base_out, high_out, jnp.concatenate(units, axis=0), low_out,
        back_low, inputs, low_acts, grad_linears, backs,
    )
    grad_mag_out = mag_sum[0] / norm_out
    grad_low_out = low_out_t.T
    grad_low_in = low_in_t.reshape(2, -1, width).transpose(0, 2, 1)
    grad_mag_in = sum(mag_sums) / norm_in
    products = jnp.concatenate(
        [part.astype(BF16).astype(F32).reshape(experts, slots_each) for part in products], axis=1
    )
    products = jnp.pad(products, ((0, 0), (0, HEAD - CAP))).reshape(ctx_count, -1, HEAD)

    partial = combine_first(token_slots, dense_gates, returned[0], halves)
    grad_heads = combine_last(
        token_slots, dense_gates, returned[1], partial, gain, grad_out, hidden, rinv, halves
    )
    grad_query, grad_keyval, arrived_products = finish(query, grad_heads, prob, seen, products)
    grad_query = (grad_query.astype(F32) * HEAD ** (-0.5)).astype(BF16)
    dense_products = jnp.zeros((tokens, experts), F32)
    for r in range(CAP):
        dense_products = dense_products + jnp.where(
            token_slots == r, arrived_products[r][None, :], 0.0
        )
    grad_gate = jnp.stack(
        [jnp.sum(jnp.where(chosen[k], dense_products, 0.0), axis=1) for k in range(top)], axis=1
    )
    grad_logits = gates * (grad_gate - jnp.sum(gates * grad_gate, axis=-1, keepdims=True))

    return (
        grad_query[None],
        grad_keyval[None],
        grad_logits[None],
        grad_low_in[None],
        grad_high_in[None],
        grad_mag_in[None],
        grad_low_out[None],
        grad_high_out[None],
        grad_mag_out[None],
    )


def solution(mesh):
    rows = P("ep", "ctx", None)
    own = lambda extra: P(("ctx", "ep"), *([None] * extra))
    in_specs = (
        rows, rows, P("ep", None), P(), rows, rows, rows,
        own(3), own(3), own(3), own(2), own(2), own(2), own(2), own(1),
    )
    out_specs = (rows, rows, rows, own(3), own(3), own(2), own(2), own(2), own(1))
    return jax.shard_map(shards, mesh=mesh, in_specs=in_specs, out_specs=out_specs, check_vma=False)
```
